128 devices in a mesh: row: 4 (over x_hi, core), seq: 32 (over y, x_lo, z).
Axes of the slice: x: 4 (x_hi: 2, x_lo: 2; x = x_hi * 2 + x_lo), y: 4, z: 4, core: 2. Of those that a mesh axis runs over, the one named last changes fastest.
Arguments:
- block_input: bfloat16 [4, 4096, 1024], P('row', 'seq'), may hold values from -6 to 6
- out_grad: bfloat16 [4, 4096, 1024], P('row', 'seq'), may hold values from -6 to 6
- lengths: int32 [4, 7], P('row'), may hold values from 1 to 4090, as said below
- w_query: bfloat16 [1024, 2048], P(('row', 'seq')), may hold values from -0.1875 to 0.1875
- w_key: bfloat16 [1024, 1024], P(('row', 'seq')), may hold values from -0.1875 to 0.1875
- w_value: bfloat16 [1024, 1024], P(('row', 'seq')), may hold values from -0.1875 to 0.1875
- w_out: bfloat16 [2048, 1024], P(None, ('row', 'seq')), may hold values from -0.125 to 0.125
- w_gate: bfloat16 [1024, 3072], P(('row', 'seq')), may hold values from -0.1875 to 0.1875
- w_up: bfloat16 [1024, 3072], P(('row', 'seq')), may hold values from -0.1875 to 0.1875
- w_down: bfloat16 [3072, 1024], P(None, ('row', 'seq')), may hold values from -0.109375 to 0.109375
- gain_query: bfloat16 [2048], P(('row', 'seq')), may hold values from 0.5 to 1.5
- gain_key: bfloat16 [1024], P(('row', 'seq')), may hold values from 0.5 to 1.5
- gain_attn: bfloat16 [1024], P(('row', 'seq')), may hold values from 0.5 to 1.5
- gain_mlp: bfloat16 [1024], P(('row', 'seq')), may hold values from 0.5 to 1.5
Outputs:
- output: float32 [4, 4096, 1024], P('row', 'seq')
- input_grad: float32 [4, 4096, 1024], P('row', 'seq')
- grad_query: float32 [1024, 2048], P(('row', 'seq'))
- grad_key: float32 [1024, 1024], P(('row', 'seq'))
- grad_value: float32 [1024, 1024], P(('row', 'seq'))
- grad_out: float32 [2048, 1024], P(None, ('row', 'seq'))
- grad_gate: float32 [1024, 3072], P(('row', 'seq'))
- grad_up: float32 [1024, 3072], P(('row', 'seq'))
- grad_down: float32 [3072, 1024], P(None, ('row', 'seq'))
- grad_gain_query: float32 [2048], P(('row', 'seq'))
- grad_gain_key: float32 [1024], P(('row', 'seq'))
- grad_gain_attn: float32 [1024], P(('row', 'seq'))
- grad_gain_mlp: float32 [1024], P(('row', 'seq'))
The draws below stay inside these ranges and needn't reach their ends.
Inputs may be any that keep to these rules, and one draw needn't show every extreme that they name: Each row's 7 lengths sum to 4096. In every row but one: the first length is under 128, the last two under max(64, 2), those between are 1024 each except the last of them, which is 1024 minus the first and the last two. In the remaining row, drawn from the seed, every length is 1 except the one before the last two, which is 4090.
All inputs are finite; a program needn't handle non-finite values.
Results may differ from the reference program's by a relative error of at most 0.023.
Values may be sent and summed in bfloat16 or wider, within the bound.
No kernel may reach another device: no remote copies, remote signals or barrier semaphores. Data moves between devices by JAX's collectives and lax.ppermute only.
A program may use at most 320 MiB of HBM per device.

```python
import functools
import math
import jax
import jax.numpy as jnp
from jax import lax

D = 1024
HD = 128
FF = 3072
TOK_DEV = 128
DOC_LEN = 1024
NDOC = 7
ROWS = 4
ROW_LEN = 4096
QW = 2048
KW = 1024


def draw_lengths(key, part):
    key = jax.random.fold_in(key, 7)
    subkeys = jax.random.split(key, 3)
    first_len = jax.random.randint(subkeys[0], (ROWS, 1), 1, TOK_DEV)
    tail_lengths = jax.random.randint(subkeys[1], (ROWS, 2), 1, max(TOK_DEV // 2, 2))
    full_docs = NDOC - 3
    whole_docs = jnp.full((ROWS, full_docs - 1), DOC_LEN, jnp.int32)
    last_doc = DOC_LEN - first_len - jnp.sum(tail_lengths, axis=1, keepdims=True)
    documents = jnp.concatenate([whole_docs, last_doc], axis=1)
    spanning = jnp.concatenate([jnp.ones((ROWS, full_docs - 1), jnp.int32), jnp.full((ROWS, 1), ROW_LEN - NDOC + 1, jnp.int32)], axis=1)
    chosen_row = jax.random.randint(subkeys[2], (), 0, ROWS)
    picked = (jnp.arange(ROWS, dtype=jnp.int32) == chosen_row)[:, None]
    first_len = jnp.where(picked, 1, first_len)
    tail_lengths = jnp.where(picked, 1, tail_lengths)
    documents = jnp.where(picked, spanning, documents)
    return jnp.concatenate([first_len, documents, tail_lengths], axis=1).astype(jnp.int32)


def levels(key, dims, cuts, smallest, top_value):
    loudness, own = 1.0, jax.random.fold_in(key, 6)
    for axis_at, shards_of in cuts:
        heights = jnp.exp(jax.random.uniform(jax.random.fold_in(own, axis_at), (shards_of,), jnp.float32, smallest / len(cuts), top_value / len(cuts)))
        loudness = loudness * jnp.repeat(heights, dims[axis_at] // shards_of).reshape([-1 if axis == axis_at else 1 for axis in range(len(dims))])
    return loudness


def scatter_about(rng, dims, spread, reach, cuts=(), held_as=jnp.bfloat16):
    values = spread * jax.random.normal(rng, dims, jnp.float32)
    if cuts:
        values = values * levels(rng, dims, cuts, -0.22, 0.18)
    return jnp.clip(values, -reach, reach).astype(held_as)


def setup_inputs(seed: int = 0) -> dict:
    arg_keys = jax.random.split(jax.random.key(seed), 15)
    block_input = scatter_about(arg_keys[0], (ROWS, ROW_LEN, D), 1.0, 6.0, ((0, 4), (1, 32)))
    out_grad = scatter_about(arg_keys[1], (ROWS, ROW_LEN, D), 1.0, 6.0, ((0, 4), (1, 32)))
    lengths = draw_lengths(jax.random.fold_in(arg_keys[14], 71), 0)
    w_query = scatter_about(arg_keys[3], (D, QW), D ** -0.5, 0.1875, ((0, 128),))
    w_key = scatter_about(arg_keys[4], (D, KW), D ** -0.5, 0.1875, ((0, 128),))
    w_value = scatter_about(arg_keys[5], (D, KW), D ** -0.5, 0.1875, ((0, 128),))
    w_out = scatter_about(arg_keys[6], (QW, D), QW ** -0.5, 0.125, ((1, 128),))
    w_gate = scatter_about(arg_keys[7], (D, FF), D ** -0.5, 0.1875, ((0, 128),))
    w_up = scatter_about(arg_keys[8], (D, FF), D ** -0.5, 0.1875, ((0, 128),))
    w_down = scatter_about(arg_keys[9], (FF, D), FF ** -0.5, 0.109375, ((1, 128),))
    gain_query = jnp.clip(1.0 + 0.1 * jax.random.normal(arg_keys[10], (QW,), jnp.float32), 0.5, 1.5).astype(jnp.bfloat16)
    gain_key = jnp.clip(1.0 + 0.1 * jax.random.normal(arg_keys[11], (KW,), jnp.float32), 0.5, 1.5).astype(jnp.bfloat16)
    gain_attn = jnp.clip(1.0 + 0.1 * jax.random.normal(arg_keys[12], (D,), jnp.float32), 0.5, 1.5).astype(jnp.bfloat16)
    gain_mlp = jnp.clip(1.0 + 0.1 * jax.random.normal(arg_keys[13], (D,), jnp.float32), 0.5, 1.5).astype(jnp.bfloat16)
    return {"block_input": block_input, "out_grad": out_grad, "lengths": lengths, "w_query": w_query, "w_key": w_key, "w_value": w_value, "w_out": w_out, "w_gate": w_gate, "w_up": w_up, "w_down": w_down, "gain_query": gain_query, "gain_key": gain_key, "gain_attn": gain_attn, "gain_mlp": gain_mlp}


EPSILON = 1e-06
THETA = 500000.0
HIGHEST_PRECISION = lax.Precision.HIGHEST

@jax.custom_vjp
def low(v):
    return lax.optimization_barrier(v.astype(jnp.bfloat16)).astype(jnp.float32)

@jax.custom_vjp
def low_back(v):
    return v

def low_keep(v):
    return (low(v), None)

def low_pass(kept, grad):
    return (grad,)

def back_keep(v):
    return (v, None)

def back_low(kept, grad):
    return (low(grad),)
low.defvjp(low_keep, low_pass)
low_back.defvjp(back_keep, back_low)

def matmul_hi(left_side, right_side):
    return jnp.dot(left_side, right_side, precision=HIGHEST_PRECISION)

def places(row_lengths, first_row, rows_here):
    spots = first_row + jnp.arange(rows_here, dtype=jnp.int32)
    ends = jnp.cumsum(row_lengths).astype(jnp.int32)
    passed = spots[:, None] >= ends[None, :]
    segment = lax.optimization_barrier(jnp.sum(passed.astype(jnp.int32), axis=1)).astype(jnp.int32)
    begins = lax.optimization_barrier(jnp.sum(jnp.where(passed, row_lengths[None, :], 0), axis=1)).astype(jnp.int32)
    return (spots, segment, spots - begins)

def rotate(vectors, offsets):
    half_width = vectors.shape[-1] // 2
    frequency = THETA ** (-(jnp.arange(half_width, dtype=jnp.float32) * 2.0 / vectors.shape[-1]))
    angles = offsets.astype(jnp.float32)[:, None] * frequency[None, :]
    cosine = jnp.cos(angles)[:, None, :]
    sine_part = jnp.sin(angles)[:, None, :]
    lower_half = vectors[..., :half_width]
    upper_half = vectors[..., half_width:]
    return jnp.concatenate([lower_half * cosine - upper_half * sine_part, upper_half * cosine + lower_half * sine_part], axis=-1)

def rms_scale(values, gain_vec):
    return values * lax.rsqrt(lax.optimization_barrier(jnp.mean(values * values, axis=-1, keepdims=True)) + EPSILON) * gain_vec

def forward_row(row_lengths, tokens, w_query, w_key, w_value, w_out, w_gate, w_up, w_down, gain_query, gain_key, gain_attn, gain_mlp):
    rows_here = tokens.shape[0]
    head_count = w_query.shape[1] // HD
    kv_count = w_key.shape[1] // HD
    group_size = head_count // kv_count
    score_scale = 1.0 / math.sqrt(HD)
    spots, segment, offsets = places(row_lengths, 0, rows_here)
    q_pre = low_back(matmul_hi(tokens, w_query))
    k_pre = low_back(matmul_hi(tokens, w_key))
    values = low(low_back(matmul_hi(tokens, w_value))).reshape(rows_here, kv_count, HD)
    queries = low(rotate(rms_scale(q_pre, gain_query).reshape(rows_here, head_count, HD), offsets))
    queries = queries.reshape(rows_here, kv_count, group_size, HD)
    keys = low(rotate(rms_scale(k_pre, gain_key).reshape(rows_here, kv_count, HD), offsets))
    block_rows = math.gcd(rows_here, 512)
    block_count = rows_here // block_rows

    def attend_block(parts):
        query_block, spot_block, segment_block = parts
        scores = low_back(jnp.einsum('tkgd,skd->kgts', query_block, keys, precision=HIGHEST_PRECISION) * score_scale)
        allowed = (spots[None, :] <= spot_block[:, None]) & (segment[None, :] == segment_block[:, None])
        scores = jnp.where(allowed, scores, -1e+30)
        largest = lax.optimization_barrier(jnp.max(scores, axis=-1, keepdims=True))
        weights = jnp.exp(scores - largest)
        probs = weights / lax.optimization_barrier(jnp.sum(weights, axis=-1, keepdims=True))
        return jnp.einsum('kgts,skd->tkgd', probs, values, precision=HIGHEST_PRECISION)
    attended = lax.map(jax.checkpoint(attend_block), (queries.reshape(block_count, block_rows, kv_count, group_size, HD), spots.reshape(block_count, block_rows), segment.reshape(block_count, block_rows)))
    attended = low(low_back(attended.reshape(rows_here, head_count * HD)))
    projected = low_back(matmul_hi(attended, w_out))
    middle = tokens + rms_scale(projected, gain_attn)
    middle_low = low(middle)
    gate_val = low_back(matmul_hi(middle_low, w_gate))
    up_val = low_back(matmul_hi(middle_low, w_up))
    activated = low(gate_val * jax.nn.sigmoid(gate_val) * up_val)
    down_out = low_back(matmul_hi(activated, w_down))
    return middle + rms_scale(down_out, gain_mlp)

def reference(block_input, out_grad, lengths, w_query, w_key, w_value, w_out, w_gate, w_up, w_down, gain_query, gain_key, gain_attn, gain_mlp):
    params = tuple((param.astype(jnp.float32) for param in (w_query, w_key, w_value, w_out, w_gate, w_up, w_down, gain_query, gain_key, gain_attn, gain_mlp)))
    totals = [jnp.zeros(param.shape, jnp.float32) for param in params]
    outputs = []
    input_grads = []
    for row_index in range(block_input.shape[0]):
        tokens = block_input[row_index].astype(jnp.float32)
        result, pullback = jax.vjp(functools.partial(forward_row, lengths[row_index]), tokens, *params)
        grads = pullback(out_grad[row_index].astype(jnp.float32))
        outputs.append(result)
        input_grads.append(grads[0])
        totals = [total_grad + new_grad for total_grad, new_grad in zip(totals, grads[1:])]
    return (jnp.stack(outputs), jnp.stack(input_grads), totals[0], totals[1], totals[2], totals[3], totals[4], totals[5], totals[6], totals[7], totals[8], totals[9], totals[10])
```

```python
import functools
import math

import jax
import jax.numpy as jnp
from jax import lax
from jax.experimental import pallas as pl
from jax.experimental.pallas import tpu as pltpu
from jax.sharding import Mesh, PartitionSpec as P

BF = jnp.bfloat16
F32 = jnp.float32
HD = 128
EPSILON = 1e-06
THETA = 500000.0
AXES = ("xh", "c", "y", "xl", "z")
SEQ = ("y", "xl", "z")
LOG2E = 1.4426950408889634
VMEM_LIMIT = 56 * 1024 * 1024
HIGHEST = lax.Precision.HIGHEST


def swap(a):
    return lax.ppermute(a, "c", [(0, 1), (1, 0)])


def shift(a, ring, by, mirrored):
    axes = ("xh", "c", "xl") if ring == "x" else ("c", ring)

    def index(c, m):
        return (m // 2) * 4 + c * 2 + m % 2 if ring == "x" else c * 4 + m

    pairs = []
    for c in range(2):
        step = -by if (mirrored and c == 1) else by
        pairs += [(index(c, m), index(c, (m + step) % 4)) for m in range(4)]
    return lax.ppermute(a, axes, pairs)


def position(ring):
    if ring == "x":
        return lax.axis_index("xh") * 2 + lax.axis_index("xl")
    return lax.axis_index(ring)


def params(limit=VMEM_LIMIT):
    return pltpu.CompilerParams(vmem_limit_bytes=limit)


VSPEC = pl.BlockSpec(memory_space=pltpu.VMEM)
SSPEC = pl.BlockSpec(memory_space=pltpu.SMEM)
ASPEC = pl.BlockSpec(memory_space=pl.ANY)


def place(groups):
    count = len(groups)
    where = jnp.stack([jnp.asarray(i, jnp.int32) for _, spots, _ in groups for i in spots])
    dims = [dim for _, _, dim in groups]
    shapes = [blocks[0].shape[:dim] + (4,) + blocks[0].shape[dim:] for blocks, _, dim in groups]

    def kernel(where_ref, *refs):
        ins, outs, sems = refs[: 4 * count], refs[4 * count : 5 * count], refs[5 * count]
        copies = []
        for p in range(count):
            for k in range(4):
                spot = where_ref[4 * p + k]
                target = outs[p].at[(slice(None),) * dims[p] + (spot,)]
                copies.append(pltpu.make_async_copy(ins[4 * p + k], target, sems.at[4 * p + k]))
        for copy in copies:
            copy.start()
        for copy in copies:
            copy.wait()

    return pl.pallas_call(
        kernel,
        out_shape=[jax.ShapeDtypeStruct(s, g[0][0].dtype) for s, g in zip(shapes, groups)],
        in_specs=[SSPEC] + [VSPEC] * (4 * count),
        out_specs=[ASPEC] * count,
        scratch_shapes=[pltpu.SemaphoreType.DMA((4 * count,))],
        compiler_params=params(),
    )(where, *[b for blocks, _, _ in groups for b in blocks])


GATHER_ORDERS = (("z", "y", "x"), ("x", "z", "y"), ("y", "x", "z"))
GATHER_DIMS = ((0, 0, 0), (0, 1, 1), (0, 0, 2))


def gather_cube(parts):
    core = lax.axis_index("c")
    sign = 1 - 2 * core
    for phase in range(3):
        groups = []
        for part, order, dims in zip(parts, GATHER_ORDERS, GATHER_DIMS):
            ring = order[phase]
            here = position(ring)
            if phase < 2:
                first, second = shift(part, ring, 1, True), shift(part, ring, -1, True)
                third = shift(part, ring, 2, False)
            else:
                first, second = shift(part, ring, 1, True), shift(part, ring, -1, True)
                third = shift(first, ring, 1, True)
            spots = [here, (here - sign) % 4, (here + sign) % 4, (here + 2) % 4]
            groups.append(((part, first, second, third), spots, dims[phase]))
        parts = place(groups)
    return parts


SCATTER_ORDERS = (("x", "y", "z"), ("y", "z", "x"), ("z", "x", "y"))


def scatter_cube(parts):
    core = lax.axis_index("c")
    sign = 1 - 2 * core
    left = [["x", "y", "z"] for _ in parts]
    for phase in range(3):
        sums = []
        for n, part in enumerate(parts):
            ring = SCATTER_ORDERS[n][phase]
            dim = left[n].index(ring)
            left[n].remove(ring)
            here = position(ring)

            def block(spot, part=part, dim=dim):
                return lax.dynamic_index_in_dim(part, spot % 4, dim, keepdims=False)

            direct = shift(block(here - sign), ring, -1, True)
            if phase == 0:
                passed = shift(block(here + 2), ring, 1, True)
                ahead = (block(here + sign).astype(F32) + passed.astype(F32)).astype(BF)
                through = shift(ahead, ring, 1, True)
                total = block(here).astype(F32) + direct.astype(F32) + through.astype(F32)
            else:
                near = shift(block(here + sign), ring, 1, True)
                far = shift(block(here + 2), ring, 2, False)
                total = (
                    block(here).astype(F32)
                    + direct.astype(F32)
                    + near.astype(F32)
                    + far.astype(F32)
                )
            sums.append(total if phase == 2 else total.astype(BF))
        parts = sums
    return parts


def qkv_kernel(x_ref, wq_ref, wkv_ref, q_ref, k_ref, v_ref, ss_ref):
    x = x_ref[...]
    q = jnp.dot(x, wq_ref[...], preferred_element_type=F32)
    kv = jnp.dot(x, wkv_ref[...], preferred_element_type=F32)
    k = kv[:, :512]
    q_ref[...] = q
    k_ref[...] = k
    v_ref[...] = kv[:, 512:].astype(BF)
    sq = jnp.sum(q * q, axis=1, keepdims=True)
    sk = jnp.sum(k * k, axis=1, keepdims=True)
    lane = lax.broadcasted_iota(jnp.int32, ss_ref.shape, 1)
    ss_ref[...] = jnp.where(lane < 64, sq, sk)


def project_qkv(x256, wq, wkv):
    tokens = x256.shape[0]
    return pl.pallas_call(
        qkv_kernel,
        out_shape=[
            jax.ShapeDtypeStruct((tokens, 1024), F32),
            jax.ShapeDtypeStruct((tokens, 512), F32),
            jax.ShapeDtypeStruct((tokens, 512), BF),
            jax.ShapeDtypeStruct((tokens, 128), F32),
        ],
        in_specs=[VSPEC] * 3,
        out_specs=[VSPEC] * 4,
        compiler_params=params(),
        cost_estimate=pl.CostEstimate(
            flops=2 * tokens * 1024 * 2048, bytes_accessed=6 << 20, transcendentals=0
        ),
    )(x256, wq, wkv)


def rope_forward(v, cos, sin):
    return v * cos + pltpu.roll(v, 64, 1) * sin


def rope_backward(d, cos, sin):
    return d * cos - pltpu.roll(d, 64, 1) * sin


def send_kernel(q_ref, k_ref, v_ref, ss_ref, gq_ref, gk_ref, cos_ref, sin_ref, out_ref):
    for r in range(2):
        rows = pl.ds(128 * r, 128)
        cos, sin = cos_ref[rows, :], sin_ref[rows, :]
        rq = lax.rsqrt(ss_ref[rows, 0:1] * (1.0 / 2048) + EPSILON)
        rk = lax.rsqrt(ss_ref[rows, 64:65] * (1.0 / 1024) + EPSILON)
        for h in range(4):
            at = r * 16 + h * 4
            for g in range(2):
                cols = pl.ds((h * 2 + g) * HD, HD)
                q = rope_forward(q_ref[rows, cols] * rq * gq_ref[:, cols], cos, sin).astype(BF)
                for j in range(4):
                    out_ref[at + j, g * 32 : (g + 1) * 32, :] = q[32 * j : 32 * j + 32]
            cols = pl.ds(h * HD, HD)
            k = rope_forward(k_ref[rows, cols] * rk * gk_ref[:, cols], cos, sin).astype(BF)
            v = v_ref[rows, cols]
            for j in range(4):
                out_ref[at + j, 64:192, :] = k
                out_ref[at + j, 192:320, :] = v


def pack_qkv(q_pre, k_pre, v16, ss, gq, gk, cos, sin):
    return pl.pallas_call(
        send_kernel,
        out_shape=jax.ShapeDtypeStruct((32, 320, HD), BF),
        in_specs=[VSPEC] * 8,
        out_specs=VSPEC,
        compiler_params=params(),
        cost_estimate=pl.CostEstimate(flops=4 << 20, bytes_accessed=4 << 20, transcendentals=512),
    )(q_pre, k_pre, v16, ss, gq, gk, cos, sin)


def tile_mask(kt, starts, spots):
    keys = kt * 512 + lax.broadcasted_iota(jnp.int32, (512, 256), 0)
    return (keys >= starts) & (keys <= spots)


def attend_kernel(scale2, low_ref, mid_ref, r_ref, start_ref, spot_ref, out_ref, acc_ref, lse_ref, vt_ref):
    for b in range(32):
        vt_ref[:, b * 128 : (b + 1) * 128] = r_ref[b, 192:320, :].T

    def tile(i, _):
        q = r_ref[pl.ds(4 * i, 4), 0:64, :].reshape(256, HD)
        starts, spots = start_ref[i], spot_ref[i]

        def step(masked, kt, carry):
            top, total, acc = carry
            k = r_ref[pl.ds(4 * kt, 4), 64:192, :].reshape(512, HD)
            s = lax.dot_general(k, q, (((1,), (1,)), ((), ())), preferred_element_type=F32)
            s = s * scale2
            if masked:
                s = jnp.where(tile_mask(kt, starts, spots), s, -1e30)
            new_top = jnp.maximum(top, jnp.max(s, axis=0, keepdims=True))
            p = jnp.exp2(s - new_top)
            if masked:
                p = jnp.where(s > -1e29, p, 0.0)
            fade = jnp.exp2(top - new_top)
            total = total * fade + jnp.sum(p, axis=0, keepdims=True)
            vt = vt_ref[:, pl.ds(pl.multiple_of(kt * 512, 512), 512)]
            acc = acc * fade + jnp.dot(vt, p.astype(BF), preferred_element_type=F32)
            return new_top, total, acc

        carry = (
            jnp.full((1, 256), -1e30, F32),
            jnp.zeros((1, 256), F32),
            jnp.zeros((HD, 256), F32),
        )
        carry = lax.fori_loop(low_ref[i], mid_ref[i], functools.partial(step, True), carry)
        carry = lax.fori_loop(mid_ref[i], i, functools.partial(step, False), carry)
        top, total, acc = step(True, i, carry)
        acc = acc / total
        acc_ref[i] = acc
        lse_ref[i] = top + jnp.log2(total)
        out_ref[pl.ds(4 * i, 4)] = acc.T.astype(BF).reshape(4, 64, HD)
        return 0

    lax.fori_loop(0, 8, tile, 0)


def attend(received, low, mid, starts, spots):
    return pl.pallas_call(
        functools.partial(attend_kernel, LOG2E / math.sqrt(HD)),
        out_shape=[
            jax.ShapeDtypeStruct((32, 64, HD), BF),
            jax.ShapeDtypeStruct((8, HD, 256), F32),
            jax.ShapeDtypeStruct((8, 1, 256), F32),
        ],
        in_specs=[SSPEC] * 2 + [VSPEC] * 3,
        out_specs=[VSPEC] * 3,
        scratch_shapes=[pltpu.VMEM((HD, 4096), BF)],
        compiler_params=params(),
        cost_estimate=pl.CostEstimate(
            flops=36 * 512 * 256 * 512, bytes_accessed=5 << 20, transcendentals=36 << 17
        ),
    )(low, mid, received, starts, spots)


def attend_grad_kernel(
    scale2, scale, low_ref, mid_ref, r_ref, do_ref, acc_ref, lse_ref, start_ref, spot_ref, out_ref, kt_ref, dk_ref, dv_ref
):
    for b in range(32):
        kt_ref[:, b * 128 : (b + 1) * 128] = r_ref[b, 64:192, :].T
    dk_ref[...] = jnp.zeros_like(dk_ref)
    dv_ref[...] = jnp.zeros_like(dv_ref)

    def tile(i, _):
        q = r_ref[pl.ds(4 * i, 4), 0:64, :].reshape(256, HD)
        do = do_ref[pl.ds(4 * i, 4)].reshape(256, HD)
        delta = jnp.sum(do.astype(F32).T * acc_ref[i], axis=0, keepdims=True)
        lse, starts, spots = lse_ref[i], start_ref[i], spot_ref[i]

        def step(masked, kt, dq):
            k = r_ref[pl.ds(4 * kt, 4), 64:192, :].reshape(512, HD)
            v = r_ref[pl.ds(4 * kt, 4), 192:320, :].reshape(512, HD)
            s = lax.dot_general(k, q, (((1,), (1,)), ((), ())), preferred_element_type=F32)
            e = s * scale2 - lse
            if masked:
                e = jnp.where(tile_mask(kt, starts, spots), e, -1e30)
            p = jnp.exp2(e)
            dp = lax.dot_general(v, do, (((1,), (1,)), ((), ())), preferred_element_type=F32)
            ds = (p * (dp - delta)).astype(BF)
            keys = pl.ds(pl.multiple_of(kt * 512, 512), 512)
            dv_ref[keys, :] += jnp.dot(p.astype(BF), do, preferred_element_type=F32)
            dk_ref[keys, :] += jnp.dot(ds, q, preferred_element_type=F32)
            return dq + jnp.dot(kt_ref[:, keys], ds, preferred_element_type=F32)

        dq = jnp.zeros((HD, 256), F32)
        dq = lax.fori_loop(low_ref[i], mid_ref[i], functools.partial(step, True), dq)
        dq = lax.fori_loop(mid_ref[i], i, functools.partial(step, False), dq)
        dq = step(True, i, dq)
        out_ref[pl.ds(4 * i, 4), 0:64, :] = (dq * scale).T.astype(BF).reshape(4, 64, HD)
        return 0

    lax.fori_loop(0, 8, tile, 0)
    for b in range(32):
        out_ref[b, 64:192, :] = (dk_ref[b * 128 : (b + 1) * 128, :] * scale).astype(BF)
        out_ref[b, 192:320, :] = dv_ref[b * 128 : (b + 1) * 128, :].astype(BF)


def attend_grad(received, d_attn, acc, lse, low, mid, starts, spots):
    return pl.pallas_call(
        functools.partial(attend_grad_kernel, LOG2E / math.sqrt(HD), 1.0 / math.sqrt(HD)),
        out_shape=jax.ShapeDtypeStruct((32, 320, HD), BF),
        in_specs=[SSPEC] * 2 + [VSPEC] * 6,
        out_specs=VSPEC,
        scratch_shapes=[
            pltpu.VMEM((HD, 4096), BF),
            pltpu.VMEM((4096, HD), F32),
            pltpu.VMEM((4096, HD), F32),
        ],
        compiler_params=params(),
        cost_estimate=pl.CostEstimate(
            flops=90 * 512 * 256 * 512, bytes_accessed=6 << 20, transcendentals=36 << 17
        ),
    )(low, mid, received, d_attn, acc, lse, starts, spots)


def unpack_kernel(
    d_ref, q_ref, k_ref, ss_ref, gq_ref, gk_ref, cos_ref, sin_ref, tq_ref, tk_ref, dv_ref, dot_ref, dgq_ref, dgk_ref
):
    lane = lax.broadcasted_iota(jnp.int32, (128, 128), 1)
    for r in range(2):
        rows = pl.ds(128 * r, 128)
        cos, sin = cos_ref[rows, :], sin_ref[rows, :]
        rq = lax.rsqrt(ss_ref[rows, 0:1] * (1.0 / 2048) + EPSILON)
        rk = lax.rsqrt(ss_ref[rows, 64:65] * (1.0 / 1024) + EPSILON)
        dot_q = jnp.zeros((128, 1), F32)
        dot_k = jnp.zeros((128, 1), F32)
        for h in range(4):
            at = r * 16 + h * 4
            for g in range(2):
                cols = pl.ds((h * 2 + g) * HD, HD)
                d = d_ref[at : at + 4, g * 32 : (g + 1) * 32, :].reshape(128, HD).astype(F32)
                d = rope_backward(d, cos, sin)
                q = q_ref[rows, cols]
                t = d * gq_ref[:, cols]
                tq_ref[rows, cols] = t
                dot_q += jnp.sum(t * q, axis=1, keepdims=True)
                part = jnp.sum(d * q * rq, axis=0, keepdims=True)
                dgq_ref[:, cols] = part if r == 0 else dgq_ref[:, cols] + part
            cols = pl.ds(h * HD, HD)
            dk = d_ref[at, 64:192, :].astype(F32)
            dv = d_ref[at, 192:320, :].astype(F32)
            for j in range(1, 4):
                dk += d_ref[at + j, 64:192, :].astype(F32)
                dv += d_ref[at + j, 192:320, :].astype(F32)
            dv_ref[rows, cols] = dv.astype(BF)
            d = rope_backward(dk, cos, sin)
            k = k_ref[rows, cols]
            t = d * gk_ref[:, cols]
            tk_ref[rows, cols] = t
            dot_k += jnp.sum(t * k, axis=1, keepdims=True)
            part = jnp.sum(d * k * rk, axis=0, keepdims=True)
            dgk_ref[:, cols] = part if r == 0 else dgk_ref[:, cols] + part
        dot_ref[rows, :] = jnp.where(lane < 64, dot_q, dot_k)


def unpack_grads(d, q_pre, k_pre, ss, gq, gk, cos, sin):
    return pl.pallas_call(
        unpack_kernel,
        out_shape=[
            jax.ShapeDtypeStruct((256, 1024), F32),
            jax.ShapeDtypeStruct((256, 512), F32),
            jax.ShapeDtypeStruct((256, 512), BF),
            jax.ShapeDtypeStruct((256, 128), F32),
            jax.ShapeDtypeStruct((1, 1024), F32),
            jax.ShapeDtypeStruct((1, 512), F32),
        ],
        in_specs=[VSPEC] * 8,
        out_specs=[VSPEC] * 6,
        compiler_params=params(),
        cost_estimate=pl.CostEstimate(flops=4 << 20, bytes_accessed=6 << 20, transcendentals=512),
    )(d, q_pre, k_pre, ss, gq, gk, cos, sin)


def row_places(row_lengths, spots):
    ends = jnp.cumsum(row_lengths)
    passed = spots[:, None] >= ends[None, :]
    return jnp.sum(jnp.where(passed, row_lengths[None, :], 0), axis=1)


def rms(v, g):
    r = lax.rsqrt(jnp.mean(v * v, axis=-1, keepdims=True) + EPSILON)
    return v * r * g, r


def rms_back(v, r, g, d):
    t = d * g
    dv = r * t - v * (r * r * r * jnp.mean(t * v, axis=-1, keepdims=True))
    return dv, jnp.sum(d * v * r, axis=0)


def dot_nn(a, b):
    return lax.dot_general(a, b, (((1,), (0,)), ((), ())), preferred_element_type=F32)


def dot_nt(a, b):
    return lax.dot_general(a, b, (((1,), (1,)), ((), ())), preferred_element_type=F32)


def dot_tn(a, b):
    return lax.dot_general(a, b, (((0,), (0,)), ((), ())), preferred_element_type=F32)


def halve(w, core):
    half = w.shape[1] // 2
    mine = lax.dynamic_slice_in_dim(w, core * half, half, 1)
    other = lax.dynamic_slice_in_dim(w, (1 - core) * half, half, 1)
    return mine, other


def chip_shard(weights, core):
    halves = [halve(w, core) for w in weights]
    mine = jnp.concatenate([m for m, _ in halves], axis=1)
    got = swap(jnp.concatenate([o for _, o in halves], axis=1))
    first = jnp.where(core == 0, mine, got)
    second = jnp.where(core == 0, got, mine)
    return jnp.concatenate([first, second], axis=0)


def body(
    block_input,
    out_grad,
    lengths,
    w_query,
    w_key,
    w_value,
    w_out,
    w_gate,
    w_up,
    w_down,
    gain_query,
    gain_key,
    gain_attn,
    gain_mlp,
):
    core = lax.axis_index("c")
    block = lax.axis_index("y") * 8 + lax.axis_index("xl") * 4 + lax.axis_index("z")

    shard1 = chip_shard((w_query, w_key, w_value, w_out.T), core)
    wq, wkv, wo = gather_cube([shard1[:, :1024], shard1[:, 1024:2048], shard1[:, 2048:]])
    shard2 = chip_shard((w_gate, w_up, w_down.T), core)
    wg, wu, wd = gather_cube([shard2[:, :1536], shard2[:, 1536:3072], shard2[:, 3072:]])
    wq, wkv, wo, wg, wu, wd = [w.reshape(1024, -1) for w in (wq, wkv, wo, wg, wu, wd)]

    gains = jnp.concatenate([gain_query, gain_key, gain_attn, gain_mlp])
    gains = jnp.broadcast_to(jnp.pad(gains, (0, 88))[None, None, :], (128, 8, 128))
    gains = lax.all_to_all(gains, AXES, split_axis=0, concat_axis=0, tiled=False)
    gains = gains[:, 0, :].astype(F32)
    gq = lax.dynamic_slice_in_dim(gains[:, 0:16].reshape(1, 2048), core * 1024, 1024, 1)
    gk = lax.dynamic_slice_in_dim(gains[:, 16:24].reshape(1, 1024), core * 512, 512, 1)

    def chip_order(v):
        return v.reshape(2, 2, 4, 2, 4, 8).transpose(0, 3, 2, 4, 1, 5).reshape(1, 1024)

    ga, gm = chip_order(gains[:, 24:32]), chip_order(gains[:, 32:40])

    d = lax.broadcasted_iota(jnp.int32, (1024, 1024), 1)
    source = (
        (d // 512) * 512
        + ((d // 8) % 2) * 256
        + ((d // 64) % 4) * 64
        + ((d // 256) % 2) * 32
        + ((d // 16) % 4) * 8
        + d % 8
    )
    reorder = (lax.broadcasted_iota(jnp.int32, (1024, 1024), 0) == source).astype(BF)
    x16 = dot_nn(block_input[0], reorder).astype(BF)
    c16 = dot_nn(out_grad[0], reorder).astype(BF)
    x256 = jnp.concatenate([x16, swap(x16)], axis=0)

    my_lengths = lengths[0]
    other_lengths = swap(my_lengths)
    here = block * 128 + jnp.arange(128, dtype=jnp.int32)
    offset = jnp.concatenate(
        [here - row_places(my_lengths, here), here - row_places(other_lengths, here)]
    )
    frequency = THETA ** (-(jnp.arange(64, dtype=F32) * 2.0 / HD))
    angles = offset.astype(F32)[:, None] * frequency[None, :]
    cosine, sine = jnp.cos(angles), jnp.sin(angles)
    cos2 = jnp.concatenate([cosine, cosine], axis=1)
    sin2 = jnp.concatenate([-sine, sine], axis=1)

    task_lengths = jnp.where(block // 16 == 0, my_lengths, other_lengths)
    spots = (
        jnp.arange(32, dtype=jnp.int32)[:, None, None] * 128
        + (block % 4) * 32
        + jnp.arange(32, dtype=jnp.int32)[None, None, :]
    )
    spots = jnp.broadcast_to(spots, (32, 2, 32)).reshape(2048)
    starts = row_places(task_lengths, spots).reshape(8, 1, 256)
    spots = spots.reshape(8, 1, 256)
    tiles = jnp.arange(8, dtype=jnp.int32)
    low = jnp.minimum(jnp.min(starts, axis=(1, 2)) // 512, tiles)
    mid = jnp.clip((jnp.max(starts, axis=(1, 2)) + 511) // 512, low, tiles)

    q_pre, k_pre, v16, ss = project_qkv(x256, wq, wkv)
    ss_other = swap(ss)
    ss = ss + jnp.concatenate([ss_other[128:], ss_other[:128]], axis=0)
    packed = pack_qkv(q_pre, k_pre, v16, ss, gq, gk, cos2, sin2)
    received = lax.all_to_all(packed, SEQ, split_axis=0, concat_axis=0, tiled=False)
    attn, acc, lse = attend(received, low, mid, starts, spots)
    attn = lax.all_to_all(attn, SEQ, split_axis=0, concat_axis=0, tiled=False)

    def to_tokens(a):
        a = a.reshape(2, 4, 4, 2, 32, HD).transpose(0, 2, 4, 1, 3, 5)
        return a.reshape(256, 1024)

    def to_tasks(a):
        a = a.reshape(2, 4, 32, 4, 2, HD).transpose(0, 3, 1, 4, 2, 5)
        return a.reshape(32, 64, HD)

    def own_sum(part):
        return part[:128] + swap(part[128:])

    def both(a):
        return jnp.concatenate([a, swap(a)], axis=0)

    attn16 = to_tokens(attn)
    proj = own_sum(dot_nt(attn16, wo))
    post, r_attn = rms(proj, ga)
    middle = x16.astype(F32) + post
    mid256 = both(middle.astype(BF))
    gate = dot_nn(mid256, wg)
    up = dot_nn(mid256, wu)
    sig = jax.nn.sigmoid(gate)
    act16 = (gate * sig * up).astype(BF)
    down = own_sum(dot_nt(act16, wd))
    post, r_mlp = rms(down, gm)
    output = middle + post

    cot = c16.astype(F32)
    d_down, dg_mlp = rms_back(down, r_mlp, gm, cot)
    dd256 = both(d_down.astype(BF))
    d_act = dot_nn(dd256, wd)
    d_gate = (d_act * up * sig * (1.0 + gate * (1.0 - sig))).astype(BF)
    d_up = (d_act * gate * sig).astype(BF)
    grad_down = dot_tn(dd256, act16).astype(BF)
    grad_gate = dot_tn(mid256, d_gate).astype(BF)
    grad_up = dot_tn(mid256, d_up).astype(BF)
    d_middle = cot + own_sum(dot_nt(d_gate, wg) + dot_nt(d_up, wu))
    d_proj, dg_attn = rms_back(proj, r_attn, ga, d_middle)
    dp256 = both(d_proj.astype(BF))
    d_attn = to_tasks(dot_nn(dp256, wo).astype(BF))
    grad_out = dot_tn(dp256, attn16).astype(BF)

    def cube(a):
        return a.reshape(4, 4, 4, 16, -1)

    d_attn = lax.all_to_all(d_attn, SEQ, split_axis=0, concat_axis=0, tiled=False)
    s_gate, s_up, s_down = scatter_cube([cube(grad_gate), cube(grad_up), cube(grad_down)])

    d_pairs = attend_grad(received, d_attn, acc, lse, low, mid, starts, spots)
    d_pairs = lax.all_to_all(d_pairs, SEQ, split_axis=0, concat_axis=0, tiled=False)
    tq, tk, dv16, dots, dgq, dgk = unpack_grads(d_pairs, q_pre, k_pre, ss, gq, gk, cos2, sin2)
    dots_other = swap(dots)
    dots = dots + jnp.concatenate([dots_other[128:], dots_other[:128]], axis=0)
    rq = lax.rsqrt(ss[:, 0:1] * (1.0 / 2048) + EPSILON)
    rk = lax.rsqrt(ss[:, 64:65] * (1.0 / 1024) + EPSILON)
    dq16 = (rq * tq - q_pre * (rq * rq * rq * dots[:, 0:1] * (1.0 / 2048))).astype(BF)
    dk16 = (rk * tk - k_pre * (rk * rk * rk * dots[:, 64:65] * (1.0 / 1024))).astype(BF)
    dkv16 = jnp.concatenate([dk16, dv16], axis=1)
    grad_q = dot_tn(x256, dq16).astype(BF)
    grad_kv = dot_tn(x256, dkv16).astype(BF)
    s_q, s_kv, s_out = scatter_cube([cube(grad_q), cube(grad_kv), cube(grad_out)])
    d_x = d_middle + own_sum(dot_nt(dq16, wq) + dot_nt(dkv16, wkv))

    dgq = jnp.where(jnp.arange(2)[:, None] == core, dgq, 0.0).reshape(128, 16)
    dgk = jnp.where(jnp.arange(2)[:, None] == core, dgk, 0.0).reshape(128, 8)

    def mesh_order(v):
        return v.reshape(2, 2, 4, 4, 2, 8).transpose(0, 4, 2, 1, 3, 5).reshape(128, 8)

    dgains = jnp.concatenate([dgq, dgk, mesh_order(dg_attn), mesh_order(dg_mlp)], axis=1)
    dgains = jnp.broadcast_to(jnp.pad(dgains, ((0, 0), (0, 88)))[:, None, :], (128, 8, 128))
    dgains = lax.all_to_all(dgains, AXES, split_axis=0, concat_axis=0, tiled=False)
    dgains = jnp.sum(dgains[:, 0, :], axis=0)

    sums = jnp.concatenate([s_q, s_kv, s_out, s_gate, s_up, s_down], axis=1)
    mine = lax.dynamic_slice_in_dim(sums, core * 8, 8, 0)
    got = swap(lax.dynamic_slice_in_dim(sums, (1 - core) * 8, 8, 0))
    first = jnp.where(core == 0, mine, got)
    second = jnp.where(core == 0, got, mine)

    def whole(at, width):
        return jnp.concatenate([first[:, at : at + width], second[:, at : at + width]], axis=1)

    back = functools.partial(lax.dot_general, dimension_numbers=(((1,), (1,)), ((), ())))
    output = back(output, reorder.astype(F32), precision=HIGHEST)
    d_x = back(d_x, reorder.astype(F32), precision=HIGHEST)
    return (
        output[None],
        d_x[None],
        whole(0, 1024),
        whole(1024, 512),
        whole(1536, 512),
        whole(2048, 1024).T,
        whole(3072, 1536),
        whole(4608, 1536),
        whole(6144, 1536).T,
        dgains[0:16],
        dgains[16:24],
        dgains[24:32],
        dgains[32:40],
    )


def solution(mesh):
    cube_mesh = Mesh(mesh.devices.reshape(2, 2, 4, 2, 4), AXES)
    row, seq = ("xh", "c"), SEQ
    everything = row + seq
    tokens, rows, cols, vec = (
        P(row, seq, None),
        P(everything, None),
        P(None, everything),
        P(everything),
    )
    in_specs = (tokens, tokens, P(row, None), rows, rows, rows, cols, rows, rows, cols) + (vec,) * 4
    out_specs = (tokens, tokens, rows, rows, rows, cols, rows, rows, cols) + (vec,) * 4
    return jax.shard_map(body, mesh=cube_mesh, in_specs=in_specs, out_specs=out_specs, check_vma=False)
```

```python
import functools
import math

import jax
import jax.numpy as jnp
from jax import lax
from jax.experimental import pallas as pl
from jax.experimental.pallas import tpu as pltpu
from jax.sharding import Mesh, PartitionSpec as P

BF = jnp.bfloat16
F32 = jnp.float32
HD = 128
EPSILON = 1e-06
THETA = 500000.0
AXES = ("xh", "c", "y", "xl", "z")
SEQ = ("y", "xl", "z")
LOG2E = 1.4426950408889634
VMEM_LIMIT = 56 * 1024 * 1024
HIGHEST = lax.Precision.HIGHEST
COST = pl.CostEstimate(flops=1, bytes_accessed=1, transcendentals=0)


def swap(a):
    return lax.ppermute(a, "c", [(0, 1), (1, 0)])


def shift(a, ring, by, mirrored):
    axes = ("xh", "c", "xl") if ring == "x" else ("c", ring)

    def index(c, m):
        return (m // 2) * 4 + c * 2 + m % 2 if ring == "x" else c * 4 + m

    pairs = []
    for c in range(2):
        step = -by if (mirrored and c == 1) else by
        pairs += [(index(c, m), index(c, (m + step) % 4)) for m in range(4)]
    return lax.ppermute(a, axes, pairs)


def position(ring):
    if ring == "x":
        return lax.axis_index("xh") * 2 + lax.axis_index("xl")
    return lax.axis_index(ring)


def params(limit=VMEM_LIMIT):
    return pltpu.CompilerParams(vmem_limit_bytes=limit)


VSPEC = pl.BlockSpec(memory_space=pltpu.VMEM)
SSPEC = pl.BlockSpec(memory_space=pltpu.SMEM)
ASPEC = pl.BlockSpec(memory_space=pl.ANY)


RINGS = ("z", "x", "y")


def ring_spots(ring):
    here, sign = position(ring), 1 - 2 * lax.axis_index("c")
    return [(here - sign * n) % 4 for n in range(4)]


def onward(block, ring):
    return shift(block, ring, 1, True)


def plus(a, b):
    return (a.astype(F32) + b.astype(F32)).astype(BF)


NEAR = (0, 3, 1, 2)


def rope_forward(v, cos, sin):
    return v * cos + pltpu.roll(v, 64, 1) * sin


def rope_backward(d, cos, sin):
    return d * cos - pltpu.roll(d, 64, 1) * sin


def lane_sums(a):
    ones = jnp.ones((8, a.shape[1]), F32)
    rows = lax.dot_general(
        ones, a, (((1,), (1,)), ((), ())), precision=HIGHEST, preferred_element_type=F32
    )
    return rows[0:1]


def column(row):
    return jnp.broadcast_to(row, (128, 128)).T


def qkv_kernel(x_ref, w_ref, q_ref, k_ref, v_ref, ss_ref):
    for n in range(8):
        rows = pl.ds(128 * n, 128)
        pre = jnp.dot(x_ref[rows, :], w_ref[:, :512], preferred_element_type=F32)
        q, k = pre[:, :256], pre[:, 256:384]
        q_ref[rows, :] = q
        k_ref[rows, :] = k
        v_ref[rows, :] = pre[:, 384:].astype(BF)
        ss_ref[n : n + 1, :] = lane_sums(q * q)
        ss_ref[8 + n : 9 + n, :] = lane_sums(k * k)


def project_qkv(x, w):
    return pl.pallas_call(
        qkv_kernel,
        out_shape=[
            jax.ShapeDtypeStruct((1024, 256), F32),
            jax.ShapeDtypeStruct((1024, 128), F32),
            jax.ShapeDtypeStruct((1024, 128), BF),
            jax.ShapeDtypeStruct((16, 128), F32),
        ],
        in_specs=[VSPEC] * 2,
        out_specs=[VSPEC] * 4,
        compiler_params=params(),
        cost_estimate=COST,
    )(x, w)


def send_kernel(spot_ref, q_ref, k_ref, v_ref, scale_ref, gq_ref, gk_ref, cos_ref, sin_ref, out_ref):
    for n in range(8):
        r, spot = n // 4, spot_ref[n % 4]
        rows = pl.ds(128 * n, 128)
        cos, sin = cos_ref[rows, :], sin_ref[rows, :]
        rq, rk = column(scale_ref[n : n + 1, :]), column(scale_ref[8 + n : 9 + n, :])
        for g in range(2):
            cols = pl.ds(g * HD, HD)
            q = rope_forward(q_ref[rows, cols] * rq * gq_ref[:, cols], cos, sin).astype(BF)
            for j in range(4):
                out_ref[r * 4 + j, spot, g * 32 : (g + 1) * 32, :] = q[32 * j : 32 * j + 32]
        k = rope_forward(k_ref[rows, :] * rk * gk_ref[...], cos, sin).astype(BF)
        v = v_ref[rows, :]
        for j in range(4):
            out_ref[r * 4 + j, spot, 64:192, :] = k
            out_ref[r * 4 + j, spot, 192:320, :] = v


def pack_qkv(spots, q_pre, k_pre, v16, scales, gq, gk, cos, sin):
    return pl.pallas_call(
        send_kernel,
        out_shape=jax.ShapeDtypeStruct((8, 4, 320, HD), BF),
        in_specs=[SSPEC] + [VSPEC] * 8,
        out_specs=VSPEC,
        compiler_params=params(),
        cost_estimate=COST,
    )(spots, q_pre, k_pre, v16, scales, gq, gk, cos, sin)


def tile_mask(kt, starts, spots):
    keys = kt * 512 + lax.broadcasted_iota(jnp.int32, (512, 256), 0)
    return (keys >= starts) & (keys <= spots)


def attend_kernel(scale2, low_ref, mid_ref, r_ref, start_ref, spot_ref, out_ref, acc_ref, lse_ref, vt_ref):
    for b in range(32):
        vt_ref[:, b * 128 : (b + 1) * 128] = r_ref[b, 192:320, :].T

    def tile(i, _):
        q = r_ref[pl.ds(4 * i, 4), 0:64, :].reshape(256, HD)
        starts, spots = start_ref[i], spot_ref[i]

        def step(masked, kt, carry):
            top, total, acc = carry
            k = r_ref[pl.ds(4 * kt, 4), 64:192, :].reshape(512, HD)
            s = lax.dot_general(k, q, (((1,), (1,)), ((), ())), preferred_element_type=F32)
            s = s * scale2
            if masked:
                s = jnp.where(tile_mask(kt, starts, spots), s, -1e30)
            new_top = jnp.maximum(top, jnp.max(s, axis=0, keepdims=True))
            p = jnp.exp2(s - new_top)
            if masked:
                p = jnp.where(s > -1e29, p, 0.0)
            fade = jnp.exp2(top - new_top)
            total = total * fade + jnp.sum(p, axis=0, keepdims=True)
            vt = vt_ref[:, pl.ds(pl.multiple_of(kt * 512, 512), 512)]
            acc = acc * fade + jnp.dot(vt, p.astype(BF), preferred_element_type=F32)
            return new_top, total, acc

        carry = (
            jnp.full((1, 256), -1e30, F32),
            jnp.zeros((1, 256), F32),
            jnp.zeros((HD, 256), F32),
        )
        carry = lax.fori_loop(low_ref[i], mid_ref[i], functools.partial(step, True), carry)
        carry = lax.fori_loop(mid_ref[i], i, functools.partial(step, False), carry)
        top, total, acc = step(True, i, carry)
        acc = acc / total
        acc_ref[i] = acc
        lse_ref[i] = top + jnp.log2(total)
        out_ref[pl.ds(4 * i, 4)] = acc.T.astype(BF).reshape(4, 64, HD)
        return 0

    lax.fori_loop(0, 8, tile, 0)


def attend(received, low, mid, starts, spots):
    return pl.pallas_call(
        functools.partial(attend_kernel, LOG2E / math.sqrt(HD)),
        out_shape=[
            jax.ShapeDtypeStruct((32, 64, HD), BF),
            jax.ShapeDtypeStruct((8, HD, 256), F32),
            jax.ShapeDtypeStruct((8, 1, 256), F32),
        ],
        in_specs=[SSPEC] * 2 + [VSPEC] * 3,
        out_specs=[VSPEC] * 3,
        scratch_shapes=[pltpu.VMEM((HD, 4096), BF)],
        compiler_params=params(),
        cost_estimate=COST,
    )(low, mid, received, starts, spots)


def attend_grad_kernel(
    scale2, scale, low_ref, mid_ref, r_ref, do_ref, acc_ref, lse_ref, start_ref, spot_ref, out_ref, kt_ref, dk_ref, dv_ref
):
    for b in range(32):
        kt_ref[:, b * 128 : (b + 1) * 128] = r_ref[b, 64:192, :].T
    dk_ref[...] = jnp.zeros_like(dk_ref)
    dv_ref[...] = jnp.zeros_like(dv_ref)

    def tile(i, _):
        q = r_ref[pl.ds(4 * i, 4), 0:64, :].reshape(256, HD)
        do = do_ref[pl.ds(4 * i, 4)].reshape(256, HD)
        delta = jnp.sum(do.astype(F32).T * acc_ref[i], axis=0, keepdims=True)
        lse, starts, spots = lse_ref[i], start_ref[i], spot_ref[i]

        def step(masked, kt, dq):
            k = r_ref[pl.ds(4 * kt, 4), 64:192, :].reshape(512, HD)
            v = r_ref[pl.ds(4 * kt, 4), 192:320, :].reshape(512, HD)
            s = lax.dot_general(k, q, (((1,), (1,)), ((), ())), preferred_element_type=F32)
            e = s * scale2 - lse
            if masked:
                e = jnp.where(tile_mask(kt, starts, spots), e, -1e30)
            p = jnp.exp2(e)
            dp = lax.dot_general(v, do, (((1,), (1,)), ((), ())), preferred_element_type=F32)
            ds = (p * (dp - delta)).astype(BF)
            keys = pl.ds(pl.multiple_of(kt * 512, 512), 512)
            dv_ref[keys, :] += jnp.dot(p.astype(BF), do, preferred_element_type=F32)
            dk_ref[keys, :] += jnp.dot(ds, q, preferred_element_type=F32)
            return dq + jnp.dot(kt_ref[:, keys], ds, preferred_element_type=F32)

        dq = jnp.zeros((HD, 256), F32)
        dq = lax.fori_loop(low_ref[i], mid_ref[i], functools.partial(step, True), dq)
        dq = lax.fori_loop(mid_ref[i], i, functools.partial(step, False), dq)
        dq = step(True, i, dq)
        out_ref[pl.ds(4 * i, 4), 0:64, :] = (dq * scale).T.astype(BF).reshape(4, 64, HD)
        return 0

    lax.fori_loop(0, 8, tile, 0)
    for b in range(32):
        out_ref[b, 64:192, :] = (dk_ref[b * 128 : (b + 1) * 128, :] * scale).astype(BF)
        out_ref[b, 192:320, :] = dv_ref[b * 128 : (b + 1) * 128, :].astype(BF)


def attend_grad(received, d_attn, acc, lse, low, mid, starts, spots):
    return pl.pallas_call(
        functools.partial(attend_grad_kernel, LOG2E / math.sqrt(HD), 1.0 / math.sqrt(HD)),
        out_shape=jax.ShapeDtypeStruct((32, 320, HD), BF),
        in_specs=[SSPEC] * 2 + [VSPEC] * 6,
        out_specs=VSPEC,
        scratch_shapes=[
            pltpu.VMEM((HD, 4096), BF),
            pltpu.VMEM((4096, HD), F32),
            pltpu.VMEM((4096, HD), F32),
        ],
        compiler_params=params(),
        cost_estimate=COST,
    )(low, mid, received, d_attn, acc, lse, starts, spots)


def unpack_kernel(
    spot_ref, d_ref, q_ref, k_ref, scale_ref, gq_ref, gk_ref, cos_ref, sin_ref, tq_ref, tk_ref, dv_ref, dot_ref, dgq_ref, dgk_ref
):
    for n in range(8):
        r, spot = n // 4, spot_ref[n % 4]
        rows = pl.ds(128 * n, 128)
        cos, sin = cos_ref[rows, :], sin_ref[rows, :]
        rq, rk = column(scale_ref[n : n + 1, :]), column(scale_ref[8 + n : 9 + n, :])
        dot_q = jnp.zeros((128, HD), F32)
        for g in range(2):
            cols = pl.ds(g * HD, HD)
            d = jnp.concatenate(
                [d_ref[r * 4 + j, spot, g * 32 : (g + 1) * 32, :] for j in range(4)], axis=0
            ).astype(F32)
            d = rope_backward(d, cos, sin)
            q = q_ref[rows, cols]
            t = d * gq_ref[:, cols]
            tq_ref[rows, cols] = t
            dot_q += t * q
            part = jnp.sum(d * q * rq, axis=0, keepdims=True)
            dgq_ref[:, cols] = part if n == 0 else dgq_ref[:, cols] + part
        dk = d_ref[r * 4, spot, 64:192, :].astype(F32)
        dv = d_ref[r * 4, spot, 192:320, :].astype(F32)
        for j in range(1, 4):
            dk += d_ref[r * 4 + j, spot, 64:192, :].astype(F32)
            dv += d_ref[r * 4 + j, spot, 192:320, :].astype(F32)
        dv_ref[rows, :] = dv.astype(BF)
        d = rope_backward(dk, cos, sin)
        k = k_ref[rows, :]
        t = d * gk_ref[...]
        tk_ref[rows, :] = t
        part = jnp.sum(d * k * rk, axis=0, keepdims=True)
        dgk_ref[...] = part if n == 0 else dgk_ref[...] + part
        dot_ref[n : n + 1, :] = lane_sums(dot_q)
        dot_ref[8 + n : 9 + n, :] = lane_sums(t * k)


def unpack_grads(spots, d, q_pre, k_pre, scales, gq, gk, cos, sin):
    return pl.pallas_call(
        unpack_kernel,
        out_shape=[
            jax.ShapeDtypeStruct((1024, 256), F32),
            jax.ShapeDtypeStruct((1024, 128), F32),
            jax.ShapeDtypeStruct((1024, 128), BF),
            jax.ShapeDtypeStruct((16, 128), F32),
            jax.ShapeDtypeStruct((1, 256), F32),
            jax.ShapeDtypeStruct((1, 128), F32),
        ],
        in_specs=[SSPEC] + [VSPEC] * 8,
        out_specs=[VSPEC] * 6,
        compiler_params=params(),
        cost_estimate=COST,
    )(spots, d, q_pre, k_pre, scales, gq, gk, cos, sin)


def qkv_grad_kernel(x_ref, tq_ref, tk_ref, dv_ref, q_ref, k_ref, scale_ref, dot_ref, gain_ref, d_ref, out_ref):
    for n in range(8):
        rows = pl.ds(128 * n, 128)
        rq, rk = column(scale_ref[n : n + 1, :]), column(scale_ref[8 + n : 9 + n, :])
        eq = rq * rq * rq * column(dot_ref[n : n + 1, :]) * (1.0 / 2048)
        ek = rk * rk * rk * column(dot_ref[8 + n : 9 + n, :]) * (1.0 / 1024)
        for g in range(2):
            cols = pl.ds(g * HD, HD)
            d_ref[rows, cols] = (rq * tq_ref[rows, cols] - eq * q_ref[rows, cols]).astype(BF)
        d_ref[rows, 256:384] = (rk * tk_ref[rows, :] - ek * k_ref[rows, :]).astype(BF)
        d_ref[rows, 384:512] = dv_ref[rows, :]
    for n in range(8):
        rows = pl.ds(128 * n, 128)
        out_ref[rows, 0:512] = lax.dot_general(
            x_ref[:, rows], d_ref[...], (((0,), (0,)), ((), ())), preferred_element_type=F32
        ).astype(BF)
    out_ref[:, 512:640] = gain_ref[...]


def qkv_grads(x, tq, tk, dv16, q_pre, k_pre, scales, dots, gain_part):
    return pl.pallas_call(
        qkv_grad_kernel,
        out_shape=[
            jax.ShapeDtypeStruct((1024, 512), BF),
            jax.ShapeDtypeStruct((1024, 640), BF),
        ],
        in_specs=[VSPEC] * 9,
        out_specs=[VSPEC] * 2,
        compiler_params=params(),
        cost_estimate=COST,
    )(x, tq, tk, dv16, q_pre, k_pre, scales, dots, gain_part)


def dot_nn(a, b):
    return lax.dot_general(a, b, (((1,), (0,)), ((), ())), preferred_element_type=F32)


def dot_nt(a, b):
    return lax.dot_general(a, b, (((1,), (1,)), ((), ())), preferred_element_type=F32)


def dot_tn(a, b):
    return lax.dot_general(a, b, (((0,), (0,)), ((), ())), preferred_element_type=F32)


def rms_rate(v):
    return lax.rsqrt(jnp.mean(v * v, axis=-1, keepdims=True) + EPSILON)


def rms_back(v, g, d):
    r = rms_rate(v)
    t = d * g
    dv = r * t - v * (r * r * r * jnp.mean(t * v, axis=-1, keepdims=True))
    return dv, jnp.sum(d * v * r, axis=0, keepdims=True)


def call(kernel, out_shape, args, us):
    return pl.pallas_call(
        kernel,
        out_shape=[jax.ShapeDtypeStruct(s, t) for s, t in out_shape],
        in_specs=[SSPEC if a.ndim == 1 else VSPEC for a in args],
        out_specs=[VSPEC] * len(out_shape),
        compiler_params=params(),
        cost_estimate=COST,
    )(*args)


def proj_kernel(spot_ref, a_ref, *refs):
    chunks, (attn_ref, own_ref, other_ref) = refs[:4], refs[4:]
    for r in range(2):
        for j in range(4):
            rows = pl.ds(r * 128 + j * 32, 32)
            for h in range(4):
                for g in range(2):
                    piece = a_ref[(r * 4 + j) * 4 + h, g * 32 : (g + 1) * 32, :]
                    attn_ref[rows, (h * 2 + g) * HD : (h * 2 + g + 1) * HD] = piece
    lefts = [
        attn_ref[:, pl.ds(pl.multiple_of(spot_ref[n] * 256, 256), 256)] for n in range(4)
    ]
    for m in range(4):
        cols = pl.ds(256 * m, 256)
        part = dot_nt(lefts[0], chunks[0][cols, 0:256])
        for n in range(1, 4):
            part += dot_nt(lefts[n], chunks[n][cols, 0:256])
        own_ref[:, cols] = part[:128]
        other_ref[:, cols] = part[128:].astype(BF)


def middle_kernel(own_ref, got_ref, x_ref, g_ref, proj_ref, middle_ref, low_ref):
    proj = own_ref[...] + got_ref[...].astype(F32)
    middle = x_ref[...].astype(F32) + proj * rms_rate(proj) * g_ref[...]
    proj_ref[...] = proj
    middle_ref[...] = middle
    low_ref[...] = middle.astype(BF)


def hidden_columns(n):
    return 256 if n < 4 else 0


def forward_kernel(mo_ref, mt_ref, *refs):
    chunks, (gate_ref, up_ref, act_ref, own_ref, other_ref) = refs[:12], refs[12:]
    m = jnp.concatenate([mo_ref[...], mt_ref[...]], axis=0)
    for n, w_ref in enumerate(chunks):
        at = hidden_columns(n)
        both = dot_nn(m, w_ref[:, at : at + 256])
        gate, up = both[:, :128], both[:, 128:]
        gate_ref[n] = gate
        up_ref[n] = up
        act_ref[n] = (gate / (1.0 + jnp.exp(-gate)) * up).astype(BF)
    for k in range(4):
        cols = pl.ds(256 * k, 256)
        part = jnp.zeros((256, 256), F32)
        for n, w_ref in enumerate(chunks):
            at = hidden_columns(n) + 256
            part += dot_nt(act_ref[n], w_ref[cols, at : at + 128])
        own_ref[:, cols] = part[:128]
        other_ref[:, cols] = part[128:].astype(BF)


def turn_kernel(own_ref, got_ref, middle_ref, g_ref, c_ref, out_ref, dd_ref, dg_ref):
    down = own_ref[...] + got_ref[...].astype(F32)
    out_ref[...] = middle_ref[...] + down * rms_rate(down) * g_ref[...]
    d_down, dg_ref[...] = rms_back(down, g_ref[...], c_ref[...].astype(F32))
    dd_ref[...] = d_down.astype(BF)


def backward_kernel(do_ref, dt_ref, gate_ref, up_ref, *refs):
    chunks, (dboth_ref, own_ref, other_ref) = refs[:12], refs[12:]
    dd = jnp.concatenate([do_ref[...], dt_ref[...]], axis=0)
    for n, w_ref in enumerate(chunks):
        at = hidden_columns(n)
        d_act = dot_nn(dd, w_ref[:, at + 256 : at + 384])
        gate, up = gate_ref[n], up_ref[n]
        sig = 1.0 / (1.0 + jnp.exp(-gate))
        dboth_ref[n, :, 0:128] = (d_act * up * sig * (1.0 + gate * (1.0 - sig))).astype(BF)
        dboth_ref[n, :, 128:256] = (d_act * gate * sig).astype(BF)
    for k in range(4):
        cols = pl.ds(256 * k, 256)
        part = jnp.zeros((256, 256), F32)
        for n, w_ref in enumerate(chunks):
            at = hidden_columns(n)
            part += dot_nt(dboth_ref[n], w_ref[cols, at : at + 256])
        own_ref[:, cols] = part[:128]
        other_ref[:, cols] = part[128:].astype(BF)


def d_proj_kernel(own_ref, got_ref, c_ref, proj_ref, g_ref, dm_ref, dp_ref, dg_ref):
    d_middle = c_ref[...].astype(F32) + own_ref[...] + got_ref[...].astype(F32)
    d_proj, dg_ref[...] = rms_back(proj_ref[...], g_ref[...], d_middle)
    dm_ref[...] = d_middle
    dp_ref[...] = d_proj.astype(BF)


def d_attn_kernel(spot_ref, do_ref, dt_ref, *refs):
    chunks, out_ref = refs[:4], refs[4]
    dp = jnp.concatenate([do_ref[...], dt_ref[...]], axis=0)
    for n in range(4):
        part = dot_nn(dp, chunks[n][:, 0:256]).astype(BF)
        for r in range(2):
            for j in range(4):
                for g in range(2):
                    piece = part[r * 128 + j * 32 : r * 128 + (j + 1) * 32, g * HD : (g + 1) * HD]
                    out_ref[(r * 4 + j) * 4 + spot_ref[n], g * 32 : (g + 1) * 32, :] = piece


def hidden_grads_kernel(first, mo_ref, mt_ref, do_ref, dt_ref, dboth_ref, act_ref, *outs):
    m = jnp.concatenate([mo_ref[...], mt_ref[...]], axis=0)
    dd = jnp.concatenate([do_ref[...], dt_ref[...]], axis=0)
    for n, out_ref in enumerate(outs):
        at = hidden_columns(first + n)
        out_ref[:, at : at + 256] = dot_tn(m, dboth_ref[first + n]).astype(BF)
        out_ref[:, at + 256 : at + 384] = dot_tn(dd, act_ref[first + n]).astype(BF)


def out_grads_kernel(spot_ref, mo_ref, mt_ref, do_ref, dt_ref, dboth_ref, act_ref, po_ref, pt_ref, attn_ref, *outs):
    hidden_grads_kernel(0, mo_ref, mt_ref, do_ref, dt_ref, dboth_ref, act_ref, *outs)
    dp = jnp.concatenate([po_ref[...], pt_ref[...]], axis=0)
    for n, out_ref in enumerate(outs):
        right = attn_ref[:, pl.ds(pl.multiple_of(spot_ref[n] * 256, 256), 256)]
        out_ref[:, 0:256] = dot_tn(dp, right).astype(BF)


def row_places(row_lengths, spots):
    ends = jnp.cumsum(row_lengths)
    passed = spots[:, None] >= ends[None, :]
    return jnp.sum(jnp.where(passed, row_lengths[None, :], 0), axis=1)


def after(value, *others):
    return lax.optimization_barrier((value,) + others)[0]


def group_sum(rows):
    a = rows.reshape(2, 2, 4, 128)
    total = a
    for by in (1, -1, 2):
        got = shift(rows, "z", by, False).reshape(2, 2, 4, 128)
        pick = [NEAR.index((NEAR[k] + by) % 4) for k in range(4)]
        total = total + jnp.stack([got[:, :, p] for p in pick], axis=2)
    return (total + swap(total)[:, ::-1]).reshape(16, 128)


def body(
    block_input,
    out_grad,
    lengths,
    w_query,
    w_key,
    w_value,
    w_out,
    w_gate,
    w_up,
    w_down,
    gain_query,
    gain_key,
    gain_attn,
    gain_mlp,
):
    core = lax.axis_index("c")
    z = lax.axis_index("z")
    peer = lax.axis_index("y") * 2 + lax.axis_index("xl")
    head = core * 4 + z
    my_x = block_input[0]

    columns = jnp.concatenate(
        [w_query.reshape(8, 8, 256), w_key.reshape(8, 8, 128), w_value.reshape(8, 8, 128)], axis=2
    )
    columns = columns.transpose(1, 0, 2).reshape(1, 2, 1, 1, 4, 8, 512)
    gains = jnp.concatenate([gain_query, gain_key, gain_attn, gain_mlp])
    gains = jnp.pad(gains[None, :], ((0, 7), (0, 88)))
    columns = jnp.concatenate(
        [columns, jnp.broadcast_to(gains, (1, 2, 1, 1, 4, 8, 128))], axis=-1
    )
    columns = jnp.broadcast_to(columns, (2, 2, 4, 2, 4, 8, 640)).reshape(128, 8, 640)
    columns = lax.all_to_all(columns, AXES, split_axis=0, concat_axis=0, tiled=False)
    gains = columns[:, 0, 512:552].astype(F32)
    w_head = columns.reshape(1024, 640)
    my_gains = lax.dynamic_slice_in_dim(gains, head * 16, 16, 0)
    gq, gk = my_gains[:, 0:16].reshape(1, 256), my_gains[:, 16:24].reshape(1, 128)

    ga, gm = gains[:, 24:32].reshape(1, 1024), gains[:, 32:40].reshape(1, 1024)

    def everywhere(a, shape):
        a = a.reshape(shape + (8, a.shape[-1]))
        return jnp.broadcast_to(a, (2, 2, 4, 2, 4, 8, a.shape[-1]))

    hidden = [w.reshape(8, 2, 3, 4, 128) for w in (w_gate, w_up, w_down.T)]
    hidden = jnp.concatenate(hidden, axis=-1).transpose(2, 1, 3, 0, 4)
    first = w_out.T.reshape(8, 2, 4, 256).transpose(1, 2, 0, 3)
    first = jnp.concatenate([first, hidden[0]], axis=-1)
    over_x = hidden[1].reshape(2, 2, 2, 8, 384).transpose(1, 0, 2, 3, 4)
    weights = jnp.concatenate(
        [
            everywhere(first, (1, 2, 1, 1, 4)),
            everywhere(over_x, (2, 2, 1, 2, 1)),
            everywhere(hidden[2], (1, 2, 4, 1, 1)),
        ],
        axis=-1,
    ).reshape(128, 8, 1408)
    weights = after(weights, w_head)
    weights = lax.all_to_all(weights, AXES, split_axis=0, concat_axis=0, tiled=False)
    weights = weights.reshape(1024, 1408)

    chunks = jnp.concatenate(
        [my_x] + [shift(my_x, "z", by, False) for by in (1, -1, 2)], axis=0
    )
    x_group = jnp.concatenate([chunks, swap(chunks)], axis=0)
    spots = jnp.stack([(z + n) % 4 for n in NEAR])

    q_pre, k_pre, v16, ss = project_qkv(x_group, w_head)
    lengths = after(lengths, ss)

    my_lengths = lengths[0]
    other_lengths = swap(my_lengths)
    here = (peer * 4 + spots[:, None]) * 128 + jnp.arange(128, dtype=jnp.int32)[None, :]
    here = here.reshape(512)
    offset = jnp.concatenate(
        [here - row_places(my_lengths, here), here - row_places(other_lengths, here)]
    )
    frequency = THETA ** (-(jnp.arange(64, dtype=F32) * 2.0 / HD))
    angles = offset.astype(F32)[:, None] * frequency[None, :]
    cosine, sine = jnp.cos(angles), jnp.sin(angles)
    cos2 = jnp.concatenate([cosine, cosine], axis=1)
    sin2 = jnp.concatenate([-sine, sine], axis=1)

    task_lengths = jnp.where(peer // 4 == 0, my_lengths, other_lengths)
    task_spots = (
        jnp.arange(32, dtype=jnp.int32)[:, None, None] * 128
        + (peer % 4) * 32
        + jnp.arange(32, dtype=jnp.int32)[None, None, :]
    )
    task_spots = jnp.broadcast_to(task_spots, (32, 2, 32)).reshape(2048)
    starts = row_places(task_lengths, task_spots).reshape(8, 1, 256)
    task_spots = task_spots.reshape(8, 1, 256)
    tiles = jnp.arange(8, dtype=jnp.int32)
    low = jnp.minimum(jnp.min(starts, axis=(1, 2)) // 512, tiles)
    mid = jnp.clip((jnp.max(starts, axis=(1, 2)) + 511) // 512, low, tiles)

    width = jnp.concatenate([jnp.full((8, 1), 2048.0), jnp.full((8, 1), 1024.0)])
    scales = lax.rsqrt(group_sum(ss) / width + EPSILON)
    packed = pack_qkv(spots, q_pre, k_pre, v16, scales, gq, gk, cos2, sin2)
    packed, weights = lax.optimization_barrier((packed, weights))
    received = lax.all_to_all(packed, ("y", "xl"), split_axis=0, concat_axis=0, tiled=False)
    chunks = [[w] for w in jnp.split(weights, [640, 1024], axis=1)]

    def step(value):
        value, *latest = lax.optimization_barrier((value, *[group[-1] for group in chunks]))
        for ring, group, last in zip(RINGS, chunks, latest):
            group[-1] = last
            group.append(onward(last, ring))
        return value

    for ring, group in zip(RINGS, chunks):
        group.append(onward(group[0], ring))
    received = step(received.reshape(32, 320, HD))
    attn, acc, lse = attend(received, low, mid, starts, task_spots)
    attn = step(attn)
    attn = lax.all_to_all(attn, SEQ, split_axis=0, concat_axis=0, tiled=False)
    z_spots = jnp.stack(ring_spots("z")).astype(jnp.int32)
    chunks = [w for group in chunks for w in group]

    x16, c16 = block_input[0], out_grad[0]
    flat, half, vec = (256, 1024), (128, 1024), (1, 1024)
    wide, both = (12, 256, 128), (12, 256, 256)
    attn16, own, other = call(
        proj_kernel, [(flat, BF), (half, F32), (half, BF)], (z_spots, attn, *chunks[:4]), 4
    )
    proj, middle, mid_own = call(
        middle_kernel, [(half, F32), (half, F32), (half, BF)], (own, swap(other), x16, ga), 2
    )
    mid_other = swap(mid_own)
    gate, up, act16, own, other = call(
        forward_kernel,
        [(wide, F32), (wide, F32), (wide, BF), (half, F32), (half, BF)],
        (mid_own, mid_other, *chunks),
        6,
    )
    output, dd_own, dg_mlp = call(
        turn_kernel,
        [(half, F32), (half, BF), (vec, F32)],
        (own, swap(other), middle, gm, c16),
        2,
    )
    dd_other = swap(dd_own)
    d_both, own, other = call(
        backward_kernel,
        [(both, BF), (half, F32), (half, BF)],
        (dd_own, dd_other, gate, up, *chunks),
        7,
    )
    d_middle, dp_own, dg_attn = call(
        d_proj_kernel,
        [(half, F32), (half, BF), (vec, F32)],
        (own, swap(other), c16, proj, ga),
        2,
    )
    dp_other = swap(dp_own)
    (d_attn,) = call(
        d_attn_kernel, [((32, 64, HD), BF)], (z_spots, dp_own, dp_other, *chunks[:4]), 3
    )

    d_attn, d_both = lax.optimization_barrier((d_attn, d_both))
    d_attn = lax.all_to_all(d_attn, SEQ, split_axis=0, concat_axis=0, tiled=False)
    sources = (mid_own, mid_other, dd_own, dd_other, d_both, act16)
    later = call(
        functools.partial(hidden_grads_kernel, 4), [((1024, 384), BF)] * 8, sources, 4
    )
    first = call(
        out_grads_kernel,
        [((1024, 640), BF)] * 4,
        (z_spots, *sources, dp_own, dp_other, attn16),
        4,
    )
    grads = (first, later[:4], later[4:])
    runs = [onward(g[1], ring) for g, ring in zip(grads, RINGS)]
    d_attn, *runs = lax.optimization_barrier((d_attn, *runs))
    runs = [plus(g[2], run) for g, run in zip(grads, runs)]
    d_attn, *runs = lax.optimization_barrier((d_attn, *runs))
    runs = [onward(run, ring) for run, ring in zip(runs, RINGS)]

    d_pairs = attend_grad(received, d_attn, acc, lse, low, mid, starts, task_spots)
    d_pairs, *runs = lax.optimization_barrier((d_pairs, *runs))
    runs = [plus(g[3], run) for g, run in zip(grads, runs)]
    runs = [onward(run, ring) for run, ring in zip(runs, RINGS)]
    d_pairs = d_pairs.reshape(8, 4, 320, HD)
    d_pairs = lax.all_to_all(d_pairs, ("y", "xl"), split_axis=0, concat_axis=0, tiled=False)
    runs = jnp.concatenate([plus(g[0], run) for g, run in zip(grads, runs)], axis=1)
    d_pairs, runs = lax.optimization_barrier((d_pairs, runs))
    sums = lax.all_to_all(
        runs.reshape(128, 8, 1408), AXES, split_axis=0, concat_axis=0, tiled=False
    )
    tq, tk, dv16, dots, dgq, dgk = unpack_grads(
        spots, d_pairs, q_pre, k_pre, scales, gq, gk, cos2, sin2
    )
    dots = group_sum(dots)

    mine_here = (jnp.arange(128)[:, None] // 16) == head
    dgains = jnp.concatenate(
        [
            jnp.where(mine_here, jnp.tile(dgq.reshape(16, 16), (8, 1)), 0.0),
            jnp.where(mine_here, jnp.tile(dgk.reshape(16, 8), (8, 1)), 0.0),
            dg_attn.reshape(128, 8),
            dg_mlp.reshape(128, 8),
        ],
        axis=1,
    )
    coarse = dgains.astype(BF)
    fine = (dgains - coarse.astype(F32)).astype(BF)
    gain_part = jnp.pad(jnp.concatenate([coarse, fine], axis=1), ((0, 0), (0, 48)))
    gain_part = jnp.pad(gain_part[:, None, :], ((0, 0), (0, 7), (0, 0))).reshape(1024, 128)
    d_pre, grad_head = qkv_grads(
        x_group, tq, tk, dv16, q_pre, k_pre, scales, dots, gain_part
    )
    grad_head, sums = lax.optimization_barrier((grad_head, sums))
    grad_head = lax.all_to_all(
        grad_head.reshape(128, 8, 640), AXES, split_axis=0, concat_axis=0, tiled=False
    )
    d_x = dot_nt(d_pre, w_head[:, :512]).astype(BF)
    d_x = (d_x[:512].astype(F32) + swap(d_x[512:]).astype(F32)).astype(BF)
    d_middle = d_middle + d_x[:128].astype(F32)
    for n, by in enumerate((-1, 1, 2)):
        d_middle = d_middle + shift(d_x[128 * (n + 1) : 128 * (n + 2)], "z", by, False).astype(F32)

    heads = grad_head.reshape(2, 2, 4, 2, 4, 8, 640).astype(F32).sum(axis=(0, 2, 3))
    dgains = heads[:, :, 0, 512:592].sum(axis=(0, 1))
    dgains = dgains[0:40] + dgains[40:80]
    heads = heads.reshape(8, 8, 640).transpose(1, 0, 2)

    sums = sums.reshape(2, 2, 4, 2, 4, 8, 1408).astype(F32)
    sum_z = sums[..., :640].sum(axis=(0, 2, 3))
    sum_x = sums[..., 640:1024].sum(axis=(2, 4)).transpose(1, 0, 2, 3, 4).reshape(2, 4, 8, 384)
    sum_y = sums[..., 1024:].sum(axis=(0, 3, 4))
    hidden = jnp.stack([sum_z[..., 256:], sum_x, sum_y], axis=1).transpose(3, 0, 1, 2, 4)
    hidden = [hidden[..., 128 * n : 128 * (n + 1)].reshape(8, 3072) for n in range(3)]
    return (
        output[None],
        d_middle[None],
        heads[:, :, 0:256].reshape(8, 2048),
        heads[:, :, 256:384].reshape(8, 1024),
        heads[:, :, 384:512].reshape(8, 1024),
        sum_z[..., :256].transpose(2, 0, 1, 3).reshape(8, 2048).T,
        hidden[0],
        hidden[1],
        hidden[2].T,
        dgains[0:16],
        dgains[16:24],
        dgains[24:32],
        dgains[32:40],
    )


def solution(mesh):
    cube_mesh = Mesh(mesh.devices.reshape(2, 2, 4, 2, 4), AXES)
    row, seq = ("xh", "c"), SEQ
    everything = row + seq
    tokens, rows, cols, vec = (
        P(row, seq, None),
        P(everything, None),
        P(None, everything),
        P(everything),
    )
    in_specs = (tokens, tokens, P(row, None), rows, rows, rows, cols, rows, rows, cols) + (vec,) * 4
    out_specs = (tokens, tokens, rows, rows, rows, cols, rows, rows, cols) + (vec,) * 4
    return jax.shard_map(body, mesh=cube_mesh, in_specs=in_specs, out_specs=out_specs, check_vma=False)
```

```python
import functools
import math

import jax
import jax.numpy as jnp
from jax import lax
from jax.experimental import pallas as pl
from jax.experimental.pallas import tpu as pltpu
from jax.sharding import Mesh, PartitionSpec as P

BF = jnp.bfloat16
F32 = jnp.float32
HD = 128
EPSILON = 1e-06
THETA = 500000.0
AXES = ("xh", "c", "y", "xl", "z")
SEQ = ("y", "xl", "z")
LOG2E = 1.4426950408889634
HIGHEST = lax.Precision.HIGHEST
COST = pl.CostEstimate(flops=1, bytes_accessed=1, transcendentals=0)


def swap(a):
    return lax.ppermute(a, "c", [(0, 1), (1, 0)])


def shift(a, ring, by, mirrored):
    axes = ("xh", "c", "xl") if ring == "x" else ("c", ring)

    def index(c, m):
        return (m // 2) * 4 + c * 2 + m % 2 if ring == "x" else c * 4 + m

    pairs = []
    for c in range(2):
        step = -by if (mirrored and c == 1) else by
        pairs += [(index(c, m), index(c, (m + step) % 4)) for m in range(4)]
    return lax.ppermute(a, axes, pairs)


def position(ring):
    if ring == "x":
        return lax.axis_index("xh") * 2 + lax.axis_index("xl")
    return lax.axis_index(ring)


def params(arrays, scratch=0):
    total = scratch + sum(math.prod(a.shape) * jnp.dtype(a.dtype).itemsize for a in arrays)
    return pltpu.CompilerParams(vmem_limit_bytes=total + total // 8 + (3 << 20))


VSPEC = pl.BlockSpec(memory_space=pltpu.VMEM)
SSPEC = pl.BlockSpec(memory_space=pltpu.SMEM)
ASPEC = pl.BlockSpec(memory_space=pl.ANY)


RINGS = ("z", "x", "y")


def ring_spots(ring):
    here, sign = position(ring), 1 - 2 * lax.axis_index("c")
    return [(here - sign * n) % 4 for n in range(4)]


def onward(block, ring):
    return shift(block, ring, 1, True)


def plus(a, b):
    return (a.astype(F32) + b.astype(F32)).astype(BF)


NEAR = (0, 3, 1, 2)


def rope_forward(v, cos, sin):
    return v * cos + pltpu.roll(v, 64, 1) * sin


def rope_backward(d, cos, sin):
    return d * cos - pltpu.roll(d, 64, 1) * sin


def lane_sums(a):
    ones = jnp.ones((8, a.shape[1]), F32)
    rows = lax.dot_general(
        ones, a, (((1,), (1,)), ((), ())), precision=HIGHEST, preferred_element_type=F32
    )
    return rows[0:1]


def column(row):
    return jnp.broadcast_to(row, (128, 128)).T


def qkv_kernel(w_ref, *refs):
    xs, (q_ref, k_ref, v_ref, ss_ref) = refs[:5], refs[5:]
    for n in range(8):
        rows = pl.ds(128 * n, 128)
        x = xs[n][...] if n < 4 else xs[4][128 * (n - 4) : 128 * (n - 3), :]
        pre = jnp.dot(x, w_ref[:, :512], preferred_element_type=F32)
        q, k = pre[:, :256], pre[:, 256:384]
        q_ref[rows, :] = q
        k_ref[rows, :] = k
        v_ref[rows, :] = pre[:, 384:].astype(BF)
        ss_ref[n : n + 1, :] = lane_sums(q * q)
        ss_ref[8 + n : 9 + n, :] = lane_sums(k * k)


def project_qkv(x, w):
    args = (w, *x)
    outs = [
            jax.ShapeDtypeStruct((1024, 256), F32),
            jax.ShapeDtypeStruct((1024, 128), F32),
            jax.ShapeDtypeStruct((1024, 128), BF),
            jax.ShapeDtypeStruct((16, 128), F32),
        ]
    return pl.pallas_call(
        qkv_kernel,
        out_shape=outs,
        in_specs=[VSPEC] * 6,
        out_specs=[VSPEC] * 4,
        compiler_params=params((*args, *outs), 0),
        cost_estimate=COST,
    )(*args)


def send_kernel(spot_ref, q_ref, k_ref, v_ref, scale_ref, gq_ref, gk_ref, cos_ref, sin_ref, out_ref):
    for n in range(8):
        r, spot = n // 4, spot_ref[n % 4]
        rows = pl.ds(128 * n, 128)
        cos, sin = cos_ref[rows, :], sin_ref[rows, :]
        rq, rk = column(scale_ref[n : n + 1, :]), column(scale_ref[8 + n : 9 + n, :])
        for g in range(2):
            cols = pl.ds(g * HD, HD)
            q = rope_forward(q_ref[rows, cols] * rq * gq_ref[:, cols], cos, sin).astype(BF)
            for j in range(4):
                out_ref[r * 4 + j, spot, g * 32 : (g + 1) * 32, :] = q[32 * j : 32 * j + 32]
        k = rope_forward(k_ref[rows, :] * rk * gk_ref[...], cos, sin).astype(BF)
        v = v_ref[rows, :]
        for j in range(4):
            out_ref[r * 4 + j, spot, 64:192, :] = k
            out_ref[r * 4 + j, spot, 192:320, :] = v


def pack_qkv(spots, q_pre, k_pre, v16, scales, gq, gk, cos, sin):
    args = (spots, q_pre, k_pre, v16, scales, gq, gk, cos, sin,)
    outs = [jax.ShapeDtypeStruct((8, 4, 320, HD), BF)]
    return pl.pallas_call(
        send_kernel,
        out_shape=outs[0],
        in_specs=[SSPEC] + [VSPEC] * 8,
        out_specs=VSPEC,
        compiler_params=params((*args, *outs), 0),
        cost_estimate=COST,
    )(*args)


def tile_mask(kt, starts, spots):
    keys = kt * 512 + lax.broadcasted_iota(jnp.int32, (512, 256), 0)
    return (keys >= starts) & (keys <= spots)


def attend_kernel(scale2, low_ref, mid_ref, r_ref, start_ref, spot_ref, out_ref, acc_ref, lse_ref, vt_ref):
    for b in range(32):
        vt_ref[:, b * 128 : (b + 1) * 128] = r_ref[b, 192:320, :].T

    def tile(i, _):
        q = r_ref[pl.ds(4 * i, 4), 0:64, :].reshape(256, HD)
        starts, spots = start_ref[i], spot_ref[i]

        def step(masked, kts, carry):
            top, total, acc = carry
            tiles = []
            for kt in kts:
                k = r_ref[pl.ds(4 * kt, 4), 64:192, :].reshape(512, HD)
                s = lax.dot_general(k, q, (((1,), (1,)), ((), ())), preferred_element_type=F32)
                s = s * scale2
                tiles.append(jnp.where(tile_mask(kt, starts, spots), s, -1e30) if masked else s)
            new_top = top
            for s in tiles:
                new_top = jnp.maximum(new_top, jnp.max(s, axis=0, keepdims=True))
            fade = jnp.exp2(top - new_top)
            total, acc = total * fade, acc * fade
            for kt, s in zip(kts, tiles):
                p = jnp.exp2(s - new_top)
                if masked:
                    p = jnp.where(s > -1e29, p, 0.0)
                total += jnp.sum(p, axis=0, keepdims=True)
                vt = vt_ref[:, pl.ds(pl.multiple_of(kt * 512, 512), 512)]
                acc += jnp.dot(vt, p.astype(BF), preferred_element_type=F32)
            return new_top, total, acc

        carry = (
            jnp.full((1, 256), -1e30, F32),
            jnp.zeros((1, 256), F32),
            jnp.zeros((HD, 256), F32),
        )
        first = mid_ref[i]
        pairs = (i - first) // 2
        carry = lax.fori_loop(low_ref[i], first, lambda kt, c: step(True, (kt,), c), carry)
        carry = lax.fori_loop(
            0, pairs, lambda n, c: step(False, (first + 2 * n, first + 2 * n + 1), c), carry
        )
        carry = lax.fori_loop(first + 2 * pairs, i, lambda kt, c: step(False, (kt,), c), carry)
        top, total, acc = step(True, (i,), carry)
        acc = acc / total
        acc_ref[i] = acc
        lse_ref[i] = top + jnp.log2(total)
        out_ref[pl.ds(4 * i, 4)] = acc.T.astype(BF).reshape(4, 64, HD)
        return 0

    lax.fori_loop(0, 8, tile, 0)


def attend(received, low, mid, starts, spots):
    args = (low, mid, received, starts, spots,)
    outs = [
            jax.ShapeDtypeStruct((32, 64, HD), BF),
            jax.ShapeDtypeStruct((8, HD, 256), F32),
            jax.ShapeDtypeStruct((8, 1, 256), F32),
        ]
    return pl.pallas_call(
        functools.partial(attend_kernel, LOG2E / math.sqrt(HD)),
        out_shape=outs,
        in_specs=[SSPEC] * 2 + [VSPEC] * 3,
        out_specs=[VSPEC] * 3,
        scratch_shapes=[pltpu.VMEM((HD, 4096), BF)],
        compiler_params=params((*args, *outs), 1 << 20),
        cost_estimate=COST,
    )(*args)


def attend_grad_kernel(
    scale2, scale, low_ref, mid_ref, r_ref, do_ref, acc_ref, lse_ref, start_ref, spot_ref, out_ref, kt_ref, dk_ref, dv_ref
):
    for b in range(32):
        kt_ref[:, b * 128 : (b + 1) * 128] = r_ref[b, 64:192, :].T
    dk_ref[...] = jnp.zeros_like(dk_ref)
    dv_ref[...] = jnp.zeros_like(dv_ref)

    def tile(i, _):
        q = r_ref[pl.ds(4 * i, 4), 0:64, :].reshape(256, HD)
        do = do_ref[pl.ds(4 * i, 4)].reshape(256, HD)
        delta = jnp.sum(do.astype(F32).T * acc_ref[i], axis=0, keepdims=True)
        lse, starts, spots = lse_ref[i], start_ref[i], spot_ref[i]

        def step(masked, kts, dq):
            for kt in kts:
                k = r_ref[pl.ds(4 * kt, 4), 64:192, :].reshape(512, HD)
                v = r_ref[pl.ds(4 * kt, 4), 192:320, :].reshape(512, HD)
                s = lax.dot_general(k, q, (((1,), (1,)), ((), ())), preferred_element_type=F32)
                e = s * scale2 - lse
                if masked:
                    e = jnp.where(tile_mask(kt, starts, spots), e, -1e30)
                p = jnp.exp2(e)
                dp = lax.dot_general(v, do, (((1,), (1,)), ((), ())), preferred_element_type=F32)
                ds = (p * (dp - delta)).astype(BF)
                keys = pl.ds(pl.multiple_of(kt * 512, 512), 512)
                dv_ref[keys, :] += jnp.dot(p.astype(BF), do, preferred_element_type=F32)
                dk_ref[keys, :] += jnp.dot(ds, q, preferred_element_type=F32)
                dq += jnp.dot(kt_ref[:, keys], ds, preferred_element_type=F32)
            return dq

        dq = jnp.zeros((HD, 256), F32)
        first = mid_ref[i]
        pairs = (i - first) // 2
        dq = lax.fori_loop(low_ref[i], first, lambda kt, c: step(True, (kt,), c), dq)
        dq = lax.fori_loop(
            0, pairs, lambda n, c: step(False, (first + 2 * n, first + 2 * n + 1), c), dq
        )
        dq = lax.fori_loop(first + 2 * pairs, i, lambda kt, c: step(False, (kt,), c), dq)
        dq = step(True, (i,), dq)
        out_ref[pl.ds(4 * i, 4), 0:64, :] = (dq * scale).T.astype(BF).reshape(4, 64, HD)
        return 0

    lax.fori_loop(0, 8, tile, 0)
    for b in range(32):
        out_ref[b, 64:192, :] = (dk_ref[b * 128 : (b + 1) * 128, :] * scale).astype(BF)
        out_ref[b, 192:320, :] = dv_ref[b * 128 : (b + 1) * 128, :].astype(BF)


def attend_grad(received, d_attn, acc, lse, low, mid, starts, spots):
    args = (low, mid, received, d_attn, acc, lse, starts, spots,)
    outs = [jax.ShapeDtypeStruct((32, 320, HD), BF)]
    return pl.pallas_call(
        functools.partial(attend_grad_kernel, LOG2E / math.sqrt(HD), 1.0 / math.sqrt(HD)),
        out_shape=outs[0],
        in_specs=[SSPEC] * 2 + [VSPEC] * 6,
        out_specs=VSPEC,
        scratch_shapes=[
            pltpu.VMEM((HD, 4096), BF),
            pltpu.VMEM((4096, HD), F32),
            pltpu.VMEM((4096, HD), F32),
        ],
        compiler_params=params((*args, *outs), 5 << 20),
        cost_estimate=COST,
    )(*args)


def unpack_kernel(
    spot_ref, d_ref, q_ref, k_ref, scale_ref, gq_ref, gk_ref, cos_ref, sin_ref, tq_ref, tk_ref, dv_ref, dot_ref, dgq_ref, dgk_ref
):
    for n in range(8):
        r, spot = n // 4, spot_ref[n % 4]
        rows = pl.ds(128 * n, 128)
        cos, sin = cos_ref[rows, :], sin_ref[rows, :]
        rq, rk = column(scale_ref[n : n + 1, :]), column(scale_ref[8 + n : 9 + n, :])
        dot_q = jnp.zeros((128, HD), F32)
        for g in range(2):
            cols = pl.ds(g * HD, HD)
            d = jnp.concatenate(
                [d_ref[r * 4 + j, spot, g * 32 : (g + 1) * 32, :] for j in range(4)], axis=0
            ).astype(F32)
            d = rope_backward(d, cos, sin)
            q = q_ref[rows, cols]
            t = d * gq_ref[:, cols]
            tq_ref[rows, cols] = t
            dot_q += t * q
            part = jnp.sum(d * q * rq, axis=0, keepdims=True)
            dgq_ref[:, cols] = part if n == 0 else dgq_ref[:, cols] + part
        dk = d_ref[r * 4, spot, 64:192, :].astype(F32)
        dv = d_ref[r * 4, spot, 192:320, :].astype(F32)
        for j in range(1, 4):
            dk += d_ref[r * 4 + j, spot, 64:192, :].astype(F32)
            dv += d_ref[r * 4 + j, spot, 192:320, :].astype(F32)
        dv_ref[rows, :] = dv.astype(BF)
        d = rope_backward(dk, cos, sin)
        k = k_ref[rows, :]
        t = d * gk_ref[...]
        tk_ref[rows, :] = t
        part = jnp.sum(d * k * rk, axis=0, keepdims=True)
        dgk_ref[...] = part if n == 0 else dgk_ref[...] + part
        dot_ref[n : n + 1, :] = lane_sums(dot_q)
        dot_ref[8 + n : 9 + n, :] = lane_sums(t * k)


def unpack_grads(spots, d, q_pre, k_pre, scales, gq, gk, cos, sin):
    args = (spots, d, q_pre, k_pre, scales, gq, gk, cos, sin,)
    outs = [
            jax.ShapeDtypeStruct((1024, 256), F32),
            jax.ShapeDtypeStruct((1024, 128), F32),
            jax.ShapeDtypeStruct((1024, 128), BF),
            jax.ShapeDtypeStruct((16, 128), F32),
            jax.ShapeDtypeStruct((1, 256), F32),
            jax.ShapeDtypeStruct((1, 128), F32),
        ]
    return pl.pallas_call(
        unpack_kernel,
        out_shape=outs,
        in_specs=[SSPEC] + [VSPEC] * 8,
        out_specs=[VSPEC] * 6,
        compiler_params=params((*args, *outs), 0),
        cost_estimate=COST,
    )(*args)


def spread(row, each, first, group, rows_of):
    count = row.shape[1]
    i = lax.broadcasted_iota(jnp.int32, (128, count), 0)
    c = lax.broadcasted_iota(jnp.int32, (128, count), 1)
    here = c // each == i - group * rows_of
    left = jnp.where(here, jnp.broadcast_to(row, (128, count)), 0.0)
    c = lax.broadcasted_iota(jnp.int32, (count, 128), 0)
    lane = lax.broadcasted_iota(jnp.int32, (count, 128), 1)
    right = (lane == first + c % each).astype(F32)
    return jnp.dot(left, right, precision=HIGHEST, preferred_element_type=F32)


def qkv_grad_kernel(
    head_ref, tq_ref, tk_ref, dv_ref, q_ref, k_ref, scale_ref, dot_ref, dgq_ref, dgk_ref, dga_ref, dgm_ref, *refs
):
    xs, (d_ref, out_ref) = refs[:5], refs[5:]
    for n in range(8):
        rows = pl.ds(128 * n, 128)
        rq, rk = column(scale_ref[n : n + 1, :]), column(scale_ref[8 + n : 9 + n, :])
        eq = rq * rq * rq * column(dot_ref[n : n + 1, :]) * (1.0 / 2048)
        ek = rk * rk * rk * column(dot_ref[8 + n : 9 + n, :]) * (1.0 / 1024)
        for g in range(2):
            cols = pl.ds(g * HD, HD)
            d_ref[rows, cols] = (rq * tq_ref[rows, cols] - eq * q_ref[rows, cols]).astype(BF)
        d_ref[rows, 256:384] = (rk * tk_ref[rows, :] - ek * k_ref[rows, :]).astype(BF)
        d_ref[rows, 384:512] = dv_ref[rows, :]
    for n in range(4):
        rows = pl.ds(256 * n, 256)
        x = jnp.concatenate([x_ref[:, rows] for x_ref in xs], axis=0)
        out_ref[rows, 0:512] = dot_tn(x, d_ref[...]).astype(BF)
    head = head_ref[0]
    gains = spread(dgq_ref[...], 16, 0, head, 16) + spread(dgk_ref[...], 8, 16, head, 16)
    gains += spread(dga_ref[...], 8, 24, 0, 0) + spread(dgm_ref[...], 8, 32, 0, 0)
    coarse = gains.astype(BF).astype(F32)
    both = coarse + pltpu.roll(gains - coarse, 64, 1)
    r = lax.broadcasted_iota(jnp.int32, (1024, 128), 0)
    i = lax.broadcasted_iota(jnp.int32, (1024, 128), 1)
    out_ref[:, 512:640] = dot_nn((r == 8 * i).astype(BF), both.astype(BF)).astype(BF)


def qkv_grads(head, tq, tk, dv16, q_pre, k_pre, scales, dots, gain_grads, x):
    args = (head, tq, tk, dv16, q_pre, k_pre, scales, dots, *gain_grads, *x)
    outs = [
        jax.ShapeDtypeStruct((1024, 512), BF),
        jax.ShapeDtypeStruct((1024, 640), BF),
    ]
    return pl.pallas_call(
        qkv_grad_kernel,
        out_shape=outs,
        in_specs=[SSPEC] + [VSPEC] * 16,
        out_specs=[VSPEC] * 2,
        compiler_params=params((*args, *outs), 4 << 20),
        cost_estimate=COST,
    )(*args)


def dot_nn(a, b):
    return lax.dot_general(a, b, (((1,), (0,)), ((), ())), preferred_element_type=F32)


def dot_nt(a, b):
    return lax.dot_general(a, b, (((1,), (1,)), ((), ())), preferred_element_type=F32)


def dot_tn(a, b):
    return lax.dot_general(a, b, (((0,), (0,)), ((), ())), preferred_element_type=F32)


def rms_rate(v):
    return lax.rsqrt(jnp.mean(v * v, axis=-1, keepdims=True) + EPSILON)


def rms_back(v, g, d):
    r = rms_rate(v)
    t = d * g
    dv = r * t - v * (r * r * r * jnp.mean(t * v, axis=-1, keepdims=True))
    return dv, d * v * r


def call(kernel, out_shape, args, us):
    args = (*args,)
    outs = [jax.ShapeDtypeStruct(s, t) for s, t in out_shape]
    return pl.pallas_call(
        kernel,
        out_shape=outs,
        in_specs=[SSPEC if a.ndim == 1 else VSPEC for a in args],
        out_specs=[VSPEC] * len(out_shape),
        compiler_params=params((*args, *outs), 0),
        cost_estimate=COST,
    )(*args)


def both_cores(part_ref, got_ref):
    got = jnp.concatenate([got_ref[128:256, :], got_ref[0:128, :]], axis=0)
    return part_ref[...].astype(F32) + got.astype(F32)


def proj_kernel(spot_ref, a_ref, *refs):
    chunks, (attn_ref, part_ref) = refs[:4], refs[4:]
    for r in range(2):
        for j in range(4):
            rows = pl.ds(r * 128 + j * 32, 32)
            for h in range(4):
                for g in range(2):
                    piece = a_ref[(r * 4 + j) * 4 + h, g * 32 : (g + 1) * 32, :]
                    attn_ref[rows, (h * 2 + g) * HD : (h * 2 + g + 1) * HD] = piece
    lefts = [
        attn_ref[:, pl.ds(pl.multiple_of(spot_ref[n] * 256, 256), 256)] for n in range(4)
    ]
    for m in range(4):
        cols = pl.ds(256 * m, 256)
        part = dot_nt(lefts[0], chunks[0][cols, 0:256])
        for n in range(1, 4):
            part += dot_nt(lefts[n], chunks[n][cols, 0:256])
        part_ref[:, cols] = part.astype(BF)


def hidden_columns(n):
    return 256 if n < 4 else 0


def forward_kernel(part_ref, got_ref, xo_ref, xt_ref, g_ref, *refs):
    chunks, (mid_ref, gate_ref, up_ref, act_ref, down_ref) = refs[:12], refs[12:]
    proj = both_cores(part_ref, got_ref)
    x = jnp.concatenate([xo_ref[...], xt_ref[...]], axis=0).astype(F32)
    m = (x + proj * rms_rate(proj) * g_ref[...]).astype(BF)
    mid_ref[...] = m
    for n, w_ref in enumerate(chunks):
        at = hidden_columns(n)
        both = dot_nn(m, w_ref[:, at : at + 256])
        gate, up = both[:, :128], both[:, 128:]
        gate_ref[n] = gate.astype(BF)
        up_ref[n] = up.astype(BF)
        act_ref[n] = (gate / (1.0 + jnp.exp(-gate)) * up).astype(BF)
    for k in range(4):
        cols = pl.ds(256 * k, 256)
        part = jnp.zeros((256, 256), F32)
        for n, w_ref in enumerate(chunks):
            at = hidden_columns(n) + 256
            part += dot_nt(act_ref[n], w_ref[cols, at : at + 128])
        down_ref[:, cols] = part.astype(BF)


def backward_kernel(
    down_ref, downg_ref, part_ref, got_ref, xo_ref, co_ref, ct_ref, ga_ref, gm_ref, gate_ref, up_ref, *refs
):
    chunks, (out_ref, dd_ref, dboth_ref, dmid_ref, dg_ref) = refs[:12], refs[12:]
    down = both_cores(down_ref, downg_ref)
    gm = gm_ref[...]
    proj = both_cores(part_ref, got_ref)[:128]
    middle = xo_ref[...].astype(F32) + proj * rms_rate(proj) * ga_ref[...]
    out_ref[...] = middle + down[:128] * rms_rate(down[:128]) * gm
    c = jnp.concatenate([co_ref[...], ct_ref[...]], axis=0).astype(F32)
    dd, terms = rms_back(down, gm, c)
    dg_ref[...] = jnp.sum(terms[:128], axis=0, keepdims=True)
    dd = dd.astype(BF)
    dd_ref[...] = dd
    for n, w_ref in enumerate(chunks):
        at = hidden_columns(n)
        d_act = dot_nn(dd, w_ref[:, at + 256 : at + 384])
        gate, up = gate_ref[n].astype(F32), up_ref[n].astype(F32)
        sig = 1.0 / (1.0 + jnp.exp(-gate))
        dboth_ref[n, :, 0:128] = (d_act * up * sig * (1.0 + gate * (1.0 - sig))).astype(BF)
        dboth_ref[n, :, 128:256] = (d_act * gate * sig).astype(BF)
    for k in range(4):
        cols = pl.ds(256 * k, 256)
        part = jnp.zeros((256, 256), F32)
        for n, w_ref in enumerate(chunks):
            at = hidden_columns(n)
            part += dot_nt(dboth_ref[n], w_ref[cols, at : at + 256])
        dmid_ref[:, cols] = part.astype(BF)


def d_attn_kernel(spot_ref, dmid_ref, dmidg_ref, part_ref, got_ref, co_ref, ct_ref, ga_ref, *refs):
    chunks, (dm_ref, dp_ref, out_ref, dg_ref) = refs[:4], refs[4:]
    c = jnp.concatenate([co_ref[...], ct_ref[...]], axis=0).astype(F32)
    d_middle = c + both_cores(dmid_ref, dmidg_ref)
    dm_ref[...] = d_middle[:128]
    dp, terms = rms_back(both_cores(part_ref, got_ref), ga_ref[...], d_middle)
    dg_ref[...] = jnp.sum(terms[:128], axis=0, keepdims=True)
    dp = dp.astype(BF)
    dp_ref[...] = dp
    for n in range(4):
        part = dot_nn(dp, chunks[n][:, 0:256]).astype(BF)
        for r in range(2):
            for j in range(4):
                for g in range(2):
                    piece = part[r * 128 + j * 32 : r * 128 + (j + 1) * 32, g * HD : (g + 1) * HD]
                    out_ref[(r * 4 + j) * 4 + spot_ref[n], g * 32 : (g + 1) * 32, :] = piece


def hidden_grads_kernel(first, m_ref, dd_ref, dboth_ref, act_ref, *outs):
    for n, out_ref in enumerate(outs):
        at = hidden_columns(first + n)
        out_ref[:, at : at + 256] = dot_tn(m_ref[...], dboth_ref[first + n]).astype(BF)
        out_ref[:, at + 256 : at + 384] = dot_tn(dd_ref[...], act_ref[first + n]).astype(BF)


def out_grads_kernel(spot_ref, m_ref, dd_ref, dboth_ref, act_ref, dp_ref, attn_ref, *outs):
    hidden_grads_kernel(0, m_ref, dd_ref, dboth_ref, act_ref, *outs)
    for n, out_ref in enumerate(outs):
        right = attn_ref[:, pl.ds(pl.multiple_of(spot_ref[n] * 256, 256), 256)]
        out_ref[:, 0:256] = dot_tn(dp_ref[...], right).astype(BF)


def row_places(row_lengths, spots):
    ends = jnp.cumsum(row_lengths)
    passed = spots[:, None] >= ends[None, :]
    return jnp.sum(jnp.where(passed, row_lengths[None, :], 0), axis=1)


def after(value, *others):
    return lax.optimization_barrier((value,) + others)[0]


def group_sum(rows):
    a = rows.reshape(2, 2, 4, 128)
    total = a
    for by in (1, -1, 2):
        got = shift(rows, "z", by, False).reshape(2, 2, 4, 128)
        pick = [NEAR.index((NEAR[k] + by) % 4) for k in range(4)]
        total = total + jnp.stack([got[:, :, p] for p in pick], axis=2)
    return (total + swap(total)[:, ::-1]).reshape(16, 128)


def body(
    block_input,
    out_grad,
    lengths,
    w_query,
    w_key,
    w_value,
    w_out,
    w_gate,
    w_up,
    w_down,
    gain_query,
    gain_key,
    gain_attn,
    gain_mlp,
):
    core = lax.axis_index("c")
    z = lax.axis_index("z")
    peer = lax.axis_index("y") * 2 + lax.axis_index("xl")
    head = core * 4 + z
    my_x = block_input[0]

    columns = jnp.concatenate(
        [w_query.reshape(8, 8, 256), w_key.reshape(8, 8, 128), w_value.reshape(8, 8, 128)], axis=2
    )
    columns = columns.transpose(1, 0, 2).reshape(1, 2, 1, 1, 4, 8, 512)
    gains = jnp.concatenate([gain_query, gain_key, gain_attn, gain_mlp])
    gains = jnp.pad(gains[None, :], ((0, 7), (0, 88)))
    columns = jnp.concatenate(
        [columns, jnp.broadcast_to(gains, (1, 2, 1, 1, 4, 8, 128))], axis=-1
    )
    columns = jnp.broadcast_to(columns, (2, 2, 4, 2, 4, 8, 640)).reshape(128, 8, 640)
    columns = lax.all_to_all(columns, AXES, split_axis=0, concat_axis=0, tiled=False)
    gains = columns[:, 0, 512:552].astype(F32)
    w_head = columns.reshape(1024, 640)
    my_gains = lax.dynamic_slice_in_dim(gains, head * 16, 16, 0)
    gq, gk = my_gains[:, 0:16].reshape(1, 256), my_gains[:, 16:24].reshape(1, 128)

    ga, gm = gains[:, 24:32].reshape(1, 1024), gains[:, 32:40].reshape(1, 1024)

    def everywhere(a, shape):
        a = a.reshape(shape + (8, a.shape[-1]))
        return jnp.broadcast_to(a, (2, 2, 4, 2, 4, 8, a.shape[-1]))

    hidden = [w.reshape(8, 2, 3, 4, 128) for w in (w_gate, w_up, w_down.T)]
    hidden = jnp.concatenate(hidden, axis=-1).transpose(2, 1, 3, 0, 4)
    first = w_out.T.reshape(8, 2, 4, 256).transpose(1, 2, 0, 3)
    first = jnp.concatenate([first, hidden[0]], axis=-1)
    over_x = hidden[1].reshape(2, 2, 2, 8, 384).transpose(1, 0, 2, 3, 4)
    weights = jnp.concatenate(
        [
            everywhere(first, (1, 2, 1, 1, 4)),
            everywhere(over_x, (2, 2, 1, 2, 1)),
            everywhere(hidden[2], (1, 2, 4, 1, 1)),
        ],
        axis=-1,
    ).reshape(128, 8, 1408)
    weights = after(weights, w_head)
    weights = lax.all_to_all(weights, AXES, split_axis=0, concat_axis=0, tiled=False)
    weights = weights.reshape(1024, 1408)

    x_group = [my_x] + [shift(my_x, "z", by, False) for by in (1, -1, 2)]
    x_group = x_group + [swap(jnp.concatenate(x_group, axis=0))]
    x_own, x_other = my_x, x_group[4][:128]
    c_own = out_grad[0]
    c_other = swap(c_own)
    spots = jnp.stack([(z + n) % 4 for n in NEAR])

    q_pre, k_pre, v16, ss = project_qkv(x_group, w_head)
    lengths = after(lengths, ss)

    my_lengths = lengths[0]
    other_lengths = swap(my_lengths)
    here = (peer * 4 + spots[:, None]) * 128 + jnp.arange(128, dtype=jnp.int32)[None, :]
    here = here.reshape(512)
    offset = jnp.concatenate(
        [here - row_places(my_lengths, here), here - row_places(other_lengths, here)]
    )
    frequency = THETA ** (-(jnp.arange(64, dtype=F32) * 2.0 / HD))
    angles = offset.astype(F32)[:, None] * frequency[None, :]
    cosine, sine = jnp.cos(angles), jnp.sin(angles)
    cos2 = jnp.concatenate([cosine, cosine], axis=1)
    sin2 = jnp.concatenate([-sine, sine], axis=1)

    task_lengths = jnp.where(peer // 4 == 0, my_lengths, other_lengths)
    task_spots = (
        jnp.arange(32, dtype=jnp.int32)[:, None, None] * 128
        + (peer % 4) * 32
        + jnp.arange(32, dtype=jnp.int32)[None, None, :]
    )
    task_spots = jnp.broadcast_to(task_spots, (32, 2, 32)).reshape(2048)
    starts = row_places(task_lengths, task_spots).reshape(8, 1, 256)
    task_spots = task_spots.reshape(8, 1, 256)
    tiles = jnp.arange(8, dtype=jnp.int32)
    low = jnp.minimum(jnp.min(starts, axis=(1, 2)) // 512, tiles)
    mid = jnp.clip((jnp.max(starts, axis=(1, 2)) + 511) // 512, low, tiles)

    width = jnp.concatenate([jnp.full((8, 1), 2048.0), jnp.full((8, 1), 1024.0)])
    scales = lax.rsqrt(group_sum(ss) / width + EPSILON)
    packed = pack_qkv(spots, q_pre, k_pre, v16, scales, gq, gk, cos2, sin2)
    z_spots = jnp.stack(ring_spots("z")).astype(jnp.int32)
    pinned = (packed, weights, low, mid, starts, task_spots, ga, gm, z_spots, x_other, c_other)
    pinned = lax.optimization_barrier(pinned)
    packed, weights, low, mid, starts, task_spots, ga, gm, z_spots, x_other, c_other = pinned
    received = lax.all_to_all(packed, ("y", "xl"), split_axis=0, concat_axis=0, tiled=False)
    chunks = [[w] for w in jnp.split(weights, [640, 1024], axis=1)]

    def step(value, rings):
        value, *latest = lax.optimization_barrier((value, *[group[-1] for group in chunks]))
        for ring, group, last in zip(RINGS, chunks, latest):
            group[-1] = last
            if ring in rings:
                group.append(onward(last, ring))
        return value

    chunks[0].append(onward(chunks[0][0], "z"))
    received = step(received.reshape(32, 320, HD), RINGS)
    attn, acc, lse = attend(received, low, mid, starts, task_spots)
    attn = step(attn, RINGS)
    attn = lax.all_to_all(attn, SEQ, split_axis=0, concat_axis=0, tiled=False)
    attn = step(attn, ("x", "y"))
    chunks = [w for group in chunks for w in group]

    flat, half, vec = (256, 1024), (128, 1024), (1, 1024)
    wide, pairs = (12, 256, 128), (12, 256, 256)
    attn16, part = call(
        proj_kernel, [(flat, BF), (flat, BF)], (z_spots, attn, *chunks[:4]), 4
    )
    parts = (part, swap(part))
    mid16, gate, up, act16, down = call(
        forward_kernel,
        [(flat, BF), (wide, BF), (wide, BF), (wide, BF), (flat, BF)],
        (*parts, x_own, x_other, ga, *chunks),
        6,
    )
    output, dd16, d_both, d_mid, dg_mlp = call(
        backward_kernel,
        [(half, F32), (flat, BF), (pairs, BF), (flat, BF), (vec, F32)],
        (down, swap(down), *parts, x_own, c_own, c_other, ga, gm, gate, up, *chunks),
        7,
    )
    d_middle, dp16, d_attn, dg_attn = call(
        d_attn_kernel,
        [(half, F32), (flat, BF), ((32, 64, HD), BF), (vec, F32)],
        (z_spots, d_mid, swap(d_mid), *parts, c_own, c_other, ga, *chunks[:4]),
        3,
    )

    d_attn, d_both = lax.optimization_barrier((d_attn, d_both))
    d_attn = lax.all_to_all(d_attn, SEQ, split_axis=0, concat_axis=0, tiled=False)
    sources = (mid16, dd16, d_both, act16)
    later = call(
        functools.partial(hidden_grads_kernel, 4), [((1024, 384), BF)] * 8, sources, 4
    )
    first = call(
        out_grads_kernel,
        [((1024, 640), BF)] * 4,
        (z_spots, *sources, dp16, attn16),
        4,
    )
    grads = (first, later[:4], later[4:])
    runs = [onward(g[1], ring) for g, ring in zip(grads, RINGS)]
    d_attn, *runs = lax.optimization_barrier((d_attn, *runs))
    runs = [plus(g[2], run) for g, run in zip(grads, runs)]
    d_attn, *runs = lax.optimization_barrier((d_attn, *runs))
    runs = [onward(run, ring) for run, ring in zip(runs, RINGS)]

    d_pairs = attend_grad(received, d_attn, acc, lse, low, mid, starts, task_spots)
    d_pairs, *runs = lax.optimization_barrier((d_pairs, *runs))
    runs = [plus(g[3], run) for g, run in zip(grads, runs)]
    runs = [onward(run, ring) for run, ring in zip(runs, RINGS)]
    d_pairs = d_pairs.reshape(8, 4, 320, HD)
    d_pairs = lax.all_to_all(d_pairs, ("y", "xl"), split_axis=0, concat_axis=0, tiled=False)
    runs = jnp.concatenate([plus(g[0], run) for g, run in zip(grads, runs)], axis=1)
    d_pairs, runs = lax.optimization_barrier((d_pairs, runs))
    sums = lax.all_to_all(
        runs.reshape(128, 8, 1408), AXES, split_axis=0, concat_axis=0, tiled=False
    )
    tq, tk, dv16, dots, dgq, dgk = unpack_grads(
        spots, d_pairs, q_pre, k_pre, scales, gq, gk, cos2, sin2
    )
    dots = group_sum(dots)

    d_pre, grad_head = qkv_grads(
        head[None], tq, tk, dv16, q_pre, k_pre, scales, dots, (dgq, dgk, dg_attn, dg_mlp), x_group
    )
    grad_head, sums = lax.optimization_barrier((grad_head, sums))
    grad_head = lax.all_to_all(
        grad_head.reshape(128, 8, 640), AXES, split_axis=0, concat_axis=0, tiled=False
    )
    d_x = dot_nt(d_pre, w_head[:, :512]).astype(BF)
    d_x = (d_x[:512].astype(F32) + swap(d_x[512:]).astype(F32)).astype(BF)
    d_middle = d_middle + d_x[:128].astype(F32)
    for n, by in enumerate((-1, 1, 2)):
        piece = shift(d_x[128 * (n + 1) : 128 * (n + 2)], "z", by, False)
        d_middle = d_middle + after(piece, grad_head).astype(F32)

    heads = grad_head.reshape(2, 2, 4, 2, 4, 8, 640).astype(F32).sum(axis=(0, 2, 3))
    dgains = heads[:, :, 0, 512:640].sum(axis=(0, 1))
    dgains = dgains[0:40] + dgains[64:104]
    heads = heads.reshape(8, 8, 640).transpose(1, 0, 2)

    sums = sums.reshape(2, 2, 4, 2, 4, 8, 1408).astype(F32)
    sum_z = sums[..., :640].sum(axis=(0, 2, 3))
    sum_x = sums[..., 640:1024].sum(axis=(2, 4)).transpose(1, 0, 2, 3, 4).reshape(2, 4, 8, 384)
    sum_y = sums[..., 1024:].sum(axis=(0, 3, 4))
    hidden = jnp.stack([sum_z[..., 256:], sum_x, sum_y], axis=1).transpose(3, 0, 1, 2, 4)
    hidden = [hidden[..., 128 * n : 128 * (n + 1)].reshape(8, 3072) for n in range(3)]
    return (
        output[None],
        d_middle[None],
        heads[:, :, 0:256].reshape(8, 2048),
        heads[:, :, 256:384].reshape(8, 1024),
        heads[:, :, 384:512].reshape(8, 1024),
        sum_z[..., :256].transpose(2, 0, 1, 3).reshape(8, 2048).T,
        hidden[0],
        hidden[1],
        hidden[2].T,
        dgains[0:16],
        dgains[16:24],
        dgains[24:32],
        dgains[32:40],
    )


def solution(mesh):
    cube_mesh = Mesh(mesh.devices.reshape(2, 2, 4, 2, 4), AXES)
    row, seq = ("xh", "c"), SEQ
    everything = row + seq
    tokens, rows, cols, vec = (
        P(row, seq, None),
        P(everything, None),
        P(None, everything),
        P(everything),
    )
    in_specs = (tokens, tokens, P(row, None), rows, rows, rows, cols, rows, rows, cols) + (vec,) * 4
    out_specs = (tokens, tokens, rows, rows, rows, cols, rows, rows, cols) + (vec,) * 4
    return jax.shard_map(body, mesh=cube_mesh, in_specs=in_specs, out_specs=out_specs, check_vma=False)
```

```python
import functools
import math

import jax
import jax.numpy as jnp
from jax import lax
from jax.experimental import pallas as pl
from jax.experimental.pallas import tpu as pltpu
from jax.sharding import Mesh, PartitionSpec as P

BF = jnp.bfloat16
F32 = jnp.float32
HD = 128
EPSILON = 1e-06
THETA = 500000.0
AXES = ("xh", "c", "y", "xl", "z")
SEQ = ("y", "xl", "z")
LOG2E = 1.4426950408889634
HIGHEST = lax.Precision.HIGHEST
COST = pl.CostEstimate(flops=1, bytes_accessed=1, transcendentals=0)


def swap(a):
    return lax.ppermute(a, "c", [(0, 1), (1, 0)])


def shift(a, ring, by, mirrored):
    axes = ("xh", "c", "xl") if ring == "x" else ("c", ring)

    def index(c, m):
        return (m // 2) * 4 + c * 2 + m % 2 if ring == "x" else c * 4 + m

    pairs = []
    for c in range(2):
        step = -by if (mirrored and c == 1) else by
        pairs += [(index(c, m), index(c, (m + step) % 4)) for m in range(4)]
    return lax.ppermute(a, axes, pairs)


def position(ring):
    if ring == "x":
        return lax.axis_index("xh") * 2 + lax.axis_index("xl")
    return lax.axis_index(ring)


def params(arrays, scratch=0):
    total = scratch + sum(math.prod(a.shape) * jnp.dtype(a.dtype).itemsize for a in arrays)
    return pltpu.CompilerParams(vmem_limit_bytes=total + total // 8 + (3 << 20))


VSPEC = pl.BlockSpec(memory_space=pltpu.VMEM)
SSPEC = pl.BlockSpec(memory_space=pltpu.SMEM)
ASPEC = pl.BlockSpec(memory_space=pl.ANY)


RINGS = ("z", "x", "y")


def ring_spots(ring):
    here, sign = position(ring), 1 - 2 * lax.axis_index("c")
    return [(here - sign * n) % 4 for n in range(4)]


def onward(block, ring):
    return shift(block, ring, 1, True)


def plus(a, b):
    return (a.astype(F32) + b.astype(F32)).astype(BF)


NEAR = (0, 3, 1, 2)


def rope_forward(v, cos, sin):
    return v * cos + pltpu.roll(v, 64, 1) * sin


def rope_backward(d, cos, sin):
    return d * cos - pltpu.roll(d, 64, 1) * sin


def lane_sums(a):
    ones = jnp.ones((8, a.shape[1]), F32)
    rows = lax.dot_general(
        ones, a, (((1,), (1,)), ((), ())), precision=HIGHEST, preferred_element_type=F32
    )
    return rows[0:1]


def store_sums(own_ref, other_ref, n, q_sum, k_sum):
    own_ref[n : n + 1, :] = q_sum
    own_ref[8 + n : 9 + n, :] = k_sum
    m = (n + 4) % 8
    other_ref[m : m + 1, :] = q_sum
    other_ref[8 + m : 9 + m, :] = k_sum


def column(row):
    return jnp.broadcast_to(row, (128, 128)).T


def group_rows(part, for_other):
    total = part + swap(for_other)
    return [total] + [shift(total, "z", by, False) for by in (1, -1, 2)]


def group_total(refs, n):
    first, k = n // 4 * 4, n % 4
    total = refs[0][n : n + 1, :]
    for ref, by in zip(refs[1:], (1, -1, 2)):
        at = first + NEAR.index((NEAR[k] + by) % 4)
        total += ref[at : at + 1, :]
    return total


def qkv_kernel(w_ref, *refs):
    xs, (q_ref, k_ref, v_ref, ss_ref, sso_ref) = refs[:5], refs[5:]
    for n in range(8):
        rows = pl.ds(128 * n, 128)
        x = xs[n][...] if n < 4 else xs[4][128 * (n - 4) : 128 * (n - 3), :]
        pre = jnp.dot(x, w_ref[:, :512], preferred_element_type=F32)
        q, k = pre[:, :256], pre[:, 256:384]
        q_ref[rows, :] = q
        k_ref[rows, :] = k
        v_ref[rows, :] = pre[:, 384:].astype(BF)
        store_sums(ss_ref, sso_ref, n, lane_sums(q * q), lane_sums(k * k))


def project_qkv(x, w):
    args = (w, *x)
    outs = [
            jax.ShapeDtypeStruct((1024, 256), F32),
            jax.ShapeDtypeStruct((1024, 128), F32),
            jax.ShapeDtypeStruct((1024, 128), BF),
            jax.ShapeDtypeStruct((16, 128), F32),
        jax.ShapeDtypeStruct((16, 128), F32),
        ]
    return pl.pallas_call(
        qkv_kernel,
        out_shape=outs,
        in_specs=[VSPEC] * 6,
        out_specs=[VSPEC] * 5,
        compiler_params=params((*args, *outs), 0),
        cost_estimate=COST,
    )(*args)


def send_kernel(
    spot_ref, q_ref, k_ref, v_ref, gq_ref, gk_ref, cos_ref, sin_ref, s0_ref, s1_ref, s2_ref, s3_ref, out_ref, scale_ref
):
    sums = (s0_ref, s1_ref, s2_ref, s3_ref)
    for n in range(16):
        width = 2048 if n < 8 else 1024
        mean = group_total(sums, n) * (1.0 / width)
        scale_ref[n : n + 1, :] = lax.rsqrt(mean + EPSILON)
    for n in range(8):
        r, spot = n // 4, spot_ref[n % 4]
        rows = pl.ds(128 * n, 128)
        cos, sin = cos_ref[rows, :], sin_ref[rows, :]
        rq, rk = column(scale_ref[n : n + 1, :]), column(scale_ref[8 + n : 9 + n, :])
        for g in range(2):
            cols = pl.ds(g * HD, HD)
            q = rope_forward(q_ref[rows, cols] * rq * gq_ref[:, cols], cos, sin).astype(BF)
            for j in range(4):
                out_ref[r * 4 + j, spot, g * 32 : (g + 1) * 32, :] = q[32 * j : 32 * j + 32]
        k = rope_forward(k_ref[rows, :] * rk * gk_ref[...], cos, sin).astype(BF)
        v = v_ref[rows, :]
        for j in range(4):
            out_ref[r * 4 + j, spot, 64:192, :] = k
            out_ref[r * 4 + j, spot, 192:320, :] = v


def pack_qkv(spots, q_pre, k_pre, v16, gq, gk, cos, sin, sums):
    args = (spots, q_pre, k_pre, v16, gq, gk, cos, sin, *sums)
    outs = [
        jax.ShapeDtypeStruct((8, 4, 320, HD), BF),
        jax.ShapeDtypeStruct((16, 128), F32),
    ]
    return pl.pallas_call(
        send_kernel,
        out_shape=outs,
        in_specs=[SSPEC] + [VSPEC] * 11,
        out_specs=[VSPEC] * 2,
        compiler_params=params((*args, *outs)),
        cost_estimate=COST,
    )(*args)


def grouped(first, last, step, carry):
    for size in (4, 2, 1):
        count = (last - first) // size

        def body(n, c, size=size, first=first):
            return step([first + size * n + m for m in range(size)], c)

        carry = lax.fori_loop(0, count, body, carry)
        first = first + size * count
    return carry


def tile_mask(kt, starts, spots):
    keys = kt * 512 + lax.broadcasted_iota(jnp.int32, (512, 256), 0)
    return (keys >= starts) & (keys <= spots)


def attend_kernel(scale2, low_ref, mid_ref, r_ref, start_ref, spot_ref, out_ref, acc_ref, lse_ref, vt_ref):
    for b in range(32):
        vt_ref[:, b * 128 : (b + 1) * 128] = r_ref[b, 192:320, :].T

    def tile(i, _):
        q = r_ref[pl.ds(4 * i, 4), 0:64, :].reshape(256, HD)
        starts, spots = start_ref[i], spot_ref[i]

        def step(masked, kts, carry):
            top, total, acc = carry
            tiles = []
            for kt in kts:
                k = r_ref[pl.ds(4 * kt, 4), 64:192, :].reshape(512, HD)
                s = lax.dot_general(k, q, (((1,), (1,)), ((), ())), preferred_element_type=F32)
                s = s * scale2
                tiles.append(jnp.where(tile_mask(kt, starts, spots), s, -1e30) if masked else s)
            new_top = top
            for s in tiles:
                new_top = jnp.maximum(new_top, jnp.max(s, axis=0, keepdims=True))
            fade = jnp.exp2(top - new_top)
            total, acc = total * fade, acc * fade
            for kt, s in zip(kts, tiles):
                p = jnp.exp2(s - new_top)
                if masked:
                    p = jnp.where(s > -1e29, p, 0.0)
                total += jnp.sum(p, axis=0, keepdims=True)
                vt = vt_ref[:, pl.ds(pl.multiple_of(kt * 512, 512), 512)]
                acc += jnp.dot(vt, p.astype(BF), preferred_element_type=F32)
            return new_top, total, acc

        carry = (
            jnp.full((1, 256), -1e30, F32),
            jnp.zeros((1, 256), F32),
            jnp.zeros((HD, 256), F32),
        )
        first = mid_ref[i]
        carry = lax.fori_loop(low_ref[i], first, lambda kt, c: step(True, (kt,), c), carry)
        carry = grouped(first, i, functools.partial(step, False), carry)
        top, total, acc = step(True, (i,), carry)
        acc = acc / total
        acc_ref[i] = acc
        lse_ref[i] = top + jnp.log2(total)
        out_ref[pl.ds(4 * i, 4)] = acc.T.astype(BF).reshape(4, 64, HD)
        return 0

    lax.fori_loop(0, 8, tile, 0)


def attend(received, low, mid, starts, spots):
    args = (low, mid, received, starts, spots,)
    outs = [
            jax.ShapeDtypeStruct((32, 64, HD), BF),
            jax.ShapeDtypeStruct((8, HD, 256), F32),
            jax.ShapeDtypeStruct((8, 1, 256), F32),
        ]
    return pl.pallas_call(
        functools.partial(attend_kernel, LOG2E / math.sqrt(HD)),
        out_shape=outs,
        in_specs=[SSPEC] * 2 + [VSPEC] * 3,
        out_specs=[VSPEC] * 3,
        scratch_shapes=[pltpu.VMEM((HD, 4096), BF)],
        compiler_params=params((*args, *outs), 1 << 20),
        cost_estimate=COST,
    )(*args)


def attend_grad_kernel(
    scale2, scale, low_ref, mid_ref, r_ref, do_ref, acc_ref, lse_ref, start_ref, spot_ref, out_ref, kt_ref, dk_ref, dv_ref
):
    for b in range(32):
        kt_ref[:, b * 128 : (b + 1) * 128] = r_ref[b, 64:192, :].T
    dk_ref[...] = jnp.zeros_like(dk_ref)
    dv_ref[...] = jnp.zeros_like(dv_ref)

    def tile(i, _):
        q = r_ref[pl.ds(4 * i, 4), 0:64, :].reshape(256, HD)
        do = do_ref[pl.ds(4 * i, 4)].reshape(256, HD)
        delta = jnp.sum(do.astype(F32).T * acc_ref[i], axis=0, keepdims=True)
        lse, starts, spots = lse_ref[i], start_ref[i], spot_ref[i]

        def step(masked, kts, dq):
            for kt in kts:
                k = r_ref[pl.ds(4 * kt, 4), 64:192, :].reshape(512, HD)
                v = r_ref[pl.ds(4 * kt, 4), 192:320, :].reshape(512, HD)
                s = lax.dot_general(k, q, (((1,), (1,)), ((), ())), preferred_element_type=F32)
                e = s * scale2 - lse
                if masked:
                    e = jnp.where(tile_mask(kt, starts, spots), e, -1e30)
                p = jnp.exp2(e)
                dp = lax.dot_general(v, do, (((1,), (1,)), ((), ())), preferred_element_type=F32)
                ds = (p * (dp - delta)).astype(BF)
                keys = pl.ds(pl.multiple_of(kt * 512, 512), 512)
                dv_ref[keys, :] += jnp.dot(p.astype(BF), do, preferred_element_type=F32)
                dk_ref[keys, :] += jnp.dot(ds, q, preferred_element_type=F32)
                dq += jnp.dot(kt_ref[:, keys], ds, preferred_element_type=F32)
            return dq

        dq = jnp.zeros((HD, 256), F32)
        first = mid_ref[i]
        dq = lax.fori_loop(low_ref[i], first, lambda kt, c: step(True, (kt,), c), dq)
        dq = grouped(first, i, functools.partial(step, False), dq)
        dq = step(True, (i,), dq)
        out_ref[pl.ds(4 * i, 4), 0:64, :] = (dq * scale).T.astype(BF).reshape(4, 64, HD)
        return 0

    lax.fori_loop(0, 8, tile, 0)
    for b in range(32):
        out_ref[b, 64:192, :] = (dk_ref[b * 128 : (b + 1) * 128, :] * scale).astype(BF)
        out_ref[b, 192:320, :] = dv_ref[b * 128 : (b + 1) * 128, :].astype(BF)


def attend_grad(received, d_attn, acc, lse, low, mid, starts, spots):
    args = (low, mid, received, d_attn, acc, lse, starts, spots,)
    outs = [jax.ShapeDtypeStruct((32, 320, HD), BF)]
    return pl.pallas_call(
        functools.partial(attend_grad_kernel, LOG2E / math.sqrt(HD), 1.0 / math.sqrt(HD)),
        out_shape=outs[0],
        in_specs=[SSPEC] * 2 + [VSPEC] * 6,
        out_specs=VSPEC,
        scratch_shapes=[
            pltpu.VMEM((HD, 4096), BF),
            pltpu.VMEM((4096, HD), F32),
            pltpu.VMEM((4096, HD), F32),
        ],
        compiler_params=params((*args, *outs), 5 << 20),
        cost_estimate=COST,
    )(*args)


def unpack_kernel(
    spot_ref, d_ref, q_ref, k_ref, scale_ref, gq_ref, gk_ref, cos_ref, sin_ref, tq_ref, tk_ref, dv_ref, dot_ref, doto_ref, dgq_ref, dgk_ref
):
    for n in range(8):
        r, spot = n // 4, spot_ref[n % 4]
        rows = pl.ds(128 * n, 128)
        cos, sin = cos_ref[rows, :], sin_ref[rows, :]
        rq, rk = column(scale_ref[n : n + 1, :]), column(scale_ref[8 + n : 9 + n, :])
        dot_q = jnp.zeros((128, HD), F32)
        for g in range(2):
            cols = pl.ds(g * HD, HD)
            d = jnp.concatenate(
                [d_ref[r * 4 + j, spot, g * 32 : (g + 1) * 32, :] for j in range(4)], axis=0
            ).astype(F32)
            d = rope_backward(d, cos, sin)
            q = q_ref[rows, cols]
            t = d * gq_ref[:, cols]
            tq_ref[rows, cols] = t
            dot_q += t * q
            part = jnp.sum(d * q * rq, axis=0, keepdims=True)
            dgq_ref[:, cols] = part if n == 0 else dgq_ref[:, cols] + part
        dk = d_ref[r * 4, spot, 64:192, :].astype(F32)
        dv = d_ref[r * 4, spot, 192:320, :].astype(F32)
        for j in range(1, 4):
            dk += d_ref[r * 4 + j, spot, 64:192, :].astype(F32)
            dv += d_ref[r * 4 + j, spot, 192:320, :].astype(F32)
        dv_ref[rows, :] = dv.astype(BF)
        d = rope_backward(dk, cos, sin)
        k = k_ref[rows, :]
        t = d * gk_ref[...]
        tk_ref[rows, :] = t
        part = jnp.sum(d * k * rk, axis=0, keepdims=True)
        dgk_ref[...] = part if n == 0 else dgk_ref[...] + part
        store_sums(dot_ref, doto_ref, n, lane_sums(dot_q), lane_sums(t * k))


def unpack_grads(spots, d, q_pre, k_pre, scales, gq, gk, cos, sin):
    args = (spots, d, q_pre, k_pre, scales, gq, gk, cos, sin,)
    outs = [
            jax.ShapeDtypeStruct((1024, 256), F32),
            jax.ShapeDtypeStruct((1024, 128), F32),
            jax.ShapeDtypeStruct((1024, 128), BF),
            jax.ShapeDtypeStruct((16, 128), F32),
        jax.ShapeDtypeStruct((16, 128), F32),
            jax.ShapeDtypeStruct((1, 256), F32),
            jax.ShapeDtypeStruct((1, 128), F32),
        ]
    return pl.pallas_call(
        unpack_kernel,
        out_shape=outs,
        in_specs=[SSPEC] + [VSPEC] * 8,
        out_specs=[VSPEC] * 7,
        compiler_params=params((*args, *outs), 0),
        cost_estimate=COST,
    )(*args)


def spread(row, each, first, group, rows_of):
    count = row.shape[1]
    i = lax.broadcasted_iota(jnp.int32, (128, count), 0)
    c = lax.broadcasted_iota(jnp.int32, (128, count), 1)
    here = c // each == i - group * rows_of
    left = jnp.where(here, jnp.broadcast_to(row, (128, count)), 0.0)
    c = lax.broadcasted_iota(jnp.int32, (count, 128), 0)
    lane = lax.broadcasted_iota(jnp.int32, (count, 128), 1)
    right = (lane == first + c % each).astype(F32)
    return jnp.dot(left, right, precision=HIGHEST, preferred_element_type=F32)


def qkv_grad_kernel(
    head_ref, tq_ref, tk_ref, dv_ref, q_ref, k_ref, scale_ref, dgq_ref, dgk_ref, dga_ref, dgm_ref, *refs
):
    sums, xs, terms, (d_ref, out_ref) = refs[:4], refs[4:9], refs[9:-2], refs[-2:]
    for n in range(8):
        rows = pl.ds(128 * n, 128)
        rq, rk = column(scale_ref[n : n + 1, :]), column(scale_ref[8 + n : 9 + n, :])
        eq = rq * rq * rq * column(group_total(sums, n)) * (1.0 / 2048)
        ek = rk * rk * rk * column(group_total(sums, 8 + n)) * (1.0 / 1024)
        for g in range(2):
            cols = pl.ds(g * HD, HD)
            d_ref[rows, cols] = (rq * tq_ref[rows, cols] - eq * q_ref[rows, cols]).astype(BF)
        d_ref[rows, 256:384] = (rk * tk_ref[rows, :] - ek * k_ref[rows, :]).astype(BF)
        d_ref[rows, 384:512] = dv_ref[rows, :]
    for n in range(4):
        rows = pl.ds(256 * n, 256)
        x = jnp.concatenate([x_ref[:, rows] for x_ref in xs], axis=0)
        out_ref[rows, 0:512] = dot_tn(x, d_ref[...]).astype(BF)
    head = head_ref[0]
    gains = spread(dgq_ref[...], 16, 0, head, 16) + spread(dgk_ref[...], 8, 16, head, 16)
    gains += spread(dga_ref[...], 8, 24, 0, 0) + spread(dgm_ref[...], 8, 32, 0, 0)
    coarse = gains.astype(BF).astype(F32)
    both = coarse + pltpu.roll(gains - coarse, 64, 1)
    r = lax.broadcasted_iota(jnp.int32, (1024, 128), 0)
    i = lax.broadcasted_iota(jnp.int32, (1024, 128), 1)
    out_ref[:, 512:640] = dot_nn((r == 8 * i).astype(BF), both.astype(BF)).astype(BF)
    at = 640
    for own_ref, run_ref in zip(terms[:3], terms[3:]):
        width = own_ref.shape[1]
        total = own_ref[...].astype(F32) + run_ref[...].astype(F32)
        out_ref[:, at : at + width] = total.astype(BF)
        at += width


def qkv_grads(head, tq, tk, dv16, q_pre, k_pre, scales, gain_grads, sums, x, terms):
    args = (head, tq, tk, dv16, q_pre, k_pre, scales, *gain_grads, *sums, *x, *terms)
    outs = [
        jax.ShapeDtypeStruct((1024, 512), BF),
        jax.ShapeDtypeStruct((1024, 2048), BF),
    ]
    return pl.pallas_call(
        qkv_grad_kernel,
        out_shape=outs,
        in_specs=[SSPEC] + [VSPEC] * (len(args) - 1),
        out_specs=[VSPEC] * 2,
        compiler_params=params((*args, *outs), 4 << 20),
        cost_estimate=COST,
    )(*args)


def dot_nn(a, b):
    return lax.dot_general(a, b, (((1,), (0,)), ((), ())), preferred_element_type=F32)


def dot_nt(a, b):
    return lax.dot_general(a, b, (((1,), (1,)), ((), ())), preferred_element_type=F32)


def dot_tn(a, b):
    return lax.dot_general(a, b, (((0,), (0,)), ((), ())), preferred_element_type=F32)


def rms_rate(v):
    return lax.rsqrt(jnp.mean(v * v, axis=-1, keepdims=True) + EPSILON)


def rms_back(v, g, d):
    r = rms_rate(v)
    t = d * g
    dv = r * t - v * (r * r * r * jnp.mean(t * v, axis=-1, keepdims=True))
    return dv, d * v * r


def call(kernel, out_shape, args, us):
    args = (*args,)
    outs = [jax.ShapeDtypeStruct(s, t) for s, t in out_shape]
    return pl.pallas_call(
        kernel,
        out_shape=outs,
        in_specs=[SSPEC if a.ndim == 1 else VSPEC for a in args],
        out_specs=[VSPEC] * len(out_shape),
        compiler_params=params((*args, *outs), 0),
        cost_estimate=COST,
    )(*args)


def both_cores(part_ref, got_ref):
    got = jnp.concatenate([got_ref[128:256, :], got_ref[0:128, :]], axis=0)
    return part_ref[...].astype(F32) + got.astype(F32)


def proj_kernel(spot_ref, a_ref, *refs):
    chunks, (attn_ref, part_ref) = refs[:4], refs[4:]
    for r in range(2):
        for j in range(4):
            rows = pl.ds(r * 128 + j * 32, 32)
            for h in range(4):
                for g in range(2):
                    piece = a_ref[(r * 4 + j) * 4 + h, g * 32 : (g + 1) * 32, :]
                    attn_ref[rows, (h * 2 + g) * HD : (h * 2 + g + 1) * HD] = piece
    lefts = [
        attn_ref[:, pl.ds(pl.multiple_of(spot_ref[n] * 256, 256), 256)] for n in range(4)
    ]
    for m in range(4):
        cols = pl.ds(256 * m, 256)
        part = dot_nt(lefts[0], chunks[0][cols, 0:256])
        for n in range(1, 4):
            part += dot_nt(lefts[n], chunks[n][cols, 0:256])
        part_ref[:, cols] = part.astype(BF)


def hidden_columns(n):
    return 256 if n < 4 else 0


def forward_kernel(part_ref, got_ref, xo_ref, xt_ref, g_ref, *refs):
    chunks, (mid_ref, gate_ref, up_ref, act_ref, down_ref) = refs[:12], refs[12:]
    proj = both_cores(part_ref, got_ref)
    x = jnp.concatenate([xo_ref[...], xt_ref[...]], axis=0).astype(F32)
    m = (x + proj * rms_rate(proj) * g_ref[...]).astype(BF)
    mid_ref[...] = m
    for n, w_ref in enumerate(chunks):
        at = hidden_columns(n)
        both = dot_nn(m, w_ref[:, at : at + 256])
        gate, up = both[:, :128], both[:, 128:]
        gate_ref[n] = gate.astype(BF)
        up_ref[n] = up.astype(BF)
        act_ref[n] = (gate / (1.0 + jnp.exp(-gate)) * up).astype(BF)
    for k in range(4):
        cols = pl.ds(256 * k, 256)
        part = jnp.zeros((256, 256), F32)
        for n, w_ref in enumerate(chunks):
            at = hidden_columns(n) + 256
            part += dot_nt(act_ref[n], w_ref[cols, at : at + 128])
        down_ref[:, cols] = part.astype(BF)


def backward_kernel(
    down_ref, downg_ref, part_ref, got_ref, xo_ref, co_ref, ct_ref, ga_ref, gm_ref, gate_ref, up_ref, *refs
):
    chunks, (out_ref, dd_ref, dboth_ref, dmid_ref, dg_ref) = refs[:12], refs[12:]
    down = both_cores(down_ref, downg_ref)
    gm = gm_ref[...]
    proj = both_cores(part_ref, got_ref)[:128]
    middle = xo_ref[...].astype(F32) + proj * rms_rate(proj) * ga_ref[...]
    out_ref[...] = middle + down[:128] * rms_rate(down[:128]) * gm
    c = jnp.concatenate([co_ref[...], ct_ref[...]], axis=0).astype(F32)
    dd, terms = rms_back(down, gm, c)
    dg_ref[...] = jnp.sum(terms[:128], axis=0, keepdims=True)
    dd = dd.astype(BF)
    dd_ref[...] = dd
    for n, w_ref in enumerate(chunks):
        at = hidden_columns(n)
        d_act = dot_nn(dd, w_ref[:, at + 256 : at + 384])
        gate, up = gate_ref[n].astype(F32), up_ref[n].astype(F32)
        sig = 1.0 / (1.0 + jnp.exp(-gate))
        dboth_ref[n, :, 0:128] = (d_act * up * sig * (1.0 + gate * (1.0 - sig))).astype(BF)
        dboth_ref[n, :, 128:256] = (d_act * gate * sig).astype(BF)
    for k in range(4):
        cols = pl.ds(256 * k, 256)
        part = jnp.zeros((256, 256), F32)
        for n, w_ref in enumerate(chunks):
            at = hidden_columns(n)
            part += dot_nt(dboth_ref[n], w_ref[cols, at : at + 256])
        dmid_ref[:, cols] = part.astype(BF)


def d_attn_kernel(spot_ref, dmid_ref, dmidg_ref, part_ref, got_ref, co_ref, ct_ref, ga_ref, *refs):
    chunks, (dm_ref, dp_ref, out_ref, dg_ref) = refs[:4], refs[4:]
    c = jnp.concatenate([co_ref[...], ct_ref[...]], axis=0).astype(F32)
    d_middle = c + both_cores(dmid_ref, dmidg_ref)
    dm_ref[...] = d_middle[:128]
    dp, terms = rms_back(both_cores(part_ref, got_ref), ga_ref[...], d_middle)
    dg_ref[...] = jnp.sum(terms[:128], axis=0, keepdims=True)
    dp = dp.astype(BF)
    dp_ref[...] = dp
    for n in range(4):
        part = dot_nn(dp, chunks[n][:, 0:256]).astype(BF)
        for r in range(2):
            for j in range(4):
                for g in range(2):
                    piece = part[r * 128 + j * 32 : r * 128 + (j + 1) * 32, g * HD : (g + 1) * HD]
                    out_ref[(r * 4 + j) * 4 + spot_ref[n], g * 32 : (g + 1) * 32, :] = piece


def hidden_grads_kernel(first, m_ref, dd_ref, dboth_ref, act_ref, *outs):
    for n, out_ref in enumerate(outs):
        at = hidden_columns(first + n)
        out_ref[:, at : at + 256] = dot_tn(m_ref[...], dboth_ref[first + n]).astype(BF)
        out_ref[:, at + 256 : at + 384] = dot_tn(dd_ref[...], act_ref[first + n]).astype(BF)


def weight_grads_kernel(spot_ref, m_ref, dd_ref, dboth_ref, act_ref, dp_ref, attn_ref, *outs):
    hidden_grads_kernel(0, m_ref, dd_ref, dboth_ref, act_ref, *outs)
    for n in range(4):
        right = attn_ref[:, pl.ds(pl.multiple_of(spot_ref[n] * 256, 256), 256)]
        outs[n][:, 0:256] = dot_tn(dp_ref[...], right).astype(BF)


def finish_kernel(s_ref, gq_ref, gk_ref, gv_ref, go_ref, gg_ref, gu_ref, gd_ref, d1_ref, d2_ref, d3_ref, d4_ref):
    def total(sources, first, last):
        part = s_ref[sources[0], :, first:last].astype(F32)
        for i in sources[1:]:
            part += s_ref[i, :, first:last].astype(F32)
        return part

    def store_hidden(part, c, first):
        cols = pl.ds(c * 1536 + first, 128)
        for n, ref in enumerate((gg_ref, gu_ref, gd_ref)):
            ref[:, cols] = part[:, 128 * n : 128 * (n + 1)]

    def device(x, c, y, z):
        return (x // 2) * 64 + c * 32 + y * 8 + (x % 2) * 4 + z

    four = range(4)
    gains = jnp.zeros((1, 128), F32)
    for c in range(2):
        for m in four:
            part = total([device(x, c, y, m) for x in four for y in four], 0, 1280)
            e = c * 4 + m
            gq_ref[:, e * 256 : (e + 1) * 256] = part[:, 0:256]
            gk_ref[:, e * 128 : (e + 1) * 128] = part[:, 256:384]
            gv_ref[:, e * 128 : (e + 1) * 128] = part[:, 384:512]
            gains += part[0:1, 512:640]
            go_ref[:, e * 256 : (e + 1) * 256] = part[:, 640:896]
            store_hidden(part[:, 896:1280], c, m * 128)
            part = total([device(m, c, y, z) for y in four for z in four], 1280, 1664)
            store_hidden(part, c, 512 + m * 128)
            part = total([device(x, c, m, z) for x in four for z in four], 1664, 2048)
            store_hidden(part, c, 1024 + m * 128)
    gains = jnp.broadcast_to(gains, (8, 128))
    gains = (gains + pltpu.roll(gains, 64, 1))[0:1]
    d1_ref[...] = gains[:, 0:16]
    d2_ref[...] = gains[:, 16:24]
    d3_ref[...] = gains[:, 24:32]
    d4_ref[...] = gains[:, 32:40]


def row_places(row_lengths, spots):
    ends = jnp.cumsum(row_lengths)
    passed = spots[:, None] >= ends[None, :]
    return jnp.sum(jnp.where(passed, row_lengths[None, :], 0), axis=1)


def after(value, *others):
    return lax.optimization_barrier((value,) + others)[0]


def body(
    block_input,
    out_grad,
    lengths,
    w_query,
    w_key,
    w_value,
    w_out,
    w_gate,
    w_up,
    w_down,
    gain_query,
    gain_key,
    gain_attn,
    gain_mlp,
):
    core = lax.axis_index("c")
    z = lax.axis_index("z")
    peer = lax.axis_index("y") * 2 + lax.axis_index("xl")
    head = core * 4 + z
    my_x = block_input[0]

    columns = jnp.concatenate(
        [w_query.reshape(8, 8, 256), w_key.reshape(8, 8, 128), w_value.reshape(8, 8, 128)], axis=2
    )
    columns = columns.transpose(1, 0, 2).reshape(1, 2, 1, 1, 4, 8, 512)
    gains = jnp.concatenate([gain_query, gain_key, gain_attn, gain_mlp])
    gains = jnp.pad(gains[None, :], ((0, 7), (0, 88)))
    columns = jnp.concatenate(
        [columns, jnp.broadcast_to(gains, (1, 2, 1, 1, 4, 8, 128))], axis=-1
    )
    columns = jnp.broadcast_to(columns, (2, 2, 4, 2, 4, 8, 640)).reshape(128, 8, 640)
    columns = lax.all_to_all(columns, AXES, split_axis=0, concat_axis=0, tiled=False)
    gains = columns[:, 0, 512:552].astype(F32)
    w_head = columns.reshape(1024, 640)
    my_gains = lax.dynamic_slice_in_dim(gains, head * 16, 16, 0)
    gq, gk = my_gains[:, 0:16].reshape(1, 256), my_gains[:, 16:24].reshape(1, 128)

    ga, gm = gains[:, 24:32].reshape(1, 1024), gains[:, 32:40].reshape(1, 1024)

    def everywhere(a, shape):
        a = a.reshape(shape + (8, a.shape[-1]))
        return jnp.broadcast_to(a, (2, 2, 4, 2, 4, 8, a.shape[-1]))

    hidden = [w.reshape(8, 2, 3, 4, 128) for w in (w_gate, w_up, w_down.T)]
    hidden = jnp.concatenate(hidden, axis=-1).transpose(2, 1, 3, 0, 4)
    first = w_out.T.reshape(8, 2, 4, 256).transpose(1, 2, 0, 3)
    first = jnp.concatenate([first, hidden[0]], axis=-1)
    over_x = hidden[1].reshape(2, 2, 2, 8, 384).transpose(1, 0, 2, 3, 4)
    weights = jnp.concatenate(
        [
            everywhere(first, (1, 2, 1, 1, 4)),
            everywhere(over_x, (2, 2, 1, 2, 1)),
            everywhere(hidden[2], (1, 2, 4, 1, 1)),
        ],
        axis=-1,
    ).reshape(128, 8, 1408)
    weights = after(weights, w_head)
    weights = lax.all_to_all(weights, AXES, split_axis=0, concat_axis=0, tiled=False)
    weights = weights.reshape(1024, 1408)

    x_group = [my_x] + [shift(my_x, "z", by, False) for by in (1, -1, 2)]
    x_group = x_group + [swap(jnp.concatenate(x_group, axis=0))]
    x_own, x_other = my_x, x_group[4][:128]
    c_own = out_grad[0]
    c_other = swap(c_own)
    spots = jnp.stack([(z + n) % 4 for n in NEAR])

    q_pre, k_pre, v16, ss, ss_other = project_qkv(x_group, w_head)
    lengths = after(lengths, ss)

    my_lengths = lengths[0]
    other_lengths = swap(my_lengths)
    here = (peer * 4 + spots[:, None]) * 128 + jnp.arange(128, dtype=jnp.int32)[None, :]
    here = here.reshape(512)
    offset = jnp.concatenate(
        [here - row_places(my_lengths, here), here - row_places(other_lengths, here)]
    )
    frequency = THETA ** (-(jnp.arange(64, dtype=F32) * 2.0 / HD))
    angles = offset.astype(F32)[:, None] * frequency[None, :]
    cosine, sine = jnp.cos(angles), jnp.sin(angles)
    cos2 = jnp.concatenate([cosine, cosine], axis=1)
    sin2 = jnp.concatenate([-sine, sine], axis=1)

    task_lengths = jnp.where(peer // 4 == 0, my_lengths, other_lengths)
    task_spots = (
        jnp.arange(32, dtype=jnp.int32)[:, None, None] * 128
        + (peer % 4) * 32
        + jnp.arange(32, dtype=jnp.int32)[None, None, :]
    )
    task_spots = jnp.broadcast_to(task_spots, (32, 2, 32)).reshape(2048)
    starts = row_places(task_lengths, task_spots).reshape(8, 1, 256)
    task_spots = task_spots.reshape(8, 1, 256)
    tiles = jnp.arange(8, dtype=jnp.int32)
    low = jnp.minimum(jnp.min(starts, axis=(1, 2)) // 512, tiles)
    mid = jnp.clip((jnp.max(starts, axis=(1, 2)) + 511) // 512, low, tiles)

    packed, scales = pack_qkv(spots, q_pre, k_pre, v16, gq, gk, cos2, sin2, group_rows(ss, ss_other))
    z_spots = jnp.stack(ring_spots("z")).astype(jnp.int32)
    pinned = (packed, weights, low, mid, starts, task_spots, ga, gm, z_spots, x_other, c_other)
    pinned = lax.optimization_barrier(pinned)
    packed, weights, low, mid, starts, task_spots, ga, gm, z_spots, x_other, c_other = pinned
    received = lax.all_to_all(packed, ("y", "xl"), split_axis=0, concat_axis=0, tiled=False)
    chunks = jnp.split(weights, [640, 1024], axis=1)

    z_one = onward(chunks[0], "z")
    received, z_one, *chunks = lax.optimization_barrier((received.reshape(32, 320, HD), z_one, *chunks))
    z_two = onward(z_one, "z")
    near = [(onward(w, ring), shift(w, ring, -1, True)) for w, ring in zip(chunks[1:], "xy")]
    attn, acc, lse = attend(received, low, mid, starts, task_spots)
    ones, threes = zip(*near)
    attn, z_two, *near = lax.optimization_barrier((attn, z_two, *ones, *threes))
    ones, threes = near[:2], near[2:]
    attn = lax.all_to_all(attn, SEQ, split_axis=0, concat_axis=0, tiled=False)
    z_three = onward(z_two, "z")
    twos = [onward(one, ring) for one, ring in zip(ones, "xy")]
    attn, z_three, *twos = lax.optimization_barrier((attn, z_three, *twos))
    whole = [chunks[0], z_one, z_two, z_three]
    for own, one, two, three in zip(chunks[1:], ones, twos, threes):
        whole += [own, one, two, three]
    chunks = whole

    flat, half, vec = (256, 1024), (128, 1024), (1, 1024)
    wide, pairs = (12, 256, 128), (12, 256, 256)
    attn16, part = call(
        proj_kernel, [(flat, BF), (flat, BF)], (z_spots, attn, *chunks[:4]), 4
    )
    parts = (part, swap(part))
    mid16, gate, up, act16, down = call(
        forward_kernel,
        [(flat, BF), (wide, BF), (wide, BF), (wide, BF), (flat, BF)],
        (*parts, x_own, x_other, ga, *chunks),
        6,
    )
    output, dd16, d_both, d_mid, dg_mlp = call(
        backward_kernel,
        [(half, F32), (flat, BF), (pairs, BF), (flat, BF), (vec, F32)],
        (down, swap(down), *parts, x_own, c_own, c_other, ga, gm, gate, up, *chunks),
        7,
    )
    d_middle, dp16, d_attn, dg_attn = call(
        d_attn_kernel,
        [(half, F32), (flat, BF), ((32, 64, HD), BF), (vec, F32)],
        (z_spots, d_mid, swap(d_mid), *parts, c_own, c_other, ga, *chunks[:4]),
        3,
    )

    d_attn, d_both = lax.optimization_barrier((d_attn, d_both))
    d_attn = lax.all_to_all(d_attn, SEQ, split_axis=0, concat_axis=0, tiled=False)
    sources = (mid16, dd16, d_both, act16)
    grads = call(
        weight_grads_kernel,
        [((1024, 640), BF)] * 4 + [((1024, 384), BF)] * 8,
        (z_spots, *sources, dp16, attn16),
        6,
    )
    grads = (grads[:4], grads[4:8], grads[8:])
    runs = [onward(g[1], ring) for g, ring in zip(grads, RINGS)]
    d_attn, *runs = lax.optimization_barrier((d_attn, *runs))
    runs = [plus(g[2], run) for g, run in zip(grads, runs)]
    d_attn, *runs = lax.optimization_barrier((d_attn, *runs))
    runs = [onward(run, ring) for run, ring in zip(runs, RINGS)]

    d_pairs = attend_grad(received, d_attn, acc, lse, low, mid, starts, task_spots)
    d_pairs, *runs = lax.optimization_barrier((d_pairs, *runs))
    runs = [plus(g[3], run) for g, run in zip(grads, runs)]
    runs = [onward(run, ring) for run, ring in zip(runs, RINGS)]
    d_pairs = d_pairs.reshape(8, 4, 320, HD)
    d_pairs = lax.all_to_all(d_pairs, ("y", "xl"), split_axis=0, concat_axis=0, tiled=False)
    tq, tk, dv16, dots, dots_other, dgq, dgk = unpack_grads(
        spots, d_pairs, q_pre, k_pre, scales, gq, gk, cos2, sin2
    )
    sums, runs = lax.optimization_barrier((group_rows(dots, dots_other), runs))

    gain_grads = (dgq, dgk, dg_attn, dg_mlp)
    terms = [g[0] for g in grads] + runs
    d_pre, shares = qkv_grads(
        head[None], tq, tk, dv16, q_pre, k_pre, scales, gain_grads, sums, x_group, terms
    )
    shares = lax.all_to_all(
        shares.reshape(128, 8, 2048), AXES, split_axis=0, concat_axis=0, tiled=False
    )
    d_x = dot_nt(d_pre, w_head[:, :512]).astype(BF)
    d_x = (d_x[:512].astype(F32) + swap(d_x[512:]).astype(F32)).astype(BF)
    widths = (2048, 1024, 1024, 2048, 3072, 3072, 3072)
    outs = [((8, w), F32) for w in widths] + [((1, w), F32) for w in (16, 8, 8, 8)]
    gq, gk, gv, go, gg, gu, gd, *dgains = call(finish_kernel, outs, (shares,), 3)
    d_middle = d_middle + d_x[:128].astype(F32)
    for n, by in enumerate((-1, 1, 2)):
        piece = shift(d_x[128 * (n + 1) : 128 * (n + 2)], "z", by, False)
        d_middle = d_middle + after(piece, gq).astype(F32)

    return (output[None], d_middle[None], gq, gk, gv, go.T, gg, gu, gd.T, *[d[0] for d in dgains])


def solution(mesh):
    cube_mesh = Mesh(mesh.devices.reshape(2, 2, 4, 2, 4), AXES)
    row, seq = ("xh", "c"), SEQ
    everything = row + seq
    tokens, rows, cols, vec = (
        P(row, seq, None),
        P(everything, None),
        P(None, everything),
        P(everything),
    )
    in_specs = (tokens, tokens, P(row, None), rows, rows, rows, cols, rows, rows, cols) + (vec,) * 4
    out_specs = (tokens, tokens, rows, rows, rows, cols, rows, rows, cols) + (vec,) * 4
    return jax.shard_map(body, mesh=cube_mesh, in_specs=in_specs, out_specs=out_specs, check_vma=False)
```

```python
import functools
import math

import jax
import jax.numpy as jnp
from jax import lax
from jax.experimental import pallas as pl
from jax.experimental.pallas import tpu as pltpu
from jax.sharding import Mesh, PartitionSpec as P

BF = jnp.bfloat16
F32 = jnp.float32
HD = 128
EPSILON = 1e-06
THETA = 500000.0
AXES = ("xh", "c", "y", "xl", "z")
SEQ = ("y", "xl", "z")
LOG2E = 1.4426950408889634
HIGHEST = lax.Precision.HIGHEST
COST = pl.CostEstimate(flops=1, bytes_accessed=1, transcendentals=0)


def swap(a):
    return lax.ppermute(a, "c", [(0, 1), (1, 0)])


def shift(a, ring, by, mirrored):
    axes = ("xh", "c", "xl") if ring == "x" else ("c", ring)

    def index(c, m):
        return (m // 2) * 4 + c * 2 + m % 2 if ring == "x" else c * 4 + m

    pairs = []
    for c in range(2):
        step = -by if (mirrored and c == 1) else by
        pairs += [(index(c, m), index(c, (m + step) % 4)) for m in range(4)]
    return lax.ppermute(a, axes, pairs)


def position(ring):
    if ring == "x":
        return lax.axis_index("xh") * 2 + lax.axis_index("xl")
    return lax.axis_index(ring)


def params(arrays, scratch=0):
    total = scratch + sum(math.prod(a.shape) * jnp.dtype(a.dtype).itemsize for a in arrays)
    return pltpu.CompilerParams(vmem_limit_bytes=total + total // 8 + (3 << 20))


VSPEC = pl.BlockSpec(memory_space=pltpu.VMEM)
SSPEC = pl.BlockSpec(memory_space=pltpu.SMEM)
HSPEC = pl.BlockSpec(memory_space=pltpu.HBM)


RINGS = ("z", "x", "y")


def ring_spots(ring):
    here, sign = position(ring), 1 - 2 * lax.axis_index("c")
    return [(here - sign * n) % 4 for n in range(4)]


def onward(block, ring):
    return shift(block, ring, 1, True)


def plus(a, b):
    return (a.astype(F32) + b.astype(F32)).astype(BF)


NEAR = (0, 3, 1, 2)


def rope_forward(v, cos, sin):
    return v * cos + pltpu.roll(v, 64, 1) * sin


def rope_backward(d, cos, sin):
    return d * cos - pltpu.roll(d, 64, 1) * sin


def lane_sums(a):
    ones = jnp.ones((8, a.shape[1]), F32)
    rows = lax.dot_general(
        ones, a, (((1,), (1,)), ((), ())), precision=HIGHEST, preferred_element_type=F32
    )
    return rows[0:1]


def store_sums(own_ref, other_ref, n, q_sum, k_sum):
    own_ref[n : n + 1, :] = q_sum
    own_ref[8 + n : 9 + n, :] = k_sum
    m = (n + 4) % 8
    other_ref[m : m + 1, :] = q_sum
    other_ref[8 + m : 9 + m, :] = k_sum


def column(row):
    return jnp.broadcast_to(row, (128, 128)).T


def group_rows(part, for_other):
    total = part + swap(for_other)
    return [total] + [shift(total, "z", by, False) for by in (1, -1, 2)]


def group_total(refs, n):
    first, k = n // 4 * 4, n % 4
    total = refs[0][n : n + 1, :]
    for ref, by in zip(refs[1:], (1, -1, 2)):
        at = first + NEAR.index((NEAR[k] + by) % 4)
        total += ref[at : at + 1, :]
    return total


def qkv_kernel(w_ref, *refs):
    xs, (q_ref, k_ref, v_ref, ss_ref, sso_ref) = refs[:5], refs[5:]
    for n in range(8):
        rows = pl.ds(128 * n, 128)
        x = xs[n][...] if n < 4 else xs[4][128 * (n - 4) : 128 * (n - 3), :]
        pre = jnp.dot(x, w_ref[:, :512], preferred_element_type=F32)
        q, k = pre[:, :256], pre[:, 256:384]
        q_ref[rows, :] = q
        k_ref[rows, :] = k
        v_ref[rows, :] = pre[:, 384:].astype(BF)
        store_sums(ss_ref, sso_ref, n, lane_sums(q * q), lane_sums(k * k))


def project_qkv(x, w):
    args = (w, *x)
    outs = [
            jax.ShapeDtypeStruct((1024, 256), F32),
            jax.ShapeDtypeStruct((1024, 128), F32),
            jax.ShapeDtypeStruct((1024, 128), BF),
            jax.ShapeDtypeStruct((16, 128), F32),
        jax.ShapeDtypeStruct((16, 128), F32),
        ]
    return pl.pallas_call(
        qkv_kernel,
        out_shape=outs,
        in_specs=[VSPEC] * 6,
        out_specs=[VSPEC] * 5,
        compiler_params=params((*args, *outs), 0),
        cost_estimate=COST,
    )(*args)


def send_kernel(
    spot_ref, q_ref, k_ref, v_ref, gq_ref, gk_ref, cos_ref, sin_ref, s0_ref, s1_ref, s2_ref, s3_ref, out_ref, scale_ref
):
    sums = (s0_ref, s1_ref, s2_ref, s3_ref)
    for n in range(16):
        width = 2048 if n < 8 else 1024
        mean = group_total(sums, n) * (1.0 / width)
        scale_ref[n : n + 1, :] = lax.rsqrt(mean + EPSILON)
    for n in range(8):
        r, spot = n // 4, spot_ref[n % 4]
        rows = pl.ds(128 * n, 128)
        cos, sin = cos_ref[rows, :], sin_ref[rows, :]
        rq, rk = column(scale_ref[n : n + 1, :]), column(scale_ref[8 + n : 9 + n, :])
        for g in range(2):
            cols = pl.ds(g * HD, HD)
            q = rope_forward(q_ref[rows, cols] * rq * gq_ref[:, cols], cos, sin).astype(BF)
            for j in range(4):
                out_ref[r * 4 + j, spot, g * 32 : (g + 1) * 32, :] = q[32 * j : 32 * j + 32]
        k = rope_forward(k_ref[rows, :] * rk * gk_ref[...], cos, sin).astype(BF)
        v = v_ref[rows, :]
        for j in range(4):
            out_ref[r * 4 + j, spot, 64:192, :] = k
            out_ref[r * 4 + j, spot, 192:320, :] = v


def pack_qkv(spots, q_pre, k_pre, v16, gq, gk, cos, sin, sums):
    args = (spots, q_pre, k_pre, v16, gq, gk, cos, sin, *sums)
    outs = [
        jax.ShapeDtypeStruct((8, 4, 320, HD), BF),
        jax.ShapeDtypeStruct((16, 128), F32),
    ]
    return pl.pallas_call(
        send_kernel,
        out_shape=outs,
        in_specs=[SSPEC] + [VSPEC] * 11,
        out_specs=[VSPEC] * 2,
        compiler_params=params((*args, *outs)),
        cost_estimate=COST,
    )(*args)


def grouped(first, last, step, carry):
    for size in (2, 1):
        count = (last - first) // size

        def body(n, c, size=size, first=first):
            return step([first + size * n + m for m in range(size)], c)

        carry = lax.fori_loop(0, count, body, carry)
        first = first + size * count
    return carry


def tile_mask(kt, starts, spots):
    keys = kt * 512 + lax.broadcasted_iota(jnp.int32, (512, 512), 0)
    return (keys >= starts) & (keys <= spots)


def attend_kernel(scale2, low_ref, mid_ref, r_ref, start_ref, spot_ref, out_ref, acc_ref, lse_ref, vt_ref):
    for b in range(32):
        vt_ref[:, b * 128 : (b + 1) * 128] = r_ref[b, 192:320, :].T

    def tile(i, _):
        q = r_ref[pl.ds(8 * i, 8), 0:64, :].reshape(512, HD)
        starts, spots = start_ref[i], spot_ref[i]

        def step(masked, kts, carry):
            top, total, acc = carry
            tiles = []
            for kt in kts:
                k = r_ref[pl.ds(4 * kt, 4), 64:192, :].reshape(512, HD)
                s = lax.dot_general(k, q, (((1,), (1,)), ((), ())), preferred_element_type=F32)
                s = s * scale2
                tiles.append(jnp.where(tile_mask(kt, starts, spots), s, -1e30) if masked else s)
            new_top = top
            for s in tiles:
                new_top = jnp.maximum(new_top, jnp.max(s, axis=0, keepdims=True))
            fade = jnp.exp2(top - new_top)
            total, acc = total * fade, acc * fade
            for kt, s in zip(kts, tiles):
                p = jnp.exp2(s - new_top)
                total += jnp.sum(p, axis=0, keepdims=True)
                vt = vt_ref[:, pl.ds(pl.multiple_of(kt * 512, 512), 512)]
                acc += jnp.dot(vt, p.astype(BF), preferred_element_type=F32)
            return new_top, total, acc

        carry = (
            jnp.full((1, 512), -1e30, F32),
            jnp.zeros((1, 512), F32),
            jnp.zeros((HD, 512), F32),
        )
        first = mid_ref[i]
        carry = lax.fori_loop(low_ref[i], first, lambda kt, c: step(True, (kt,), c), carry)
        carry = grouped(first, 2 * i, functools.partial(step, False), carry)
        top, total, acc = step(True, (2 * i, 2 * i + 1), carry)
        acc = acc / total
        acc_ref[i] = acc
        lse_ref[i] = top + jnp.log2(total)
        out_ref[pl.ds(8 * i, 8)] = acc.T.astype(BF).reshape(8, 64, HD)
        return 0

    lax.fori_loop(0, 4, tile, 0)


def attend(received, low, mid, starts, spots):
    args = (low, mid, received, starts, spots,)
    outs = [
            jax.ShapeDtypeStruct((32, 64, HD), BF),
            jax.ShapeDtypeStruct((4, HD, 512), F32),
            jax.ShapeDtypeStruct((4, 1, 512), F32),
        ]
    return pl.pallas_call(
        functools.partial(attend_kernel, LOG2E / math.sqrt(HD)),
        out_shape=outs,
        in_specs=[SSPEC] * 2 + [VSPEC] * 3,
        out_specs=[VSPEC] * 3,
        scratch_shapes=[pltpu.VMEM((HD, 4096), BF)],
        compiler_params=params((*args, *outs), 1 << 20),
        cost_estimate=COST,
    )(*args)


def attend_grad_kernel(
    scale2, scale, low_ref, mid_ref, r_ref, do_ref, acc_ref, lse_ref, start_ref, spot_ref, out_ref, kt_ref, dk_ref, dv_ref
):
    for b in range(32):
        kt_ref[:, b * 128 : (b + 1) * 128] = r_ref[b, 64:192, :].T
    dk_ref[...] = jnp.zeros_like(dk_ref)
    dv_ref[...] = jnp.zeros_like(dv_ref)

    def tile(i, _):
        q = r_ref[pl.ds(8 * i, 8), 0:64, :].reshape(512, HD)
        do = do_ref[pl.ds(8 * i, 8)].reshape(512, HD)
        delta = jnp.sum(do.astype(F32).T * acc_ref[i], axis=0, keepdims=True)
        lse, starts, spots = lse_ref[i], start_ref[i], spot_ref[i]

        def step(masked, kts, dq):
            for kt in kts:
                k = r_ref[pl.ds(4 * kt, 4), 64:192, :].reshape(512, HD)
                v = r_ref[pl.ds(4 * kt, 4), 192:320, :].reshape(512, HD)
                s = lax.dot_general(k, q, (((1,), (1,)), ((), ())), preferred_element_type=F32)
                e = s * scale2 - lse
                if masked:
                    e = jnp.where(tile_mask(kt, starts, spots), e, -1e30)
                p = jnp.exp2(e)
                dp = lax.dot_general(v, do, (((1,), (1,)), ((), ())), preferred_element_type=F32)
                ds = (p * (dp - delta)).astype(BF)
                keys = pl.ds(pl.multiple_of(kt * 512, 512), 512)
                dv_ref[keys, :] += jnp.dot(p.astype(BF), do, preferred_element_type=F32)
                dk_ref[keys, :] += jnp.dot(ds, q, preferred_element_type=F32)
                dq += jnp.dot(kt_ref[:, keys], ds, preferred_element_type=F32)
            return dq

        dq = jnp.zeros((HD, 512), F32)
        first = mid_ref[i]
        dq = lax.fori_loop(low_ref[i], first, lambda kt, c: step(True, (kt,), c), dq)
        dq = grouped(first, 2 * i, functools.partial(step, False), dq)
        dq = step(True, (2 * i, 2 * i + 1), dq)
        out_ref[pl.ds(8 * i, 8), 0:64, :] = (dq * scale).T.astype(BF).reshape(8, 64, HD)
        return 0

    lax.fori_loop(0, 4, tile, 0)
    for b in range(32):
        out_ref[b, 64:192, :] = (dk_ref[b * 128 : (b + 1) * 128, :] * scale).astype(BF)
        out_ref[b, 192:320, :] = dv_ref[b * 128 : (b + 1) * 128, :].astype(BF)


def attend_grad(received, d_attn, acc, lse, low, mid, starts, spots):
    args = (low, mid, received, d_attn, acc, lse, starts, spots,)
    outs = [jax.ShapeDtypeStruct((32, 320, HD), BF)]
    return pl.pallas_call(
        functools.partial(attend_grad_kernel, LOG2E / math.sqrt(HD), 1.0 / math.sqrt(HD)),
        out_shape=outs[0],
        in_specs=[SSPEC] * 2 + [VSPEC] * 6,
        out_specs=VSPEC,
        scratch_shapes=[
            pltpu.VMEM((HD, 4096), BF),
            pltpu.VMEM((4096, HD), F32),
            pltpu.VMEM((4096, HD), F32),
        ],
        compiler_params=params((*args, *outs), 5 << 20),
        cost_estimate=COST,
    )(*args)


def unpack_kernel(
    spot_ref, d_ref, q_ref, k_ref, scale_ref, gq_ref, gk_ref, cos_ref, sin_ref, tq_ref, tk_ref, dv_ref, dot_ref, doto_ref, dgq_ref, dgk_ref
):
    for n in range(8):
        r, spot = n // 4, spot_ref[n % 4]
        rows = pl.ds(128 * n, 128)
        cos, sin = cos_ref[rows, :], sin_ref[rows, :]
        rq, rk = column(scale_ref[n : n + 1, :]), column(scale_ref[8 + n : 9 + n, :])
        dot_q = jnp.zeros((128, HD), F32)
        for g in range(2):
            cols = pl.ds(g * HD, HD)
            d = jnp.concatenate(
                [d_ref[r * 4 + j, spot, g * 32 : (g + 1) * 32, :] for j in range(4)], axis=0
            ).astype(F32)
            d = rope_backward(d, cos, sin)
            q = q_ref[rows, cols]
            t = d * gq_ref[:, cols]
            tq_ref[rows, cols] = t
            dot_q += t * q
            part = jnp.sum(d * q * rq, axis=0, keepdims=True)
            dgq_ref[:, cols] = part if n == 0 else dgq_ref[:, cols] + part
        dk = d_ref[r * 4, spot, 64:192, :].astype(F32)
        dv = d_ref[r * 4, spot, 192:320, :].astype(F32)
        for j in range(1, 4):
            dk += d_ref[r * 4 + j, spot, 64:192, :].astype(F32)
            dv += d_ref[r * 4 + j, spot, 192:320, :].astype(F32)
        dv_ref[rows, :] = dv.astype(BF)
        d = rope_backward(dk, cos, sin)
        k = k_ref[rows, :]
        t = d * gk_ref[...]
        tk_ref[rows, :] = t
        part = jnp.sum(d * k * rk, axis=0, keepdims=True)
        dgk_ref[...] = part if n == 0 else dgk_ref[...] + part
        store_sums(dot_ref, doto_ref, n, lane_sums(dot_q), lane_sums(t * k))


def unpack_grads(spots, d, q_pre, k_pre, scales, gq, gk, cos, sin):
    args = (spots, d, q_pre, k_pre, scales, gq, gk, cos, sin,)
    outs = [
            jax.ShapeDtypeStruct((1024, 256), F32),
            jax.ShapeDtypeStruct((1024, 128), F32),
            jax.ShapeDtypeStruct((1024, 128), BF),
            jax.ShapeDtypeStruct((16, 128), F32),
        jax.ShapeDtypeStruct((16, 128), F32),
            jax.ShapeDtypeStruct((1, 256), F32),
            jax.ShapeDtypeStruct((1, 128), F32),
        ]
    return pl.pallas_call(
        unpack_kernel,
        out_shape=outs,
        in_specs=[SSPEC] + [VSPEC] * 8,
        out_specs=[VSPEC] * 7,
        compiler_params=params((*args, *outs), 0),
        cost_estimate=COST,
    )(*args)


def spread(row, each, first, group, rows_of):
    count = row.shape[1]
    i = lax.broadcasted_iota(jnp.int32, (128, count), 0)
    c = lax.broadcasted_iota(jnp.int32, (128, count), 1)
    here = c // each == i - group * rows_of
    left = jnp.where(here, jnp.broadcast_to(row, (128, count)), 0.0)
    c = lax.broadcasted_iota(jnp.int32, (count, 128), 0)
    lane = lax.broadcasted_iota(jnp.int32, (count, 128), 1)
    right = (lane == first + c % each).astype(F32)
    return jnp.dot(left, right, precision=HIGHEST, preferred_element_type=F32)


def qkv_grad_kernel(
    head_ref, tq_ref, tk_ref, dv_ref, q_ref, k_ref, scale_ref, dgq_ref, dgk_ref, dga_ref, dgm_ref, *refs
):
    sums, xs, (d_ref, shares_ref, out_ref, sem) = refs[:4], refs[4:9], refs[10:]
    for n in range(8):
        rows = pl.ds(128 * n, 128)
        rq, rk = column(scale_ref[n : n + 1, :]), column(scale_ref[8 + n : 9 + n, :])
        eq = rq * rq * rq * column(group_total(sums, n)) * (1.0 / 2048)
        ek = rk * rk * rk * column(group_total(sums, 8 + n)) * (1.0 / 1024)
        for g in range(2):
            cols = pl.ds(g * HD, HD)
            d_ref[rows, cols] = (rq * tq_ref[rows, cols] - eq * q_ref[rows, cols]).astype(BF)
        d_ref[rows, 256:384] = (rk * tk_ref[rows, :] - ek * k_ref[rows, :]).astype(BF)
        d_ref[rows, 384:512] = dv_ref[rows, :]
    for n in range(4):
        rows = pl.ds(256 * n, 256)
        x = jnp.concatenate([x_ref[:, rows] for x_ref in xs], axis=0)
        out_ref[rows, 0:512] = dot_tn(x, d_ref[...]).astype(BF)
    head = head_ref[0]
    gains = spread(dgq_ref[...], 16, 0, head, 16) + spread(dgk_ref[...], 8, 16, head, 16)
    gains += spread(dga_ref[...], 8, 24, 0, 0) + spread(dgm_ref[...], 8, 32, 0, 0)
    coarse = gains.astype(BF).astype(F32)
    both = coarse + pltpu.roll(gains - coarse, 64, 1)
    r = lax.broadcasted_iota(jnp.int32, (1024, 128), 0)
    i = lax.broadcasted_iota(jnp.int32, (1024, 128), 1)
    out_ref[:, 512:640] = dot_nn((r == 8 * i).astype(BF), both.astype(BF)).astype(BF)
    copy = pltpu.make_async_copy(out_ref, shares_ref.at[:, 0:640], sem)
    copy.start()
    copy.wait()


def qkv_grads(head, tq, tk, dv16, q_pre, k_pre, scales, gain_grads, sums, x, shares):
    args = (head, tq, tk, dv16, q_pre, k_pre, scales, *gain_grads, *sums, *x, shares)
    outs = [
        jax.ShapeDtypeStruct((1024, 512), BF),
        jax.ShapeDtypeStruct((1024, 2048), BF),
    ]
    return pl.pallas_call(
        qkv_grad_kernel,
        out_shape=outs,
        in_specs=[SSPEC] + [VSPEC] * (len(args) - 2) + [HSPEC],
        out_specs=[VSPEC, HSPEC],
        scratch_shapes=[pltpu.VMEM((1024, 640), BF), pltpu.SemaphoreType.DMA],
        input_output_aliases={len(args) - 1: 1},
        compiler_params=params(args[:-1] + (outs[0],), 6 << 20),
        cost_estimate=COST,
    )(*args)


def ring_end_kernel(*refs):
    terms, (shares_ref, total_ref, sems) = refs[:6], refs[6:]
    copies, at = [], 0
    for n, (own_ref, run_ref) in enumerate(zip(terms[:3], terms[3:])):
        width = own_ref.shape[1]
        total = own_ref[...].astype(F32) + run_ref[...].astype(F32)
        total_ref[:, at : at + width] = total.astype(BF)
        target = shares_ref.at[:, 640 + at : 640 + at + width]
        copies.append(pltpu.make_async_copy(total_ref.at[:, at : at + width], target, sems.at[n]))
        copies[-1].start()
        at += width
    for copy in copies:
        copy.wait()


def ring_end(terms):
    out = jax.ShapeDtypeStruct((1024, 2048), BF)
    return pl.pallas_call(
        ring_end_kernel,
        out_shape=out,
        in_specs=[VSPEC] * 6,
        out_specs=HSPEC,
        scratch_shapes=[pltpu.VMEM((1024, 1408), BF), pltpu.SemaphoreType.DMA((3,))],
        compiler_params=params(terms, 3 << 20),
        cost_estimate=COST,
    )(*terms)


def dot_nn(a, b):
    return lax.dot_general(a, b, (((1,), (0,)), ((), ())), preferred_element_type=F32)


def dot_nt(a, b):
    return lax.dot_general(a, b, (((1,), (1,)), ((), ())), preferred_element_type=F32)


def dot_tn(a, b):
    return lax.dot_general(a, b, (((0,), (0,)), ((), ())), preferred_element_type=F32)


def rms_rate(v):
    return lax.rsqrt(jnp.mean(v * v, axis=-1, keepdims=True) + EPSILON)


def rms_back(v, g, d):
    r = rms_rate(v)
    t = d * g
    dv = r * t - v * (r * r * r * jnp.mean(t * v, axis=-1, keepdims=True))
    return dv, d * v * r


def call(kernel, out_shape, args, us):
    args = (*args,)
    outs = [jax.ShapeDtypeStruct(s, t) for s, t in out_shape]
    return pl.pallas_call(
        kernel,
        out_shape=outs,
        in_specs=[SSPEC if a.ndim == 1 else VSPEC for a in args],
        out_specs=[VSPEC] * len(out_shape),
        compiler_params=params((*args, *outs), 0),
        cost_estimate=COST,
    )(*args)


def both_cores(part_ref, got_ref):
    got = jnp.concatenate([got_ref[128:256, :], got_ref[0:128, :]], axis=0)
    return part_ref[...].astype(F32) + got.astype(F32)


def proj_kernel(spot_ref, a_ref, *refs):
    chunks, (attn_ref, part_ref) = refs[:4], refs[4:]
    for r in range(2):
        for j in range(4):
            rows = pl.ds(r * 128 + j * 32, 32)
            for h in range(4):
                for g in range(2):
                    piece = a_ref[(r * 4 + j) * 4 + h, g * 32 : (g + 1) * 32, :]
                    attn_ref[rows, (h * 2 + g) * HD : (h * 2 + g + 1) * HD] = piece
    lefts = [
        attn_ref[:, pl.ds(pl.multiple_of(spot_ref[n] * 256, 256), 256)] for n in range(4)
    ]
    for m in range(4):
        cols = pl.ds(256 * m, 256)
        part = dot_nt(lefts[0], chunks[0][cols, 0:256])
        for n in range(1, 4):
            part += dot_nt(lefts[n], chunks[n][cols, 0:256])
        part_ref[:, cols] = part.astype(BF)


def hidden_columns(n):
    return 256 if n < 4 else 0


def forward_kernel(part_ref, got_ref, xo_ref, xt_ref, g_ref, *refs):
    chunks, (mid_ref, gate_ref, up_ref, act_ref, down_ref) = refs[:12], refs[12:]
    proj = both_cores(part_ref, got_ref)
    x = jnp.concatenate([xo_ref[...], xt_ref[...]], axis=0).astype(F32)
    m = (x + proj * rms_rate(proj) * g_ref[...]).astype(BF)
    mid_ref[...] = m
    for n, w_ref in enumerate(chunks):
        at = hidden_columns(n)
        both = dot_nn(m, w_ref[:, at : at + 256])
        gate, up = both[:, :128], both[:, 128:]
        gate_ref[n] = gate.astype(BF)
        up_ref[n] = up.astype(BF)
        act_ref[n] = (gate / (1.0 + jnp.exp(-gate)) * up).astype(BF)
    for k in range(4):
        cols = pl.ds(256 * k, 256)
        part = jnp.zeros((256, 256), F32)
        for n, w_ref in enumerate(chunks):
            at = hidden_columns(n) + 256
            part += dot_nt(act_ref[n], w_ref[cols, at : at + 128])
        down_ref[:, cols] = part.astype(BF)


def backward_kernel(
    down_ref, downg_ref, part_ref, got_ref, xo_ref, co_ref, ct_ref, ga_ref, gm_ref, gate_ref, up_ref, *refs
):
    chunks, (out_ref, dd_ref, dboth_ref, dmid_ref, dg_ref) = refs[:12], refs[12:]
    down = both_cores(down_ref, downg_ref)
    gm = gm_ref[...]
    proj = both_cores(part_ref, got_ref)[:128]
    middle = xo_ref[...].astype(F32) + proj * rms_rate(proj) * ga_ref[...]
    out_ref[...] = middle + down[:128] * rms_rate(down[:128]) * gm
    c = jnp.concatenate([co_ref[...], ct_ref[...]], axis=0).astype(F32)
    dd, terms = rms_back(down, gm, c)
    dg_ref[...] = jnp.sum(terms[:128], axis=0, keepdims=True)
    dd = dd.astype(BF)
    dd_ref[...] = dd
    for n, w_ref in enumerate(chunks):
        at = hidden_columns(n)
        d_act = dot_nn(dd, w_ref[:, at + 256 : at + 384])
        gate, up = gate_ref[n].astype(F32), up_ref[n].astype(F32)
        sig = 1.0 / (1.0 + jnp.exp(-gate))
        dboth_ref[n, :, 0:128] = (d_act * up * sig * (1.0 + gate * (1.0 - sig))).astype(BF)
        dboth_ref[n, :, 128:256] = (d_act * gate * sig).astype(BF)
    for k in range(4):
        cols = pl.ds(256 * k, 256)
        part = jnp.zeros((256, 256), F32)
        for n, w_ref in enumerate(chunks):
            at = hidden_columns(n)
            part += dot_nt(dboth_ref[n], w_ref[cols, at : at + 256])
        dmid_ref[:, cols] = part.astype(BF)


def d_attn_kernel(spot_ref, dmid_ref, dmidg_ref, part_ref, got_ref, co_ref, ct_ref, ga_ref, *refs):
    chunks, (dm_ref, dp_ref, out_ref, dg_ref) = refs[:4], refs[4:]
    c = jnp.concatenate([co_ref[...], ct_ref[...]], axis=0).astype(F32)
    d_middle = c + both_cores(dmid_ref, dmidg_ref)
    dm_ref[...] = d_middle[:128]
    dp, terms = rms_back(both_cores(part_ref, got_ref), ga_ref[...], d_middle)
    dg_ref[...] = jnp.sum(terms[:128], axis=0, keepdims=True)
    dp = dp.astype(BF)
    dp_ref[...] = dp
    for n in range(4):
        part = dot_nn(dp, chunks[n][:, 0:256]).astype(BF)
        for r in range(2):
            for j in range(4):
                for g in range(2):
                    piece = part[r * 128 + j * 32 : r * 128 + (j + 1) * 32, g * HD : (g + 1) * HD]
                    out_ref[(r * 4 + j) * 4 + spot_ref[n], g * 32 : (g + 1) * 32, :] = piece


def hidden_grads_kernel(first, m_ref, dd_ref, dboth_ref, act_ref, *outs):
    for n, out_ref in enumerate(outs):
        at = hidden_columns(first + n)
        out_ref[:, at : at + 256] = dot_tn(m_ref[...], dboth_ref[first + n]).astype(BF)
        out_ref[:, at + 256 : at + 384] = dot_tn(dd_ref[...], act_ref[first + n]).astype(BF)


def weight_grads_kernel(spot_ref, m_ref, dd_ref, dboth_ref, act_ref, dp_ref, attn_ref, *outs):
    hidden_grads_kernel(0, m_ref, dd_ref, dboth_ref, act_ref, *outs)
    for n in range(4):
        right = attn_ref[:, pl.ds(pl.multiple_of(spot_ref[n] * 256, 256), 256)]
        outs[n][:, 0:256] = dot_tn(dp_ref[...], right).astype(BF)


def finish_kernel(s_ref, gq_ref, gk_ref, gv_ref, go_ref, gg_ref, gu_ref, gd_ref, d1_ref, d2_ref, d3_ref, d4_ref):
    def total(sources, first, last):
        part = s_ref[sources[0], :, first:last].astype(F32)
        for i in sources[1:]:
            part += s_ref[i, :, first:last].astype(F32)
        return part

    def store_hidden(part, c, first):
        cols = pl.ds(c * 1536 + first, 128)
        for n, ref in enumerate((gg_ref, gu_ref, gd_ref)):
            ref[:, cols] = part[:, 128 * n : 128 * (n + 1)]

    def device(x, c, y, z):
        return (x // 2) * 64 + c * 32 + y * 8 + (x % 2) * 4 + z

    four = range(4)
    gains = jnp.zeros((1, 128), F32)
    for c in range(2):
        for m in four:
            part = total([device(x, c, y, m) for x in four for y in four], 0, 1280)
            e = c * 4 + m
            gq_ref[:, e * 256 : (e + 1) * 256] = part[:, 0:256]
            gk_ref[:, e * 128 : (e + 1) * 128] = part[:, 256:384]
            gv_ref[:, e * 128 : (e + 1) * 128] = part[:, 384:512]
            gains += part[0:1, 512:640]
            go_ref[:, e * 256 : (e + 1) * 256] = part[:, 640:896]
            store_hidden(part[:, 896:1280], c, m * 128)
            part = total([device(m, c, y, z) for y in four for z in four], 1280, 1664)
            store_hidden(part, c, 512 + m * 128)
            part = total([device(x, c, m, z) for x in four for z in four], 1664, 2048)
            store_hidden(part, c, 1024 + m * 128)
    gains = jnp.broadcast_to(gains, (8, 128))
    gains = (gains + pltpu.roll(gains, 64, 1))[0:1]
    d1_ref[...] = gains[:, 0:16]
    d2_ref[...] = gains[:, 16:24]
    d3_ref[...] = gains[:, 24:32]
    d4_ref[...] = gains[:, 32:40]


def row_places(row_lengths, spots):
    ends = jnp.cumsum(row_lengths)
    passed = spots[:, None] >= ends[None, :]
    return jnp.sum(jnp.where(passed, row_lengths[None, :], 0), axis=1)


def after(value, *others):
    return lax.optimization_barrier((value,) + others)[0]


def body(
    block_input,
    out_grad,
    lengths,
    w_query,
    w_key,
    w_value,
    w_out,
    w_gate,
    w_up,
    w_down,
    gain_query,
    gain_key,
    gain_attn,
    gain_mlp,
):
    core = lax.axis_index("c")
    z = lax.axis_index("z")
    peer = lax.axis_index("y") * 2 + lax.axis_index("xl")
    head = core * 4 + z
    my_x = block_input[0]

    columns = jnp.concatenate(
        [w_query.reshape(8, 8, 256), w_key.reshape(8, 8, 128), w_value.reshape(8, 8, 128)], axis=2
    )
    columns = columns.transpose(1, 0, 2).reshape(1, 2, 1, 1, 4, 8, 512)
    gains = jnp.concatenate([gain_query, gain_key, gain_attn, gain_mlp])
    gains = jnp.pad(gains[None, :], ((0, 7), (0, 88)))
    columns = jnp.concatenate(
        [columns, jnp.broadcast_to(gains, (1, 2, 1, 1, 4, 8, 128))], axis=-1
    )
    columns = jnp.broadcast_to(columns, (2, 2, 4, 2, 4, 8, 640)).reshape(128, 8, 640)
    columns = lax.all_to_all(columns, AXES, split_axis=0, concat_axis=0, tiled=False)
    gains = columns[:, 0, 512:552].astype(F32)
    w_head = columns.reshape(1024, 640)
    my_gains = lax.dynamic_slice_in_dim(gains, head * 16, 16, 0)
    gq, gk = my_gains[:, 0:16].reshape(1, 256), my_gains[:, 16:24].reshape(1, 128)

    ga, gm = gains[:, 24:32].reshape(1, 1024), gains[:, 32:40].reshape(1, 1024)

    def everywhere(a, shape):
        a = a.reshape(shape + (8, a.shape[-1]))
        return jnp.broadcast_to(a, (2, 2, 4, 2, 4, 8, a.shape[-1]))

    hidden = [w.reshape(8, 2, 3, 4, 128) for w in (w_gate, w_up, w_down.T)]
    hidden = jnp.concatenate(hidden, axis=-1).transpose(2, 1, 3, 0, 4)
    first = w_out.T.reshape(8, 2, 4, 256).transpose(1, 2, 0, 3)
    first = jnp.concatenate([first, hidden[0]], axis=-1)
    over_x = hidden[1].reshape(2, 2, 2, 8, 384).transpose(1, 0, 2, 3, 4)
    weights = jnp.concatenate(
        [
            everywhere(first, (1, 2, 1, 1, 4)),
            everywhere(over_x, (2, 2, 1, 2, 1)),
            everywhere(hidden[2], (1, 2, 4, 1, 1)),
        ],
        axis=-1,
    ).reshape(128, 8, 1408)
    weights = after(weights, w_head)
    weights = lax.all_to_all(weights, AXES, split_axis=0, concat_axis=0, tiled=False)
    weights = weights.reshape(1024, 1408)

    x_group = [my_x] + [shift(my_x, "z", by, False) for by in (1, -1, 2)]
    x_group = x_group + [swap(jnp.concatenate(x_group, axis=0))]
    x_own, x_other = my_x, x_group[4][:128]
    c_own = out_grad[0]
    c_other = swap(c_own)
    spots = jnp.stack([(z + n) % 4 for n in NEAR])

    q_pre, k_pre, v16, ss, ss_other = project_qkv(x_group, w_head)
    lengths = after(lengths, ss)

    my_lengths = lengths[0]
    other_lengths = swap(my_lengths)
    here = (peer * 4 + spots[:, None]) * 128 + jnp.arange(128, dtype=jnp.int32)[None, :]
    here = here.reshape(512)
    offset = jnp.concatenate(
        [here - row_places(my_lengths, here), here - row_places(other_lengths, here)]
    )
    frequency = THETA ** (-(jnp.arange(64, dtype=F32) * 2.0 / HD))
    angles = offset.astype(F32)[:, None] * frequency[None, :]
    cosine, sine = jnp.cos(angles), jnp.sin(angles)
    cos2 = jnp.concatenate([cosine, cosine], axis=1)
    sin2 = jnp.concatenate([-sine, sine], axis=1)

    task_lengths = jnp.where(peer // 4 == 0, my_lengths, other_lengths)
    task_spots = (
        jnp.arange(32, dtype=jnp.int32)[:, None, None] * 128
        + (peer % 4) * 32
        + jnp.arange(32, dtype=jnp.int32)[None, None, :]
    )
    task_spots = jnp.broadcast_to(task_spots, (32, 2, 32)).reshape(2048)
    starts = row_places(task_lengths, task_spots).reshape(4, 1, 512)
    task_spots = task_spots.reshape(4, 1, 512)
    tiles = 2 * jnp.arange(4, dtype=jnp.int32)
    low = jnp.minimum(jnp.min(starts, axis=(1, 2)) // 512, tiles)
    mid = jnp.clip((jnp.max(starts, axis=(1, 2)) + 511) // 512, low, tiles)

    packed, scales = pack_qkv(spots, q_pre, k_pre, v16, gq, gk, cos2, sin2, group_rows(ss, ss_other))
    z_spots = jnp.stack(ring_spots("z")).astype(jnp.int32)
    pinned = (packed, weights, low, mid, starts, task_spots, ga, gm, z_spots, x_other, c_other)
    pinned = lax.optimization_barrier(pinned)
    packed, weights, low, mid, starts, task_spots, ga, gm, z_spots, x_other, c_other = pinned
    received = lax.all_to_all(packed, ("y", "xl"), split_axis=0, concat_axis=0, tiled=False)
    chunks = jnp.split(weights, [640, 1024], axis=1)

    z_one = onward(chunks[0], "z")
    received, z_one, *chunks = lax.optimization_barrier((received.reshape(32, 320, HD), z_one, *chunks))
    z_two = onward(z_one, "z")
    near = [(onward(w, ring), shift(w, ring, -1, True)) for w, ring in zip(chunks[1:], "xy")]
    attn, acc, lse = attend(received, low, mid, starts, task_spots)
    ones, threes = zip(*near)
    attn, z_two, *near = lax.optimization_barrier((attn, z_two, *ones, *threes))
    ones, threes = near[:2], near[2:]
    attn = lax.all_to_all(attn, SEQ, split_axis=0, concat_axis=0, tiled=False)
    z_three = onward(z_two, "z")
    twos = [onward(one, ring) for one, ring in zip(ones, "xy")]
    attn, z_three, *twos = lax.optimization_barrier((attn, z_three, *twos))
    whole = [chunks[0], z_one, z_two, z_three]
    for own, one, two, three in zip(chunks[1:], ones, twos, threes):
        whole += [own, one, two, three]
    chunks = whole

    flat, half, vec = (256, 1024), (128, 1024), (1, 1024)
    wide, pairs = (12, 256, 128), (12, 256, 256)
    attn16, part = call(
        proj_kernel, [(flat, BF), (flat, BF)], (z_spots, attn, *chunks[:4]), 4
    )
    parts = (part, swap(part))
    mid16, gate, up, act16, down = call(
        forward_kernel,
        [(flat, BF), (wide, BF), (wide, BF), (wide, BF), (flat, BF)],
        (*parts, x_own, x_other, ga, *chunks),
        6,
    )
    output, dd16, d_both, d_mid, dg_mlp = call(
        backward_kernel,
        [(half, F32), (flat, BF), (pairs, BF), (flat, BF), (vec, F32)],
        (down, swap(down), *parts, x_own, c_own, c_other, ga, gm, gate, up, *chunks),
        7,
    )
    d_middle, dp16, d_attn, dg_attn = call(
        d_attn_kernel,
        [(half, F32), (flat, BF), ((32, 64, HD), BF), (vec, F32)],
        (z_spots, d_mid, swap(d_mid), *parts, c_own, c_other, ga, *chunks[:4]),
        3,
    )

    d_attn, d_both = lax.optimization_barrier((d_attn, d_both))
    d_attn = lax.all_to_all(d_attn, SEQ, split_axis=0, concat_axis=0, tiled=False)
    sources = (mid16, dd16, d_both, act16)
    grads = call(
        weight_grads_kernel,
        [((1024, 640), BF)] * 4 + [((1024, 384), BF)] * 8,
        (z_spots, *sources, dp16, attn16),
        6,
    )
    grads = (grads[:4], grads[4:8], grads[8:])
    runs = [onward(g[1], ring) for g, ring in zip(grads, RINGS)]
    d_attn, *runs = lax.optimization_barrier((d_attn, *runs))
    runs = [plus(g[2], run) for g, run in zip(grads, runs)]
    d_attn, *runs = lax.optimization_barrier((d_attn, *runs))
    runs = [onward(run, ring) for run, ring in zip(runs, RINGS)]

    d_pairs = attend_grad(received, d_attn, acc, lse, low, mid, starts, task_spots)
    d_pairs, *runs = lax.optimization_barrier((d_pairs, *runs))
    runs = [plus(g[3], run) for g, run in zip(grads, runs)]
    runs = [onward(run, ring) for run, ring in zip(runs, RINGS)]
    d_pairs = d_pairs.reshape(8, 4, 320, HD)
    d_pairs = lax.all_to_all(d_pairs, ("y", "xl"), split_axis=0, concat_axis=0, tiled=False)
    tq, tk, dv16, dots, dots_other, dgq, dgk = unpack_grads(
        spots, d_pairs, q_pre, k_pre, scales, gq, gk, cos2, sin2
    )
    shares = ring_end([g[0] for g in grads] + list(runs))
    sums, shares = lax.optimization_barrier((group_rows(dots, dots_other), shares))

    gain_grads = (dgq, dgk, dg_attn, dg_mlp)
    d_pre, shares = qkv_grads(
        head[None], tq, tk, dv16, q_pre, k_pre, scales, gain_grads, sums, x_group, shares
    )
    shares = lax.all_to_all(
        shares.reshape(128, 8, 2048), AXES, split_axis=0, concat_axis=0, tiled=False
    )
    d_x = dot_nt(d_pre, w_head[:, :512]).astype(BF)
    d_x = (d_x[:512].astype(F32) + swap(d_x[512:]).astype(F32)).astype(BF)
    widths = (2048, 1024, 1024, 2048, 3072, 3072, 3072)
    outs = [((8, w), F32) for w in widths] + [((1, w), F32) for w in (16, 8, 8, 8)]
    gq, gk, gv, go, gg, gu, gd, *dgains = call(finish_kernel, outs, (shares,), 3)
    d_middle = d_middle + d_x[:128].astype(F32)
    for n, by in enumerate((-1, 1, 2)):
        piece = shift(d_x[128 * (n + 1) : 128 * (n + 2)], "z", by, False)
        d_middle = d_middle + after(piece, gq).astype(F32)

    return (output[None], d_middle[None], gq, gk, gv, go.T, gg, gu, gd.T, *[d[0] for d in dgains])


def solution(mesh):
    cube_mesh = Mesh(mesh.devices.reshape(2, 2, 4, 2, 4), AXES)
    row, seq = ("xh", "c"), SEQ
    everything = row + seq
    tokens, rows, cols, vec = (
        P(row, seq, None),
        P(everything, None),
        P(None, everything),
        P(everything),
    )
    in_specs = (tokens, tokens, P(row, None), rows, rows, rows, cols, rows, rows, cols) + (vec,) * 4
    out_specs = (tokens, tokens, rows, rows, rows, cols, rows, rows, cols) + (vec,) * 4
    return jax.shard_map(body, mesh=cube_mesh, in_specs=in_specs, out_specs=out_specs, check_vma=False)
```

```python
import functools
import math

import jax
import jax.numpy as jnp
from jax import lax
from jax.experimental import pallas as pl
from jax.experimental.pallas import tpu as pltpu
from jax.sharding import Mesh, PartitionSpec as P

BF = jnp.bfloat16
F32 = jnp.float32
HD = 128
EPSILON = 1e-06
THETA = 500000.0
AXES = ("xh", "c", "y", "xl", "z")
SEQ = ("y", "xl", "z")
LOG2E = 1.4426950408889634
HIGHEST = lax.Precision.HIGHEST
COST = pl.CostEstimate(flops=1, bytes_accessed=1, transcendentals=0)


def swap(a):
    return lax.ppermute(a, "c", [(0, 1), (1, 0)])


def shift(a, ring, by, mirrored):
    axes = ("xh", "c", "xl") if ring == "x" else ("c", ring)

    def index(c, m):
        return (m // 2) * 4 + c * 2 + m % 2 if ring == "x" else c * 4 + m

    pairs = []
    for c in range(2):
        step = -by if (mirrored and c == 1) else by
        pairs += [(index(c, m), index(c, (m + step) % 4)) for m in range(4)]
    return lax.ppermute(a, axes, pairs)


def position(ring):
    if ring == "x":
        return lax.axis_index("xh") * 2 + lax.axis_index("xl")
    return lax.axis_index(ring)


def params(arrays, scratch=0):
    total = scratch + sum(math.prod(a.shape) * jnp.dtype(a.dtype).itemsize for a in arrays)
    return pltpu.CompilerParams(vmem_limit_bytes=total + total // 8 + (3 << 20))


VSPEC = pl.BlockSpec(memory_space=pltpu.VMEM)
SSPEC = pl.BlockSpec(memory_space=pltpu.SMEM)
HSPEC = pl.BlockSpec(memory_space=pltpu.HBM)


RINGS = ("z", "x", "y")


def ring_spots(ring):
    here, sign = position(ring), 1 - 2 * lax.axis_index("c")
    return [(here - sign * n) % 4 for n in range(4)]


def onward(block, ring):
    return shift(block, ring, 1, True)


def plus(a, b):
    return (a.astype(F32) + b.astype(F32)).astype(BF)


NEAR = (0, 3, 1, 2)


def turn_pair(turn):
    left = lax.broadcasted_iota(jnp.int32, turn.shape, 1) < 64
    other = pltpu.roll(turn, 64, 1)
    return jnp.where(left, turn, other), jnp.where(left, -other, turn)


def rope_forward(v, cos, sin):
    return v * cos + pltpu.roll(v, 64, 1) * sin


def rope_backward(d, cos, sin):
    return d * cos - pltpu.roll(d, 64, 1) * sin


def lane_sums(a):
    ones = jnp.ones((8, a.shape[1]), F32)
    rows = lax.dot_general(
        ones, a, (((1,), (1,)), ((), ())), precision=HIGHEST, preferred_element_type=F32
    )
    return rows[0:1]


def store_sums(own_ref, other_ref, n, q_sum, k_sum):
    own_ref[n : n + 1, :] = q_sum
    own_ref[8 + n : 9 + n, :] = k_sum
    m = (n + 4) % 8
    other_ref[m : m + 1, :] = q_sum
    other_ref[8 + m : 9 + m, :] = k_sum


def column(row):
    return jnp.broadcast_to(row, (128, 128)).T


def group_rows(part, for_other):
    total = part + swap(for_other)
    return [total] + [shift(total, "z", by, False) for by in (1, -1, 2)]


def group_total(refs, n):
    first, k = n // 4 * 4, n % 4
    total = refs[0][n : n + 1, :]
    for ref, by in zip(refs[1:], (1, -1, 2)):
        at = first + NEAR.index((NEAR[k] + by) % 4)
        total += ref[at : at + 1, :]
    return total


def qkv_kernel(w_ref, *refs):
    xs, (q_ref, k_ref, v_ref, ss_ref, sso_ref) = refs[:5], refs[5:]
    for n in range(8):
        rows = pl.ds(128 * n, 128)
        x = xs[n][...] if n < 4 else xs[4][128 * (n - 4) : 128 * (n - 3), :]
        pre = jnp.dot(x, w_ref[:, :512], preferred_element_type=F32)
        q, k = pre[:, :256], pre[:, 256:384]
        q_ref[rows, :] = q
        k_ref[rows, :] = k
        v_ref[rows, :] = pre[:, 384:].astype(BF)
        store_sums(ss_ref, sso_ref, n, lane_sums(q * q), lane_sums(k * k))


def project_qkv(x, w):
    args = (w, *x)
    outs = [
            jax.ShapeDtypeStruct((1024, 256), F32),
            jax.ShapeDtypeStruct((1024, 128), F32),
            jax.ShapeDtypeStruct((1024, 128), BF),
            jax.ShapeDtypeStruct((16, 128), F32),
        jax.ShapeDtypeStruct((16, 128), F32),
        ]
    return pl.pallas_call(
        qkv_kernel,
        out_shape=outs,
        in_specs=[VSPEC] * 6,
        out_specs=[VSPEC] * 5,
        compiler_params=params((*args, *outs), 0),
        cost_estimate=COST,
    )(*args)


def send_kernel(
    spot_ref, q_ref, k_ref, v_ref, gq_ref, gk_ref, turn_ref, s0_ref, s1_ref, s2_ref, s3_ref, out_ref, scale_ref
):
    sums = (s0_ref, s1_ref, s2_ref, s3_ref)
    for n in range(16):
        width = 2048 if n < 8 else 1024
        mean = group_total(sums, n) * (1.0 / width)
        scale_ref[n : n + 1, :] = lax.rsqrt(mean + EPSILON)
    for n in range(8):
        r, spot = n // 4, spot_ref[n % 4]
        rows = pl.ds(128 * n, 128)
        cos, sin = turn_pair(turn_ref[rows, :])
        rq, rk = column(scale_ref[n : n + 1, :]), column(scale_ref[8 + n : 9 + n, :])
        for g in range(2):
            cols = pl.ds(g * HD, HD)
            q = rope_forward(q_ref[rows, cols] * rq * gq_ref[:, cols], cos, sin).astype(BF)
            for j in range(4):
                out_ref[r * 4 + j, spot, g * 32 : (g + 1) * 32, :] = q[32 * j : 32 * j + 32]
        k = rope_forward(k_ref[rows, :] * rk * gk_ref[...], cos, sin).astype(BF)
        v = v_ref[rows, :]
        for j in range(4):
            out_ref[r * 4 + j, spot, 64:192, :] = k
            out_ref[r * 4 + j, spot, 192:320, :] = v


def pack_qkv(spots, q_pre, k_pre, v16, gq, gk, turns, sums):
    args = (spots, q_pre, k_pre, v16, gq, gk, turns, *sums)
    outs = [
        jax.ShapeDtypeStruct((8, 4, 320, HD), BF),
        jax.ShapeDtypeStruct((16, 128), F32),
    ]
    return pl.pallas_call(
        send_kernel,
        out_shape=outs,
        in_specs=[SSPEC] + [VSPEC] * 10,
        out_specs=[VSPEC] * 2,
        compiler_params=params((*args, *outs)),
        cost_estimate=COST,
    )(*args)


def grouped(first, last, step, carry):
    for size in (2, 1):
        count = (last - first) // size

        def body(n, c, size=size, first=first):
            return step([first + size * n + m for m in range(size)], c)

        carry = lax.fori_loop(0, count, body, carry)
        first = first + size * count
    return carry


def tile_keys(ref, kt, tiles, first, last):
    return ref[pl.ds(4 * kt, 4 * tiles), first:last, :].reshape(512 * tiles, HD)


def tile_mask(kt, starts, spots, tiles=1):
    keys = kt * 512 + lax.broadcasted_iota(jnp.int32, (512 * tiles, 512), 0)
    return (keys >= starts) & (keys <= spots)


def attend_kernel(scale2, low_ref, mid_ref, r_ref, start_ref, spot_ref, out_ref, acc_ref, lse_ref, vt_ref):
    for b in range(32):
        vt_ref[:, b * 128 : (b + 1) * 128] = r_ref[b, 192:320, :].T

    def tile(i, _):
        q = r_ref[pl.ds(8 * i, 8), 0:64, :].reshape(512, HD)
        starts, spots = start_ref[i], spot_ref[i]

        def step(masked, kts, carry):
            top, total, acc = carry
            tiles = []
            for kt in kts:
                k = r_ref[pl.ds(4 * kt, 4), 64:192, :].reshape(512, HD)
                s = lax.dot_general(k, q, (((1,), (1,)), ((), ())), preferred_element_type=F32)
                s = s * scale2
                tiles.append(jnp.where(tile_mask(kt, starts, spots), s, -1e30) if masked else s)
            new_top = top
            for s in tiles:
                new_top = jnp.maximum(new_top, jnp.max(s, axis=0, keepdims=True))
            fade = jnp.exp2(top - new_top)
            total, acc = total * fade, acc * fade
            for kt, s in zip(kts, tiles):
                p = jnp.exp2(s - new_top)
                total += jnp.sum(p, axis=0, keepdims=True)
                vt = vt_ref[:, pl.ds(pl.multiple_of(kt * 512, 512), 512)]
                acc += jnp.dot(vt, p.astype(BF), preferred_element_type=F32)
            return new_top, total, acc

        carry = (
            jnp.full((1, 512), -1e30, F32),
            jnp.zeros((1, 512), F32),
            jnp.zeros((HD, 512), F32),
        )
        first = mid_ref[i]
        carry = lax.fori_loop(low_ref[i], first, lambda kt, c: step(True, (kt,), c), carry)
        carry = grouped(first, 2 * i, functools.partial(step, False), carry)
        top, total, acc = step(True, (2 * i, 2 * i + 1), carry)
        acc = acc / total
        acc_ref[i] = acc
        lse_ref[i] = top + jnp.log2(total)
        out_ref[pl.ds(8 * i, 8)] = acc.T.astype(BF).reshape(8, 64, HD)
        return 0

    lax.fori_loop(0, 4, tile, 0)


def attend(received, low, mid, starts, spots):
    args = (low, mid, received, starts, spots,)
    outs = [
            jax.ShapeDtypeStruct((32, 64, HD), BF),
            jax.ShapeDtypeStruct((4, HD, 512), F32),
            jax.ShapeDtypeStruct((4, 1, 512), F32),
        ]
    return pl.pallas_call(
        functools.partial(attend_kernel, LOG2E / math.sqrt(HD)),
        out_shape=outs,
        in_specs=[SSPEC] * 2 + [VSPEC] * 3,
        out_specs=[VSPEC] * 3,
        scratch_shapes=[pltpu.VMEM((HD, 4096), BF)],
        compiler_params=params((*args, *outs), 1 << 20),
        cost_estimate=COST,
    )(*args)


def attend_grad_kernel(
    scale2, scale, low_ref, mid_ref, r_ref, do_ref, acc_ref, lse_ref, start_ref, spot_ref, out_ref, kt_ref, dk_ref, dv_ref
):
    for b in range(32):
        kt_ref[:, b * 128 : (b + 1) * 128] = r_ref[b, 64:192, :].T

    def tile(i, _):
        q = r_ref[pl.ds(8 * i, 8), 0:64, :].reshape(512, HD)
        do = do_ref[pl.ds(8 * i, 8)].reshape(512, HD)
        delta = jnp.sum(do.astype(F32).T * acc_ref[i], axis=0, keepdims=True)
        lse, starts, spots = lse_ref[i], start_ref[i], spot_ref[i]

        def step(masked, tiles, kt, dq):
            k = tile_keys(r_ref, kt, tiles, 64, 192)
            v = tile_keys(r_ref, kt, tiles, 192, 320)
            s = lax.dot_general(k, q, (((1,), (1,)), ((), ())), preferred_element_type=F32)
            e = s * scale2 - lse
            if masked:
                e = jnp.where(tile_mask(kt, starts, spots, tiles), e, -1e30)
            p = jnp.exp2(e)
            dp = lax.dot_general(v, do, (((1,), (1,)), ((), ())), preferred_element_type=F32)
            ds = (p * (dp - delta)).astype(BF)
            keys = pl.ds(pl.multiple_of(kt * 512, 512), 512 * tiles)
            dv = jnp.dot(p.astype(BF), do, preferred_element_type=F32)
            dk = jnp.dot(ds, q, preferred_element_type=F32)
            if masked and tiles == 2:
                dv_ref[keys, :] = dv
                dk_ref[keys, :] = dk
            else:
                dv_ref[keys, :] += dv
                dk_ref[keys, :] += dk
            return dq + jnp.dot(kt_ref[:, keys], ds, preferred_element_type=F32)

        dq = jnp.zeros((HD, 512), F32)
        first, last = mid_ref[i], 2 * i
        pairs = (last - first) // 2
        dq = lax.fori_loop(low_ref[i], first, functools.partial(step, True, 1), dq)
        dq = lax.fori_loop(0, pairs, lambda n, c: step(False, 2, first + 2 * n, c), dq)
        dq = lax.fori_loop(first + 2 * pairs, last, functools.partial(step, False, 1), dq)
        dq = step(True, 2, last, dq)
        out_ref[pl.ds(8 * i, 8), 0:64, :] = (dq * scale).T.astype(BF).reshape(8, 64, HD)
        return 0

    lax.fori_loop(0, 4, tile, 0)
    for b in range(32):
        out_ref[b, 64:192, :] = (dk_ref[b * 128 : (b + 1) * 128, :] * scale).astype(BF)
        out_ref[b, 192:320, :] = dv_ref[b * 128 : (b + 1) * 128, :].astype(BF)


def attend_grad(received, d_attn, acc, lse, low, mid, starts, spots):
    args = (low, mid, received, d_attn, acc, lse, starts, spots,)
    outs = [jax.ShapeDtypeStruct((32, 320, HD), BF)]
    return pl.pallas_call(
        functools.partial(attend_grad_kernel, LOG2E / math.sqrt(HD), 1.0 / math.sqrt(HD)),
        out_shape=outs[0],
        in_specs=[SSPEC] * 2 + [VSPEC] * 6,
        out_specs=VSPEC,
        scratch_shapes=[
            pltpu.VMEM((HD, 4096), BF),
            pltpu.VMEM((4096, HD), F32),
            pltpu.VMEM((4096, HD), F32),
        ],
        compiler_params=params((*args, *outs), 22 << 20),
        cost_estimate=COST,
    )(*args)


def unpack_kernel(
    spot_ref, d_ref, q_ref, k_ref, scale_ref, gq_ref, gk_ref, turn_ref, tq_ref, tk_ref, dv_ref, dot_ref, doto_ref, dgq_ref, dgk_ref
):
    for n in range(8):
        r, spot = n // 4, spot_ref[n % 4]
        rows = pl.ds(128 * n, 128)
        cos, sin = turn_pair(turn_ref[rows, :])
        rq, rk = column(scale_ref[n : n + 1, :]), column(scale_ref[8 + n : 9 + n, :])
        dot_q = jnp.zeros((128, HD), F32)
        for g in range(2):
            cols = pl.ds(g * HD, HD)
            d = jnp.concatenate(
                [d_ref[r * 4 + j, spot, g * 32 : (g + 1) * 32, :] for j in range(4)], axis=0
            ).astype(F32)
            d = rope_backward(d, cos, sin)
            q = q_ref[rows, cols]
            t = d * gq_ref[:, cols]
            tq_ref[rows, cols] = t
            dot_q += t * q
            part = jnp.sum(d * q * rq, axis=0, keepdims=True)
            dgq_ref[:, cols] = part if n == 0 else dgq_ref[:, cols] + part
        dk = d_ref[r * 4, spot, 64:192, :].astype(F32)
        dv = d_ref[r * 4, spot, 192:320, :].astype(F32)
        for j in range(1, 4):
            dk += d_ref[r * 4 + j, spot, 64:192, :].astype(F32)
            dv += d_ref[r * 4 + j, spot, 192:320, :].astype(F32)
        dv_ref[rows, :] = dv.astype(BF)
        d = rope_backward(dk, cos, sin)
        k = k_ref[rows, :]
        t = d * gk_ref[...]
        tk_ref[rows, :] = t
        part = jnp.sum(d * k * rk, axis=0, keepdims=True)
        dgk_ref[...] = part if n == 0 else dgk_ref[...] + part
        store_sums(dot_ref, doto_ref, n, lane_sums(dot_q), lane_sums(t * k))


def unpack_grads(spots, d, q_pre, k_pre, scales, gq, gk, turns):
    args = (spots, d, q_pre, k_pre, scales, gq, gk, turns,)
    outs = [
            jax.ShapeDtypeStruct((1024, 256), F32),
            jax.ShapeDtypeStruct((1024, 128), F32),
            jax.ShapeDtypeStruct((1024, 128), BF),
            jax.ShapeDtypeStruct((16, 128), F32),
        jax.ShapeDtypeStruct((16, 128), F32),
            jax.ShapeDtypeStruct((1, 256), F32),
            jax.ShapeDtypeStruct((1, 128), F32),
        ]
    return pl.pallas_call(
        unpack_kernel,
        out_shape=outs,
        in_specs=[SSPEC] + [VSPEC] * 7,
        out_specs=[VSPEC] * 7,
        compiler_params=params((*args, *outs), 0),
        cost_estimate=COST,
    )(*args)


def spread(row, each, first, group, rows_of):
    count = row.shape[1]
    i = lax.broadcasted_iota(jnp.int32, (128, count), 0)
    c = lax.broadcasted_iota(jnp.int32, (128, count), 1)
    here = c // each == i - group * rows_of
    left = jnp.where(here, jnp.broadcast_to(row, (128, count)), 0.0)
    c = lax.broadcasted_iota(jnp.int32, (count, 128), 0)
    lane = lax.broadcasted_iota(jnp.int32, (count, 128), 1)
    right = (lane == first + c % each).astype(F32)
    return jnp.dot(left, right, precision=HIGHEST, preferred_element_type=F32)


def qkv_grad_kernel(
    head_ref, tq_ref, tk_ref, dv_ref, q_ref, k_ref, scale_ref, dgq_ref, dgk_ref, dga_ref, dgm_ref, *refs
):
    sums, xs, (d_ref, shares_ref, out_ref, sem) = refs[:4], refs[4:9], refs[10:]
    for n in range(8):
        rows = pl.ds(128 * n, 128)
        rq, rk = column(scale_ref[n : n + 1, :]), column(scale_ref[8 + n : 9 + n, :])
        eq = rq * rq * rq * column(group_total(sums, n)) * (1.0 / 2048)
        ek = rk * rk * rk * column(group_total(sums, 8 + n)) * (1.0 / 1024)
        for g in range(2):
            cols = pl.ds(g * HD, HD)
            d_ref[rows, cols] = (rq * tq_ref[rows, cols] - eq * q_ref[rows, cols]).astype(BF)
        d_ref[rows, 256:384] = (rk * tk_ref[rows, :] - ek * k_ref[rows, :]).astype(BF)
        d_ref[rows, 384:512] = dv_ref[rows, :]
    for n in range(4):
        rows = pl.ds(256 * n, 256)
        x = jnp.concatenate([x_ref[:, rows] for x_ref in xs], axis=0)
        out_ref[rows, 0:512] = dot_tn(x, d_ref[...]).astype(BF)
    head = head_ref[0]
    gains = spread(dgq_ref[...], 16, 0, head, 16) + spread(dgk_ref[...], 8, 16, head, 16)
    gains += spread(dga_ref[...], 8, 24, 0, 0) + spread(dgm_ref[...], 8, 32, 0, 0)
    coarse = gains.astype(BF).astype(F32)
    both = coarse + pltpu.roll(gains - coarse, 64, 1)
    r = lax.broadcasted_iota(jnp.int32, (1024, 128), 0)
    i = lax.broadcasted_iota(jnp.int32, (1024, 128), 1)
    out_ref[:, 512:640] = dot_nn((r == 8 * i).astype(BF), both.astype(BF)).astype(BF)
    copy = pltpu.make_async_copy(out_ref, shares_ref.at[:, 0:640], sem)
    copy.start()
    copy.wait()


def qkv_grads(head, tq, tk, dv16, q_pre, k_pre, scales, gain_grads, sums, x, shares):
    args = (head, tq, tk, dv16, q_pre, k_pre, scales, *gain_grads, *sums, *x, shares)
    outs = [
        jax.ShapeDtypeStruct((1024, 512), BF),
        jax.ShapeDtypeStruct((1024, 2048), BF),
    ]
    return pl.pallas_call(
        qkv_grad_kernel,
        out_shape=outs,
        in_specs=[SSPEC] + [VSPEC] * (len(args) - 2) + [HSPEC],
        out_specs=[VSPEC, HSPEC],
        scratch_shapes=[pltpu.VMEM((1024, 640), BF), pltpu.SemaphoreType.DMA],
        input_output_aliases={len(args) - 1: 1},
        compiler_params=params(args[:-1] + (outs[0],), 6 << 20),
        cost_estimate=COST,
    )(*args)


def ring_end_kernel(*refs):
    terms, (shares_ref, total_ref, sems) = refs[:6], refs[6:]
    copies, at = [], 0
    for n, (own_ref, run_ref) in enumerate(zip(terms[:3], terms[3:])):
        width = own_ref.shape[1]
        total = own_ref[...].astype(F32) + run_ref[...].astype(F32)
        total_ref[:, at : at + width] = total.astype(BF)
        target = shares_ref.at[:, 640 + at : 640 + at + width]
        copies.append(pltpu.make_async_copy(total_ref.at[:, at : at + width], target, sems.at[n]))
        copies[-1].start()
        at += width
    for copy in copies:
        copy.wait()


def ring_end(terms):
    out = jax.ShapeDtypeStruct((1024, 2048), BF)
    return pl.pallas_call(
        ring_end_kernel,
        out_shape=out,
        in_specs=[VSPEC] * 6,
        out_specs=HSPEC,
        scratch_shapes=[pltpu.VMEM((1024, 1408), BF), pltpu.SemaphoreType.DMA((3,))],
        compiler_params=params(terms, 3 << 20),
        cost_estimate=COST,
    )(*terms)


def dot_nn(a, b):
    return lax.dot_general(a, b, (((1,), (0,)), ((), ())), preferred_element_type=F32)


def dot_nt(a, b):
    return lax.dot_general(a, b, (((1,), (1,)), ((), ())), preferred_element_type=F32)


def dot_tn(a, b):
    return lax.dot_general(a, b, (((0,), (0,)), ((), ())), preferred_element_type=F32)


def rms_rate(v):
    return lax.rsqrt(jnp.mean(v * v, axis=-1, keepdims=True) + EPSILON)


def rms_back(v, g, d):
    r = rms_rate(v)
    t = d * g
    dv = r * t - v * (r * r * r * jnp.mean(t * v, axis=-1, keepdims=True))
    return dv, d * v * r


def call(kernel, out_shape, args, us):
    args = (*args,)
    outs = [jax.ShapeDtypeStruct(s, t) for s, t in out_shape]
    return pl.pallas_call(
        kernel,
        out_shape=outs,
        in_specs=[SSPEC if a.ndim == 1 else VSPEC for a in args],
        out_specs=[VSPEC] * len(out_shape),
        compiler_params=params((*args, *outs), 0),
        cost_estimate=COST,
    )(*args)


def both_cores(part_ref, got_ref):
    got = jnp.concatenate([got_ref[128:256, :], got_ref[0:128, :]], axis=0)
    return part_ref[...].astype(F32) + got.astype(F32)


def proj_kernel(spot_ref, a_ref, *refs):
    chunks, (attn_ref, part_ref) = refs[:4], refs[4:]
    for r in range(2):
        for j in range(4):
            rows = pl.ds(r * 128 + j * 32, 32)
            for h in range(4):
                for g in range(2):
                    piece = a_ref[(r * 4 + j) * 4 + h, g * 32 : (g + 1) * 32, :]
                    attn_ref[rows, (h * 2 + g) * HD : (h * 2 + g + 1) * HD] = piece
    lefts = [
        attn_ref[:, pl.ds(pl.multiple_of(spot_ref[n] * 256, 256), 256)] for n in range(4)
    ]
    for m in range(4):
        cols = pl.ds(256 * m, 256)
        part = dot_nt(lefts[0], chunks[0][cols, 0:256])
        for n in range(1, 4):
            part += dot_nt(lefts[n], chunks[n][cols, 0:256])
        part_ref[:, cols] = part.astype(BF)


def hidden_columns(n):
    return 256 if n < 4 else 0


def forward_kernel(part_ref, got_ref, xo_ref, xt_ref, g_ref, *refs):
    chunks, (mid_ref, gate_ref, up_ref, act_ref, down_ref) = refs[:12], refs[12:]
    proj = both_cores(part_ref, got_ref)
    x = jnp.concatenate([xo_ref[...], xt_ref[...]], axis=0).astype(F32)
    m = (x + proj * rms_rate(proj) * g_ref[...]).astype(BF)
    mid_ref[...] = m
    for n, w_ref in enumerate(chunks):
        at = hidden_columns(n)
        both = dot_nn(m, w_ref[:, at : at + 256])
        gate, up = both[:, :128], both[:, 128:]
        gate_ref[n] = gate.astype(BF)
        up_ref[n] = up.astype(BF)
        act_ref[n] = (gate / (1.0 + jnp.exp(-gate)) * up).astype(BF)
    for k in range(4):
        cols = pl.ds(256 * k, 256)
        part = jnp.zeros((256, 256), F32)
        for n, w_ref in enumerate(chunks):
            at = hidden_columns(n) + 256
            part += dot_nt(act_ref[n], w_ref[cols, at : at + 128])
        down_ref[:, cols] = part.astype(BF)


def backward_kernel(
    down_ref, downg_ref, part_ref, got_ref, xo_ref, co_ref, ct_ref, ga_ref, gm_ref, gate_ref, up_ref, *refs
):
    chunks, (out_ref, dd_ref, dboth_ref, dmid_ref, dg_ref) = refs[:12], refs[12:]
    down = both_cores(down_ref, downg_ref)
    gm = gm_ref[...]
    proj = both_cores(part_ref, got_ref)[:128]
    middle = xo_ref[...].astype(F32) + proj * rms_rate(proj) * ga_ref[...]
    out_ref[...] = middle + down[:128] * rms_rate(down[:128]) * gm
    c = jnp.concatenate([co_ref[...], ct_ref[...]], axis=0).astype(F32)
    dd, terms = rms_back(down, gm, c)
    dg_ref[...] = jnp.sum(terms[:128], axis=0, keepdims=True)
    dd = dd.astype(BF)
    dd_ref[...] = dd
    for n, w_ref in enumerate(chunks):
        at = hidden_columns(n)
        d_act = dot_nn(dd, w_ref[:, at + 256 : at + 384])
        gate, up = gate_ref[n].astype(F32), up_ref[n].astype(F32)
        sig = 1.0 / (1.0 + jnp.exp(-gate))
        dboth_ref[n, :, 0:128] = (d_act * up * sig * (1.0 + gate * (1.0 - sig))).astype(BF)
        dboth_ref[n, :, 128:256] = (d_act * gate * sig).astype(BF)
    for k in range(4):
        cols = pl.ds(256 * k, 256)
        part = jnp.zeros((256, 256), F32)
        for n, w_ref in enumerate(chunks):
            at = hidden_columns(n)
            part += dot_nt(dboth_ref[n], w_ref[cols, at : at + 256])
        dmid_ref[:, cols] = part.astype(BF)


def d_attn_kernel(spot_ref, dmid_ref, dmidg_ref, part_ref, got_ref, co_ref, ct_ref, ga_ref, *refs):
    chunks, (dm_ref, dp_ref, out_ref, dg_ref) = refs[:4], refs[4:]
    c = jnp.concatenate([co_ref[...], ct_ref[...]], axis=0).astype(F32)
    d_middle = c + both_cores(dmid_ref, dmidg_ref)
    dm_ref[...] = d_middle[:128]
    dp, terms = rms_back(both_cores(part_ref, got_ref), ga_ref[...], d_middle)
    dg_ref[...] = jnp.sum(terms[:128], axis=0, keepdims=True)
    dp = dp.astype(BF)
    dp_ref[...] = dp
    for n in range(4):
        part = dot_nn(dp, chunks[n][:, 0:256]).astype(BF)
        for r in range(2):
            for j in range(4):
                for g in range(2):
                    piece = part[r * 128 + j * 32 : r * 128 + (j + 1) * 32, g * HD : (g + 1) * HD]
                    out_ref[(r * 4 + j) * 4 + spot_ref[n], g * 32 : (g + 1) * 32, :] = piece


def hidden_grads_kernel(first, m_ref, dd_ref, dboth_ref, act_ref, *outs):
    for n, out_ref in enumerate(outs):
        at = hidden_columns(first + n)
        out_ref[:, at : at + 256] = dot_tn(m_ref[...], dboth_ref[first + n]).astype(BF)
        out_ref[:, at + 256 : at + 384] = dot_tn(dd_ref[...], act_ref[first + n]).astype(BF)


def weight_grads_kernel(spot_ref, m_ref, dd_ref, dboth_ref, act_ref, dp_ref, attn_ref, *outs):
    hidden_grads_kernel(0, m_ref, dd_ref, dboth_ref, act_ref, *outs)
    for n in range(4):
        right = attn_ref[:, pl.ds(pl.multiple_of(spot_ref[n] * 256, 256), 256)]
        outs[n][:, 0:256] = dot_tn(dp_ref[...], right).astype(BF)


def finish_kernel(s_ref, gq_ref, gk_ref, gv_ref, go_ref, gg_ref, gu_ref, gd_ref, d1_ref, d2_ref, d3_ref, d4_ref):
    def total(sources, first, last):
        part = s_ref[sources[0], :, first:last].astype(F32)
        for i in sources[1:]:
            part += s_ref[i, :, first:last].astype(F32)
        return part

    def store_hidden(part, c, first):
        cols = pl.ds(c * 1536 + first, 128)
        for n, ref in enumerate((gg_ref, gu_ref, gd_ref)):
            ref[:, cols] = part[:, 128 * n : 128 * (n + 1)]

    def device(x, c, y, z):
        return (x // 2) * 64 + c * 32 + y * 8 + (x % 2) * 4 + z

    four = range(4)
    gains = jnp.zeros((1, 128), F32)
    for c in range(2):
        for m in four:
            part = total([device(x, c, y, m) for x in four for y in four], 0, 1280)
            e = c * 4 + m
            gq_ref[:, e * 256 : (e + 1) * 256] = part[:, 0:256]
            gk_ref[:, e * 128 : (e + 1) * 128] = part[:, 256:384]
            gv_ref[:, e * 128 : (e + 1) * 128] = part[:, 384:512]
            gains += part[0:1, 512:640]
            go_ref[:, e * 256 : (e + 1) * 256] = part[:, 640:896]
            store_hidden(part[:, 896:1280], c, m * 128)
            part = total([device(m, c, y, z) for y in four for z in four], 1280, 1664)
            store_hidden(part, c, 512 + m * 128)
            part = total([device(x, c, m, z) for x in four for z in four], 1664, 2048)
            store_hidden(part, c, 1024 + m * 128)
    gains = jnp.broadcast_to(gains, (8, 128))
    gains = (gains + pltpu.roll(gains, 64, 1))[0:1]
    d1_ref[...] = gains[:, 0:16]
    d2_ref[...] = gains[:, 16:24]
    d3_ref[...] = gains[:, 24:32]
    d4_ref[...] = gains[:, 32:40]


def row_places(row_lengths, spots):
    ends = jnp.cumsum(row_lengths)
    passed = spots[:, None] >= ends[None, :]
    return jnp.sum(jnp.where(passed, row_lengths[None, :], 0), axis=1)


def after(value, *others):
    return lax.optimization_barrier((value,) + others)[0]


def body(
    block_input,
    out_grad,
    lengths,
    w_query,
    w_key,
    w_value,
    w_out,
    w_gate,
    w_up,
    w_down,
    gain_query,
    gain_key,
    gain_attn,
    gain_mlp,
):
    core = lax.axis_index("c")
    z = lax.axis_index("z")
    peer = lax.axis_index("y") * 2 + lax.axis_index("xl")
    head = core * 4 + z
    my_x = block_input[0]

    columns = jnp.concatenate(
        [w_query.reshape(8, 8, 256), w_key.reshape(8, 8, 128), w_value.reshape(8, 8, 128)], axis=2
    )
    columns = columns.transpose(1, 0, 2).reshape(1, 2, 1, 1, 4, 8, 512)
    gains = jnp.concatenate([gain_query, gain_key, gain_attn, gain_mlp])
    gains = jnp.pad(gains[None, :], ((0, 7), (0, 88)))
    columns = jnp.concatenate(
        [columns, jnp.broadcast_to(gains, (1, 2, 1, 1, 4, 8, 128))], axis=-1
    )
    columns = jnp.broadcast_to(columns, (2, 2, 4, 2, 4, 8, 640)).reshape(128, 8, 640)
    columns = lax.all_to_all(columns, AXES, split_axis=0, concat_axis=0, tiled=False)
    gains = columns[:, 0, 512:552].astype(F32)
    w_head = columns.reshape(1024, 640)
    my_gains = lax.dynamic_slice_in_dim(gains, head * 16, 16, 0)
    gq, gk = my_gains[:, 0:16].reshape(1, 256), my_gains[:, 16:24].reshape(1, 128)

    ga, gm = gains[:, 24:32].reshape(1, 1024), gains[:, 32:40].reshape(1, 1024)

    def everywhere(a, shape):
        a = a.reshape(shape + (8, a.shape[-1]))
        return jnp.broadcast_to(a, (2, 2, 4, 2, 4, 8, a.shape[-1]))

    hidden = [w.reshape(8, 2, 3, 4, 128) for w in (w_gate, w_up, w_down.T)]
    hidden = jnp.concatenate(hidden, axis=-1).transpose(2, 1, 3, 0, 4)
    first = w_out.T.reshape(8, 2, 4, 256).transpose(1, 2, 0, 3)
    first = jnp.concatenate([first, hidden[0]], axis=-1)
    over_x = hidden[1].reshape(2, 2, 2, 8, 384).transpose(1, 0, 2, 3, 4)
    weights = jnp.concatenate(
        [
            everywhere(first, (1, 2, 1, 1, 4)),
            everywhere(over_x, (2, 2, 1, 2, 1)),
            everywhere(hidden[2], (1, 2, 4, 1, 1)),
        ],
        axis=-1,
    ).reshape(128, 8, 1408)
    weights = after(weights, w_head)
    weights = lax.all_to_all(weights, AXES, split_axis=0, concat_axis=0, tiled=False)
    weights = weights.reshape(1024, 1408)

    x_group = [my_x] + [shift(my_x, "z", by, False) for by in (1, -1, 2)]
    x_group = x_group + [swap(jnp.concatenate(x_group, axis=0))]
    x_own, x_other = my_x, x_group[4][:128]
    c_own = out_grad[0]
    c_other = swap(c_own)
    spots = jnp.stack([(z + n) % 4 for n in NEAR])

    q_pre, k_pre, v16, ss, ss_other = project_qkv(x_group, w_head)
    lengths = after(lengths, ss)

    my_lengths = lengths[0]
    other_lengths = swap(my_lengths)
    here = (peer * 4 + spots[:, None]) * 128 + jnp.arange(128, dtype=jnp.int32)[None, :]
    here = here.reshape(512)
    offset = jnp.concatenate(
        [here - row_places(my_lengths, here), here - row_places(other_lengths, here)]
    )
    frequency = THETA ** (-(jnp.arange(64, dtype=F32) * 2.0 / HD))
    angles = offset.astype(F32)[:, None] * frequency[None, :]
    cosine, sine = jnp.cos(angles), jnp.sin(angles)
    turns = jnp.concatenate([cosine, sine], axis=1)

    task_lengths = jnp.where(peer // 4 == 0, my_lengths, other_lengths)
    task_spots = (
        jnp.arange(32, dtype=jnp.int32)[:, None, None] * 128
        + (peer % 4) * 32
        + jnp.arange(32, dtype=jnp.int32)[None, None, :]
    )
    task_spots = jnp.broadcast_to(task_spots, (32, 2, 32)).reshape(2048)
    starts = row_places(task_lengths, task_spots).reshape(4, 1, 512)
    task_spots = task_spots.reshape(4, 1, 512)
    tiles = 2 * jnp.arange(4, dtype=jnp.int32)
    low = jnp.minimum(jnp.min(starts, axis=(1, 2)) // 512, tiles)
    mid = jnp.clip((jnp.max(starts, axis=(1, 2)) + 511) // 512, low, tiles)

    packed, scales = pack_qkv(spots, q_pre, k_pre, v16, gq, gk, turns, group_rows(ss, ss_other))
    z_spots = jnp.stack(ring_spots("z")).astype(jnp.int32)
    pinned = (packed, weights, low, mid, starts, task_spots, ga, gm, z_spots, x_other, c_other)
    pinned = lax.optimization_barrier(pinned)
    packed, weights, low, mid, starts, task_spots, ga, gm, z_spots, x_other, c_other = pinned
    received = lax.all_to_all(packed, ("y", "xl"), split_axis=0, concat_axis=0, tiled=False)
    chunks = jnp.split(weights, [640, 1024], axis=1)

    z_one = onward(chunks[0], "z")
    received, z_one, *chunks = lax.optimization_barrier((received.reshape(32, 320, HD), z_one, *chunks))
    z_two = onward(z_one, "z")
    near = [(onward(w, ring), shift(w, ring, -1, True)) for w, ring in zip(chunks[1:], "xy")]
    attn, acc, lse = attend(received, low, mid, starts, task_spots)
    ones, threes = zip(*near)
    attn, z_two, *near = lax.optimization_barrier((attn, z_two, *ones, *threes))
    ones, threes = near[:2], near[2:]
    attn = lax.all_to_all(attn, SEQ, split_axis=0, concat_axis=0, tiled=False)
    z_three = onward(z_two, "z")
    twos = [onward(one, ring) for one, ring in zip(ones, "xy")]
    attn, z_three, *twos = lax.optimization_barrier((attn, z_three, *twos))
    whole = [chunks[0], z_one, z_two, z_three]
    for own, one, two, three in zip(chunks[1:], ones, twos, threes):
        whole += [own, one, two, three]
    chunks = whole

    flat, half, vec = (256, 1024), (128, 1024), (1, 1024)
    wide, pairs = (12, 256, 128), (12, 256, 256)
    attn16, part = call(
        proj_kernel, [(flat, BF), (flat, BF)], (z_spots, attn, *chunks[:4]), 4
    )
    parts = (part, swap(part))
    mid16, gate, up, act16, down = call(
        forward_kernel,
        [(flat, BF), (wide, BF), (wide, BF), (wide, BF), (flat, BF)],
        (*parts, x_own, x_other, ga, *chunks),
        6,
    )
    output, dd16, d_both, d_mid, dg_mlp = call(
        backward_kernel,
        [(half, F32), (flat, BF), (pairs, BF), (flat, BF), (vec, F32)],
        (down, swap(down), *parts, x_own, c_own, c_other, ga, gm, gate, up, *chunks),
        7,
    )
    d_middle, dp16, d_attn, dg_attn = call(
        d_attn_kernel,
        [(half, F32), (flat, BF), ((32, 64, HD), BF), (vec, F32)],
        (z_spots, d_mid, swap(d_mid), *parts, c_own, c_other, ga, *chunks[:4]),
        3,
    )

    d_attn, d_both = lax.optimization_barrier((d_attn, d_both))
    d_attn = lax.all_to_all(d_attn, SEQ, split_axis=0, concat_axis=0, tiled=False)
    sources = (mid16, dd16, d_both, act16)
    grads = call(
        weight_grads_kernel,
        [((1024, 640), BF)] * 4 + [((1024, 384), BF)] * 8,
        (z_spots, *sources, dp16, attn16),
        6,
    )
    grads = (grads[:4], grads[4:8], grads[8:])
    runs = [onward(g[1], ring) for g, ring in zip(grads, RINGS)]
    d_attn, *runs = lax.optimization_barrier((d_attn, *runs))
    runs = [plus(g[2], run) for g, run in zip(grads, runs)]
    d_attn, *runs = lax.optimization_barrier((d_attn, *runs))
    runs = [onward(run, ring) for run, ring in zip(runs, RINGS)]

    d_pairs = attend_grad(received, d_attn, acc, lse, low, mid, starts, task_spots)
    d_pairs, *runs = lax.optimization_barrier((d_pairs, *runs))
    runs = [plus(g[3], run) for g, run in zip(grads, runs)]
    runs = [onward(run, ring) for run, ring in zip(runs, RINGS)]
    d_pairs = d_pairs.reshape(8, 4, 320, HD)
    d_pairs = lax.all_to_all(d_pairs, ("y", "xl"), split_axis=0, concat_axis=0, tiled=False)
    tq, tk, dv16, dots, dots_other, dgq, dgk = unpack_grads(
        spots, d_pairs, q_pre, k_pre, scales, gq, gk, turns
    )
    shares = ring_end([g[0] for g in grads] + list(runs))
    sums, shares = lax.optimization_barrier((group_rows(dots, dots_other), shares))

    gain_grads = (dgq, dgk, dg_attn, dg_mlp)
    d_pre, shares = qkv_grads(
        head[None], tq, tk, dv16, q_pre, k_pre, scales, gain_grads, sums, x_group, shares
    )
    shares = lax.all_to_all(
        shares.reshape(128, 8, 2048), AXES, split_axis=0, concat_axis=0, tiled=False
    )
    d_x = dot_nt(d_pre, w_head[:, :512]).astype(BF)
    d_x = (d_x[:512].astype(F32) + swap(d_x[512:]).astype(F32)).astype(BF)
    widths = (2048, 1024, 1024, 2048, 3072, 3072, 3072)
    outs = [((8, w), F32) for w in widths] + [((1, w), F32) for w in (16, 8, 8, 8)]
    gq, gk, gv, go, gg, gu, gd, *dgains = call(finish_kernel, outs, (shares,), 3)
    d_middle = d_middle + d_x[:128].astype(F32)
    for n, by in enumerate((-1, 1, 2)):
        piece = shift(d_x[128 * (n + 1) : 128 * (n + 2)], "z", by, False)
        d_middle = d_middle + after(piece, gq).astype(F32)

    return (output[None], d_middle[None], gq, gk, gv, go.T, gg, gu, gd.T, *[d[0] for d in dgains])


def solution(mesh):
    cube_mesh = Mesh(mesh.devices.reshape(2, 2, 4, 2, 4), AXES)
    row, seq = ("xh", "c"), SEQ
    everything = row + seq
    tokens, rows, cols, vec = (
        P(row, seq, None),
        P(everything, None),
        P(None, everything),
        P(everything),
    )
    in_specs = (tokens, tokens, P(row, None), rows, rows, rows, cols, rows, rows, cols) + (vec,) * 4
    out_specs = (tokens, tokens, rows, rows, rows, cols, rows, rows, cols) + (vec,) * 4
    return jax.shard_map(body, mesh=cube_mesh, in_specs=in_specs, out_specs=out_specs, check_vma=False)
```

```python
import functools
import math

import jax
import jax.numpy as jnp
from jax import lax
from jax.experimental import pallas as pl
from jax.experimental.pallas import tpu as pltpu
from jax.sharding import Mesh, PartitionSpec as P

BF = jnp.bfloat16
F32 = jnp.float32
HD = 128
EPSILON = 1e-06
THETA = 500000.0
AXES = ("xh", "c", "y", "xl", "z")
SEQ = ("y", "xl", "z")
LOG2E = 1.4426950408889634
HIGHEST = lax.Precision.HIGHEST
COST = pl.CostEstimate(flops=1, bytes_accessed=1, transcendentals=0)


def swap(a):
    return lax.ppermute(a, "c", [(0, 1), (1, 0)])


def shift(a, ring, by, mirrored):
    axes = ("xh", "c", "xl") if ring == "x" else ("c", ring)

    def index(c, m):
        return (m // 2) * 4 + c * 2 + m % 2 if ring == "x" else c * 4 + m

    pairs = []
    for c in range(2):
        step = -by if (mirrored and c == 1) else by
        pairs += [(index(c, m), index(c, (m + step) % 4)) for m in range(4)]
    return lax.ppermute(a, axes, pairs)


def position(ring):
    if ring == "x":
        return lax.axis_index("xh") * 2 + lax.axis_index("xl")
    return lax.axis_index(ring)


def params(arrays, scratch=0):
    total = scratch + sum(math.prod(a.shape) * jnp.dtype(a.dtype).itemsize for a in arrays)
    return pltpu.CompilerParams(vmem_limit_bytes=total + total // 8 + (3 << 20))


VSPEC = pl.BlockSpec(memory_space=pltpu.VMEM)
SSPEC = pl.BlockSpec(memory_space=pltpu.SMEM)
HSPEC = pl.BlockSpec(memory_space=pltpu.HBM)


RINGS = ("z", "x", "y")


def ring_spots(ring):
    here, sign = position(ring), 1 - 2 * lax.axis_index("c")
    return [(here - sign * n) % 4 for n in range(4)]


def onward(block, ring):
    return shift(block, ring, 1, True)


def plus(a, b):
    return (a.astype(F32) + b.astype(F32)).astype(BF)


NEAR = (0, 3, 1, 2)


def rope_forward(v, cos, sin):
    return v * cos + pltpu.roll(v, 64, 1) * sin


def rope_backward(d, cos, sin):
    return d * cos - pltpu.roll(d, 64, 1) * sin


def lane_sums(a):
    ones = jnp.ones((8, a.shape[1]), F32)
    rows = lax.dot_general(
        ones, a, (((1,), (1,)), ((), ())), precision=HIGHEST, preferred_element_type=F32
    )
    return rows[0:1]


def store_sums(own_ref, other_ref, n, q_sum, k_sum):
    own_ref[n : n + 1, :] = q_sum
    own_ref[8 + n : 9 + n, :] = k_sum
    m = (n + 4) % 8
    other_ref[m : m + 1, :] = q_sum
    other_ref[8 + m : 9 + m, :] = k_sum


def column(row):
    return jnp.broadcast_to(row, (128, 128)).T


def group_rows(part, for_other):
    total = part + swap(for_other)
    return [total] + [shift(total, "z", by, False) for by in (1, -1, 2)]


def group_total(refs, n):
    first, k = n // 4 * 4, n % 4
    total = refs[0][n : n + 1, :]
    for ref, by in zip(refs[1:], (1, -1, 2)):
        at = first + NEAR.index((NEAR[k] + by) % 4)
        total += ref[at : at + 1, :]
    return total


def qkv_kernel(w_ref, *refs):
    xs, (q_ref, k_ref, v_ref, ss_ref, sso_ref) = refs[:5], refs[5:]
    for n in range(8):
        rows = pl.ds(128 * n, 128)
        x = xs[n][...] if n < 4 else xs[4][128 * (n - 4) : 128 * (n - 3), :]
        pre = jnp.dot(x, w_ref[:, :512], preferred_element_type=F32)
        q, k = pre[:, :256], pre[:, 256:384]
        q_ref[rows, :] = q
        k_ref[rows, :] = k
        v_ref[rows, :] = pre[:, 384:].astype(BF)
        store_sums(ss_ref, sso_ref, n, lane_sums(q * q), lane_sums(k * k))


def project_qkv(x, w):
    args = (w, *x)
    outs = [
            jax.ShapeDtypeStruct((1024, 256), F32),
            jax.ShapeDtypeStruct((1024, 128), F32),
            jax.ShapeDtypeStruct((1024, 128), BF),
            jax.ShapeDtypeStruct((16, 128), F32),
        jax.ShapeDtypeStruct((16, 128), F32),
        ]
    return pl.pallas_call(
        qkv_kernel,
        out_shape=outs,
        in_specs=[VSPEC] * 6,
        out_specs=[VSPEC] * 5,
        compiler_params=params((*args, *outs), 0),
        cost_estimate=COST,
    )(*args)


def send_kernel(
    spot_ref, q_ref, k_ref, v_ref, gq_ref, gk_ref, cos_ref, sin_ref, s0_ref, s1_ref, s2_ref, s3_ref, out_ref, scale_ref
):
    sums = (s0_ref, s1_ref, s2_ref, s3_ref)
    for n in range(16):
        width = 2048 if n < 8 else 1024
        mean = group_total(sums, n) * (1.0 / width)
        scale_ref[n : n + 1, :] = lax.rsqrt(mean + EPSILON)
    for n in range(8):
        r, spot = n // 4, spot_ref[n % 4]
        rows = pl.ds(128 * n, 128)
        cos, sin = cos_ref[rows, :], sin_ref[rows, :]
        rq, rk = column(scale_ref[n : n + 1, :]), column(scale_ref[8 + n : 9 + n, :])
        for g in range(2):
            cols = pl.ds(g * HD, HD)
            q = rope_forward(q_ref[rows, cols] * rq * gq_ref[:, cols], cos, sin).astype(BF)
            for j in range(4):
                out_ref[r * 4 + j, spot, g * 32 : (g + 1) * 32, :] = q[32 * j : 32 * j + 32]
        k = rope_forward(k_ref[rows, :] * rk * gk_ref[...], cos, sin).astype(BF)
        v = v_ref[rows, :]
        for j in range(4):
            out_ref[r * 4 + j, spot, 64:192, :] = k
            out_ref[r * 4 + j, spot, 192:320, :] = v


def pack_qkv(spots, q_pre, k_pre, v16, gq, gk, cos, sin, sums):
    args = (spots, q_pre, k_pre, v16, gq, gk, cos, sin, *sums)
    outs = [
        jax.ShapeDtypeStruct((8, 4, 320, HD), BF),
        jax.ShapeDtypeStruct((16, 128), F32),
    ]
    return pl.pallas_call(
        send_kernel,
        out_shape=outs,
        in_specs=[SSPEC] + [VSPEC] * 11,
        out_specs=[VSPEC] * 2,
        compiler_params=params((*args, *outs)),
        cost_estimate=COST,
    )(*args)


def tile_keys(ref, kt, tiles, first, last):
    return ref[pl.ds(4 * kt, 4 * tiles), first:last, :].reshape(512 * tiles, HD)


def tile_mask(kt, tiles, starts, spots):
    keys = kt * 512 + lax.broadcasted_iota(jnp.int32, (512 * tiles, 512), 0)
    return (keys >= starts) & (keys <= spots)


def attend_kernel(scale2, low_ref, mid_ref, r_ref, start_ref, spot_ref, out_ref, acc_ref, lse_ref, vt_ref):
    for b in range(32):
        vt_ref[:, b * 128 : (b + 1) * 128] = r_ref[b, 192:320, :].T

    def tile(i, _):
        q = r_ref[pl.ds(8 * i, 8), 0:64, :].reshape(512, HD)
        starts, spots = start_ref[i], spot_ref[i]

        def step(masked, tiles, kt, carry):
            top, total, acc = carry
            k = tile_keys(r_ref, kt, tiles, 64, 192)
            s = lax.dot_general(k, q, (((1,), (1,)), ((), ())), preferred_element_type=F32)
            s = s * scale2
            if masked:
                s = jnp.where(tile_mask(kt, tiles, starts, spots), s, -1e30)
            new_top = jnp.maximum(top, jnp.max(s, axis=0, keepdims=True))
            fade = jnp.exp2(top - new_top)
            p = jnp.exp2(s - new_top)
            total = total * fade + jnp.sum(p, axis=0, keepdims=True)
            vt = vt_ref[:, pl.ds(pl.multiple_of(kt * 512, 512), 512 * tiles)]
            acc = acc * fade + jnp.dot(vt, p.astype(BF), preferred_element_type=F32)
            return new_top, total, acc

        carry = (
            jnp.full((1, 512), -1e30, F32),
            jnp.zeros((1, 512), F32),
            jnp.zeros((HD, 512), F32),
        )
        first, last = mid_ref[i], 2 * i
        pairs = (last - first) // 2
        carry = lax.fori_loop(low_ref[i], first, functools.partial(step, True, 1), carry)
        carry = lax.fori_loop(
            0, pairs, lambda n, c: step(False, 2, first + 2 * n, c), carry
        )
        carry = lax.fori_loop(first + 2 * pairs, last, functools.partial(step, False, 1), carry)
        top, total, acc = step(True, 2, last, carry)
        acc = acc / total
        acc_ref[i] = acc
        lse_ref[i] = top + jnp.log2(total)
        out_ref[pl.ds(8 * i, 8)] = acc.T.astype(BF).reshape(8, 64, HD)
        return 0

    lax.fori_loop(0, 4, tile, 0)


def attend(received, low, mid, starts, spots):
    args = (low, mid, received, starts, spots,)
    outs = [
            jax.ShapeDtypeStruct((32, 64, HD), BF),
            jax.ShapeDtypeStruct((4, HD, 512), F32),
            jax.ShapeDtypeStruct((4, 1, 512), F32),
        ]
    return pl.pallas_call(
        functools.partial(attend_kernel, LOG2E / math.sqrt(HD)),
        out_shape=outs,
        in_specs=[SSPEC] * 2 + [VSPEC] * 3,
        out_specs=[VSPEC] * 3,
        scratch_shapes=[pltpu.VMEM((HD, 4096), BF)],
        compiler_params=params((*args, *outs), 12 << 20),
        cost_estimate=COST,
    )(*args)


def attend_grad_kernel(
    scale2, scale, low_ref, mid_ref, r_ref, do_ref, acc_ref, lse_ref, start_ref, spot_ref, out_ref, kt_ref, dk_ref, dv_ref
):
    for b in range(32):
        kt_ref[:, b * 128 : (b + 1) * 128] = r_ref[b, 64:192, :].T

    def tile(i, _):
        q = r_ref[pl.ds(8 * i, 8), 0:64, :].reshape(512, HD)
        do = do_ref[pl.ds(8 * i, 8)].reshape(512, HD)
        delta = jnp.sum(do.astype(F32).T * acc_ref[i], axis=0, keepdims=True)
        lse, starts, spots = lse_ref[i], start_ref[i], spot_ref[i]

        def step(masked, tiles, kt, dq):
            k = tile_keys(r_ref, kt, tiles, 64, 192)
            v = tile_keys(r_ref, kt, tiles, 192, 320)
            s = lax.dot_general(k, q, (((1,), (1,)), ((), ())), preferred_element_type=F32)
            e = s * scale2 - lse
            if masked:
                e = jnp.where(tile_mask(kt, tiles, starts, spots), e, -1e30)
            p = jnp.exp2(e)
            dp = lax.dot_general(v, do, (((1,), (1,)), ((), ())), preferred_element_type=F32)
            ds = (p * (dp - delta)).astype(BF)
            keys = pl.ds(pl.multiple_of(kt * 512, 512), 512 * tiles)
            dv = jnp.dot(p.astype(BF), do, preferred_element_type=F32)
            dk = jnp.dot(ds, q, preferred_element_type=F32)
            if masked and tiles == 2:
                dv_ref[keys, :] = dv
                dk_ref[keys, :] = dk
            else:
                dv_ref[keys, :] += dv
                dk_ref[keys, :] += dk
            return dq + jnp.dot(kt_ref[:, keys], ds, preferred_element_type=F32)

        dq = jnp.zeros((HD, 512), F32)
        first, last = mid_ref[i], 2 * i
        pairs = (last - first) // 2
        dq = lax.fori_loop(low_ref[i], first, functools.partial(step, True, 1), dq)
        dq = lax.fori_loop(0, pairs, lambda n, c: step(False, 2, first + 2 * n, c), dq)
        dq = lax.fori_loop(first + 2 * pairs, last, functools.partial(step, False, 1), dq)
        dq = step(True, 2, last, dq)
        out_ref[pl.ds(8 * i, 8), 0:64, :] = (dq * scale).T.astype(BF).reshape(8, 64, HD)
        return 0

    lax.fori_loop(0, 4, tile, 0)
    for b in range(32):
        out_ref[b, 64:192, :] = (dk_ref[b * 128 : (b + 1) * 128, :] * scale).astype(BF)
        out_ref[b, 192:320, :] = dv_ref[b * 128 : (b + 1) * 128, :].astype(BF)


def attend_grad(received, d_attn, acc, lse, low, mid, starts, spots):
    args = (low, mid, received, d_attn, acc, lse, starts, spots,)
    outs = [jax.ShapeDtypeStruct((32, 320, HD), BF)]
    return pl.pallas_call(
        functools.partial(attend_grad_kernel, LOG2E / math.sqrt(HD), 1.0 / math.sqrt(HD)),
        out_shape=outs[0],
        in_specs=[SSPEC] * 2 + [VSPEC] * 6,
        out_specs=VSPEC,
        scratch_shapes=[
            pltpu.VMEM((HD, 4096), BF),
            pltpu.VMEM((4096, HD), F32),
            pltpu.VMEM((4096, HD), F32),
        ],
        compiler_params=params((*args, *outs), 22 << 20),
        cost_estimate=COST,
    )(*args)


def unpack_kernel(
    spot_ref, d_ref, q_ref, k_ref, scale_ref, gq_ref, gk_ref, cos_ref, sin_ref, tq_ref, tk_ref, dv_ref, dot_ref, doto_ref, dgq_ref, dgk_ref
):
    for n in range(8):
        r, spot = n // 4, spot_ref[n % 4]
        rows = pl.ds(128 * n, 128)
        cos, sin = cos_ref[rows, :], sin_ref[rows, :]
        rq, rk = column(scale_ref[n : n + 1, :]), column(scale_ref[8 + n : 9 + n, :])
        dot_q = jnp.zeros((128, HD), F32)
        for g in range(2):
            cols = pl.ds(g * HD, HD)
            d = jnp.concatenate(
                [d_ref[r * 4 + j, spot, g * 32 : (g + 1) * 32, :] for j in range(4)], axis=0
            ).astype(F32)
            d = rope_backward(d, cos, sin)
            q = q_ref[rows, cols]
            t = d * gq_ref[:, cols]
            tq_ref[rows, cols] = t
            dot_q += t * q
            part = jnp.sum(d * q * rq, axis=0, keepdims=True)
            dgq_ref[:, cols] = part if n == 0 else dgq_ref[:, cols] + part
        dk = d_ref[r * 4, spot, 64:192, :].astype(F32)
        dv = d_ref[r * 4, spot, 192:320, :].astype(F32)
        for j in range(1, 4):
            dk += d_ref[r * 4 + j, spot, 64:192, :].astype(F32)
            dv += d_ref[r * 4 + j, spot, 192:320, :].astype(F32)
        dv_ref[rows, :] = dv.astype(BF)
        d = rope_backward(dk, cos, sin)
        k = k_ref[rows, :]
        t = d * gk_ref[...]
        tk_ref[rows, :] = t
        part = jnp.sum(d * k * rk, axis=0, keepdims=True)
        dgk_ref[...] = part if n == 0 else dgk_ref[...] + part
        store_sums(dot_ref, doto_ref, n, lane_sums(dot_q), lane_sums(t * k))


def unpack_grads(spots, d, q_pre, k_pre, scales, gq, gk, cos, sin):
    args = (spots, d, q_pre, k_pre, scales, gq, gk, cos, sin,)
    outs = [
            jax.ShapeDtypeStruct((1024, 256), F32),
            jax.ShapeDtypeStruct((1024, 128), F32),
            jax.ShapeDtypeStruct((1024, 128), BF),
            jax.ShapeDtypeStruct((16, 128), F32),
        jax.ShapeDtypeStruct((16, 128), F32),
            jax.ShapeDtypeStruct((1, 256), F32),
            jax.ShapeDtypeStruct((1, 128), F32),
        ]
    return pl.pallas_call(
        unpack_kernel,
        out_shape=outs,
        in_specs=[SSPEC] + [VSPEC] * 8,
        out_specs=[VSPEC] * 7,
        compiler_params=params((*args, *outs), 0),
        cost_estimate=COST,
    )(*args)


def spread(row, each, first, group, rows_of):
    count = row.shape[1]
    i = lax.broadcasted_iota(jnp.int32, (128, count), 0)
    c = lax.broadcasted_iota(jnp.int32, (128, count), 1)
    here = c // each == i - group * rows_of
    left = jnp.where(here, jnp.broadcast_to(row, (128, count)), 0.0)
    c = lax.broadcasted_iota(jnp.int32, (count, 128), 0)
    lane = lax.broadcasted_iota(jnp.int32, (count, 128), 1)
    right = (lane == first + c % each).astype(F32)
    return jnp.dot(left, right, precision=HIGHEST, preferred_element_type=F32)


def qkv_grad_kernel(
    head_ref, tq_ref, tk_ref, dv_ref, q_ref, k_ref, scale_ref, dgq_ref, dgk_ref, dga_ref, dgm_ref, *refs
):
    sums, xs, (d_ref, shares_ref, out_ref, sem) = refs[:4], refs[4:9], refs[10:]
    for n in range(8):
        rows = pl.ds(128 * n, 128)
        rq, rk = column(scale_ref[n : n + 1, :]), column(scale_ref[8 + n : 9 + n, :])
        eq = rq * rq * rq * column(group_total(sums, n)) * (1.0 / 2048)
        ek = rk * rk * rk * column(group_total(sums, 8 + n)) * (1.0 / 1024)
        for g in range(2):
            cols = pl.ds(g * HD, HD)
            d_ref[rows, cols] = (rq * tq_ref[rows, cols] - eq * q_ref[rows, cols]).astype(BF)
        d_ref[rows, 256:384] = (rk * tk_ref[rows, :] - ek * k_ref[rows, :]).astype(BF)
        d_ref[rows, 384:512] = dv_ref[rows, :]
    for n in range(4):
        rows = pl.ds(256 * n, 256)
        x = jnp.concatenate([x_ref[:, rows] for x_ref in xs], axis=0)
        out_ref[rows, 0:512] = dot_tn(x, d_ref[...]).astype(BF)
    head = head_ref[0]
    gains = spread(dgq_ref[...], 16, 0, head, 16) + spread(dgk_ref[...], 8, 16, head, 16)
    gains += spread(dga_ref[...], 8, 24, 0, 0) + spread(dgm_ref[...], 8, 32, 0, 0)
    coarse = gains.astype(BF).astype(F32)
    both = coarse + pltpu.roll(gains - coarse, 64, 1)
    r = lax.broadcasted_iota(jnp.int32, (1024, 128), 0)
    i = lax.broadcasted_iota(jnp.int32, (1024, 128), 1)
    out_ref[:, 512:640] = dot_nn((r == 8 * i).astype(BF), both.astype(BF)).astype(BF)
    copy = pltpu.make_async_copy(out_ref, shares_ref.at[:, 0:640], sem)
    copy.start()
    copy.wait()


def qkv_grads(head, tq, tk, dv16, q_pre, k_pre, scales, gain_grads, sums, x, shares):
    args = (head, tq, tk, dv16, q_pre, k_pre, scales, *gain_grads, *sums, *x, shares)
    outs = [
        jax.ShapeDtypeStruct((1024, 512), BF),
        jax.ShapeDtypeStruct((1024, 2048), BF),
    ]
    return pl.pallas_call(
        qkv_grad_kernel,
        out_shape=outs,
        in_specs=[SSPEC] + [VSPEC] * (len(args) - 2) + [HSPEC],
        out_specs=[VSPEC, HSPEC],
        scratch_shapes=[pltpu.VMEM((1024, 640), BF), pltpu.SemaphoreType.DMA],
        input_output_aliases={len(args) - 1: 1},
        compiler_params=params(args[:-1] + (outs[0],), 6 << 20),
        cost_estimate=COST,
    )(*args)


def ring_end_kernel(*refs):
    terms, (shares_ref, total_ref, sems) = refs[:6], refs[6:]
    copies, at = [], 0
    for n, (own_ref, run_ref) in enumerate(zip(terms[:3], terms[3:])):
        width = own_ref.shape[1]
        total = own_ref[...].astype(F32) + run_ref[...].astype(F32)
        total_ref[:, at : at + width] = total.astype(BF)
        target = shares_ref.at[:, 640 + at : 640 + at + width]
        copies.append(pltpu.make_async_copy(total_ref.at[:, at : at + width], target, sems.at[n]))
        copies[-1].start()
        at += width
    for copy in copies:
        copy.wait()


def ring_end(terms):
    out = jax.ShapeDtypeStruct((1024, 2048), BF)
    return pl.pallas_call(
        ring_end_kernel,
        out_shape=out,
        in_specs=[VSPEC] * 6,
        out_specs=HSPEC,
        scratch_shapes=[pltpu.VMEM((1024, 1408), BF), pltpu.SemaphoreType.DMA((3,))],
        compiler_params=params(terms, 3 << 20),
        cost_estimate=COST,
    )(*terms)


def dot_nn(a, b):
    return lax.dot_general(a, b, (((1,), (0,)), ((), ())), preferred_element_type=F32)


def dot_nt(a, b):
    return lax.dot_general(a, b, (((1,), (1,)), ((), ())), preferred_element_type=F32)


def dot_tn(a, b):
    return lax.dot_general(a, b, (((0,), (0,)), ((), ())), preferred_element_type=F32)


def rms_rate(v):
    return lax.rsqrt(jnp.mean(v * v, axis=-1, keepdims=True) + EPSILON)


def rms_back(v, g, d):
    r = rms_rate(v)
    t = d * g
    dv = r * t - v * (r * r * r * jnp.mean(t * v, axis=-1, keepdims=True))
    return dv, d * v * r


def call(kernel, out_shape, args, us):
    args = (*args,)
    outs = [jax.ShapeDtypeStruct(s, t) for s, t in out_shape]
    return pl.pallas_call(
        kernel,
        out_shape=outs,
        in_specs=[SSPEC if a.ndim == 1 else VSPEC for a in args],
        out_specs=[VSPEC] * len(out_shape),
        compiler_params=params((*args, *outs), 0),
        cost_estimate=COST,
    )(*args)


def both_cores(part_ref, got_ref):
    got = jnp.concatenate([got_ref[128:256, :], got_ref[0:128, :]], axis=0)
    return part_ref[...].astype(F32) + got.astype(F32)


def proj_kernel(spot_ref, a_ref, *refs):
    chunks, (attn_ref, part_ref) = refs[:4], refs[4:]
    for r in range(2):
        for j in range(4):
            rows = pl.ds(r * 128 + j * 32, 32)
            for h in range(4):
                for g in range(2):
                    piece = a_ref[(r * 4 + j) * 4 + h, g * 32 : (g + 1) * 32, :]
                    attn_ref[rows, (h * 2 + g) * HD : (h * 2 + g + 1) * HD] = piece
    lefts = [
        attn_ref[:, pl.ds(pl.multiple_of(spot_ref[n] * 256, 256), 256)] for n in range(4)
    ]
    for m in range(4):
        cols = pl.ds(256 * m, 256)
        part = dot_nt(lefts[0], chunks[0][cols, 0:256])
        for n in range(1, 4):
            part += dot_nt(lefts[n], chunks[n][cols, 0:256])
        part_ref[:, cols] = part.astype(BF)


def hidden_columns(n):
    return 256 if n < 4 else 0


def forward_kernel(part_ref, got_ref, xo_ref, xt_ref, g_ref, *refs):
    chunks, (mid_ref, gate_ref, up_ref, act_ref, down_ref) = refs[:12], refs[12:]
    proj = both_cores(part_ref, got_ref)
    x = jnp.concatenate([xo_ref[...], xt_ref[...]], axis=0).astype(F32)
    m = (x + proj * rms_rate(proj) * g_ref[...]).astype(BF)
    mid_ref[...] = m
    for n, w_ref in enumerate(chunks):
        at = hidden_columns(n)
        both = dot_nn(m, w_ref[:, at : at + 256])
        gate, up = both[:, :128], both[:, 128:]
        gate_ref[n] = gate.astype(BF)
        up_ref[n] = up.astype(BF)
        act_ref[n] = (gate / (1.0 + jnp.exp(-gate)) * up).astype(BF)
    for k in range(4):
        cols = pl.ds(256 * k, 256)
        part = jnp.zeros((256, 256), F32)
        for n, w_ref in enumerate(chunks):
            at = hidden_columns(n) + 256
            part += dot_nt(act_ref[n], w_ref[cols, at : at + 128])
        down_ref[:, cols] = part.astype(BF)


def backward_kernel(
    down_ref, downg_ref, part_ref, got_ref, xo_ref, co_ref, ct_ref, ga_ref, gm_ref, gate_ref, up_ref, *refs
):
    chunks, (out_ref, dd_ref, dboth_ref, dmid_ref, dg_ref) = refs[:12], refs[12:]
    down = both_cores(down_ref, downg_ref)
    gm = gm_ref[...]
    proj = both_cores(part_ref, got_ref)[:128]
    middle = xo_ref[...].astype(F32) + proj * rms_rate(proj) * ga_ref[...]
    out_ref[...] = middle + down[:128] * rms_rate(down[:128]) * gm
    c = jnp.concatenate([co_ref[...], ct_ref[...]], axis=0).astype(F32)
    dd, terms = rms_back(down, gm, c)
    dg_ref[...] = jnp.sum(terms[:128], axis=0, keepdims=True)
    dd = dd.astype(BF)
    dd_ref[...] = dd
    for n, w_ref in enumerate(chunks):
        at = hidden_columns(n)
        d_act = dot_nn(dd, w_ref[:, at + 256 : at + 384])
        gate, up = gate_ref[n].astype(F32), up_ref[n].astype(F32)
        sig = 1.0 / (1.0 + jnp.exp(-gate))
        dboth_ref[n, :, 0:128] = (d_act * up * sig * (1.0 + gate * (1.0 - sig))).astype(BF)
        dboth_ref[n, :, 128:256] = (d_act * gate * sig).astype(BF)
    for k in range(4):
        cols = pl.ds(256 * k, 256)
        part = jnp.zeros((256, 256), F32)
        for n, w_ref in enumerate(chunks):
            at = hidden_columns(n)
            part += dot_nt(dboth_ref[n], w_ref[cols, at : at + 256])
        dmid_ref[:, cols] = part.astype(BF)


def d_attn_kernel(spot_ref, dmid_ref, dmidg_ref, part_ref, got_ref, co_ref, ct_ref, ga_ref, *refs):
    chunks, (dm_ref, dp_ref, out_ref, dg_ref) = refs[:4], refs[4:]
    c = jnp.concatenate([co_ref[...], ct_ref[...]], axis=0).astype(F32)
    d_middle = c + both_cores(dmid_ref, dmidg_ref)
    dm_ref[...] = d_middle[:128]
    dp, terms = rms_back(both_cores(part_ref, got_ref), ga_ref[...], d_middle)
    dg_ref[...] = jnp.sum(terms[:128], axis=0, keepdims=True)
    dp = dp.astype(BF)
    dp_ref[...] = dp
    for n in range(4):
        part = dot_nn(dp, chunks[n][:, 0:256]).astype(BF)
        for r in range(2):
            for j in range(4):
                for g in range(2):
                    piece = part[r * 128 + j * 32 : r * 128 + (j + 1) * 32, g * HD : (g + 1) * HD]
                    out_ref[(r * 4 + j) * 4 + spot_ref[n], g * 32 : (g + 1) * 32, :] = piece


def hidden_grads_kernel(first, m_ref, dd_ref, dboth_ref, act_ref, *outs):
    for n, out_ref in enumerate(outs):
        at = hidden_columns(first + n)
        out_ref[:, at : at + 256] = dot_tn(m_ref[...], dboth_ref[first + n]).astype(BF)
        out_ref[:, at + 256 : at + 384] = dot_tn(dd_ref[...], act_ref[first + n]).astype(BF)


def weight_grads_kernel(spot_ref, m_ref, dd_ref, dboth_ref, act_ref, dp_ref, attn_ref, *outs):
    hidden_grads_kernel(0, m_ref, dd_ref, dboth_ref, act_ref, *outs)
    for n in range(4):
        right = attn_ref[:, pl.ds(pl.multiple_of(spot_ref[n] * 256, 256), 256)]
        outs[n][:, 0:256] = dot_tn(dp_ref[...], right).astype(BF)


def finish_kernel(s_ref, gq_ref, gk_ref, gv_ref, go_ref, gg_ref, gu_ref, gd_ref, d1_ref, d2_ref, d3_ref, d4_ref):
    def total(sources, first, last):
        part = s_ref[sources[0], :, first:last].astype(F32)
        for i in sources[1:]:
            part += s_ref[i, :, first:last].astype(F32)
        return part

    def store_hidden(part, c, first):
        cols = pl.ds(c * 1536 + first, 128)
        for n, ref in enumerate((gg_ref, gu_ref, gd_ref)):
            ref[:, cols] = part[:, 128 * n : 128 * (n + 1)]

    def device(x, c, y, z):
        return (x // 2) * 64 + c * 32 + y * 8 + (x % 2) * 4 + z

    four = range(4)
    gains = jnp.zeros((1, 128), F32)
    for c in range(2):
        for m in four:
            part = total([device(x, c, y, m) for x in four for y in four], 0, 1280)
            e = c * 4 + m
            gq_ref[:, e * 256 : (e + 1) * 256] = part[:, 0:256]
            gk_ref[:, e * 128 : (e + 1) * 128] = part[:, 256:384]
            gv_ref[:, e * 128 : (e + 1) * 128] = part[:, 384:512]
            gains += part[0:1, 512:640]
            go_ref[:, e * 256 : (e + 1) * 256] = part[:, 640:896]
            store_hidden(part[:, 896:1280], c, m * 128)
            part = total([device(m, c, y, z) for y in four for z in four], 1280, 1664)
            store_hidden(part, c, 512 + m * 128)
            part = total([device(x, c, m, z) for x in four for z in four], 1664, 2048)
            store_hidden(part, c, 1024 + m * 128)
    gains = jnp.broadcast_to(gains, (8, 128))
    gains = (gains + pltpu.roll(gains, 64, 1))[0:1]
    d1_ref[...] = gains[:, 0:16]
    d2_ref[...] = gains[:, 16:24]
    d3_ref[...] = gains[:, 24:32]
    d4_ref[...] = gains[:, 32:40]


def row_places(row_lengths, spots):
    ends = jnp.cumsum(row_lengths)
    passed = spots[:, None] >= ends[None, :]
    return jnp.sum(jnp.where(passed, row_lengths[None, :], 0), axis=1)


def after(value, *others):
    return lax.optimization_barrier((value,) + others)[0]


def body(
    block_input,
    out_grad,
    lengths,
    w_query,
    w_key,
    w_value,
    w_out,
    w_gate,
    w_up,
    w_down,
    gain_query,
    gain_key,
    gain_attn,
    gain_mlp,
):
    core = lax.axis_index("c")
    z = lax.axis_index("z")
    peer = lax.axis_index("y") * 2 + lax.axis_index("xl")
    head = core * 4 + z
    my_x = block_input[0]

    columns = jnp.concatenate(
        [w_query.reshape(8, 8, 256), w_key.reshape(8, 8, 128), w_value.reshape(8, 8, 128)], axis=2
    )
    columns = columns.transpose(1, 0, 2).reshape(1, 2, 1, 1, 4, 8, 512)
    gains = jnp.concatenate([gain_query, gain_key, gain_attn, gain_mlp])
    gains = jnp.pad(gains[None, :], ((0, 7), (0, 88)))
    columns = jnp.concatenate(
        [columns, jnp.broadcast_to(gains, (1, 2, 1, 1, 4, 8, 128))], axis=-1
    )
    columns = jnp.broadcast_to(columns, (2, 2, 4, 2, 4, 8, 640)).reshape(128, 8, 640)
    columns = lax.all_to_all(columns, AXES, split_axis=0, concat_axis=0, tiled=False)
    gains = columns[:, 0, 512:552].astype(F32)
    w_head = columns.reshape(1024, 640)
    my_gains = lax.dynamic_slice_in_dim(gains, head * 16, 16, 0)
    gq, gk = my_gains[:, 0:16].reshape(1, 256), my_gains[:, 16:24].reshape(1, 128)

    ga, gm = gains[:, 24:32].reshape(1, 1024), gains[:, 32:40].reshape(1, 1024)

    def everywhere(a, shape):
        a = a.reshape(shape + (8, a.shape[-1]))
        return jnp.broadcast_to(a, (2, 2, 4, 2, 4, 8, a.shape[-1]))

    hidden = [w.reshape(8, 2, 3, 4, 128) for w in (w_gate, w_up, w_down.T)]
    hidden = jnp.concatenate(hidden, axis=-1).transpose(2, 1, 3, 0, 4)
    first = w_out.T.reshape(8, 2, 4, 256).transpose(1, 2, 0, 3)
    first = jnp.concatenate([first, hidden[0]], axis=-1)
    over_x = hidden[1].reshape(2, 2, 2, 8, 384).transpose(1, 0, 2, 3, 4)
    weights = jnp.concatenate(
        [
            everywhere(first, (1, 2, 1, 1, 4)),
            everywhere(over_x, (2, 2, 1, 2, 1)),
            everywhere(hidden[2], (1, 2, 4, 1, 1)),
        ],
        axis=-1,
    ).reshape(128, 8, 1408)
    weights = after(weights, w_head)
    weights = lax.all_to_all(weights, AXES, split_axis=0, concat_axis=0, tiled=False)
    weights = weights.reshape(1024, 1408)

    x_group = [my_x] + [shift(my_x, "z", by, False) for by in (1, -1, 2)]
    x_group = x_group + [swap(jnp.concatenate(x_group, axis=0))]
    x_own, x_other = my_x, x_group[4][:128]
    c_own = out_grad[0]
    c_other = swap(c_own)
    spots = jnp.stack([(z + n) % 4 for n in NEAR])

    q_pre, k_pre, v16, ss, ss_other = project_qkv(x_group, w_head)
    lengths = after(lengths, ss)

    my_lengths = lengths[0]
    other_lengths = swap(my_lengths)
    here = (peer * 4 + spots[:, None]) * 128 + jnp.arange(128, dtype=jnp.int32)[None, :]
    here = here.reshape(512)
    offset = jnp.concatenate(
        [here - row_places(my_lengths, here), here - row_places(other_lengths, here)]
    )
    frequency = THETA ** (-(jnp.arange(64, dtype=F32) * 2.0 / HD))
    angles = offset.astype(F32)[:, None] * frequency[None, :]
    cosine, sine = jnp.cos(angles), jnp.sin(angles)
    cos2 = jnp.concatenate([cosine, cosine], axis=1)
    sin2 = jnp.concatenate([-sine, sine], axis=1)

    task_lengths = jnp.where(peer // 4 == 0, my_lengths, other_lengths)
    task_spots = (
        jnp.arange(32, dtype=jnp.int32)[:, None, None] * 128
        + (peer % 4) * 32
        + jnp.arange(32, dtype=jnp.int32)[None, None, :]
    )
    task_spots = jnp.broadcast_to(task_spots, (32, 2, 32)).reshape(2048)
    starts = row_places(task_lengths, task_spots).reshape(4, 1, 512)
    task_spots = task_spots.reshape(4, 1, 512)
    tiles = 2 * jnp.arange(4, dtype=jnp.int32)
    low = jnp.minimum(jnp.min(starts, axis=(1, 2)) // 512, tiles)
    mid = jnp.clip((jnp.max(starts, axis=(1, 2)) + 511) // 512, low, tiles)

    packed, scales = pack_qkv(spots, q_pre, k_pre, v16, gq, gk, cos2, sin2, group_rows(ss, ss_other))
    z_spots = jnp.stack(ring_spots("z")).astype(jnp.int32)
    pinned = (packed, weights, low, mid, starts, task_spots, ga, gm, z_spots, x_other, c_other)
    pinned = lax.optimization_barrier(pinned)
    packed, weights, low, mid, starts, task_spots, ga, gm, z_spots, x_other, c_other = pinned
    received = lax.all_to_all(packed, ("y", "xl"), split_axis=0, concat_axis=0, tiled=False)
    chunks = jnp.split(weights, [640, 1024], axis=1)

    z_one = onward(chunks[0], "z")
    received, z_one, *chunks = lax.optimization_barrier((received.reshape(32, 320, HD), z_one, *chunks))
    z_two = onward(z_one, "z")
    near = [(onward(w, ring), shift(w, ring, -1, True)) for w, ring in zip(chunks[1:], "xy")]
    attn, acc, lse = attend(received, low, mid, starts, task_spots)
    ones, threes = zip(*near)
    attn, z_two, *near = lax.optimization_barrier((attn, z_two, *ones, *threes))
    ones, threes = near[:2], near[2:]
    attn = lax.all_to_all(attn, SEQ, split_axis=0, concat_axis=0, tiled=False)
    z_three = onward(z_two, "z")
    twos = [onward(one, ring) for one, ring in zip(ones, "xy")]
    attn, z_three, *twos = lax.optimization_barrier((attn, z_three, *twos))
    whole = [chunks[0], z_one, z_two, z_three]
    for own, one, two, three in zip(chunks[1:], ones, twos, threes):
        whole += [own, one, two, three]
    chunks = whole

    flat, half, vec = (256, 1024), (128, 1024), (1, 1024)
    wide, pairs = (12, 256, 128), (12, 256, 256)
    attn16, part = call(
        proj_kernel, [(flat, BF), (flat, BF)], (z_spots, attn, *chunks[:4]), 4
    )
    parts = (part, swap(part))
    mid16, gate, up, act16, down = call(
        forward_kernel,
        [(flat, BF), (wide, BF), (wide, BF), (wide, BF), (flat, BF)],
        (*parts, x_own, x_other, ga, *chunks),
        6,
    )
    output, dd16, d_both, d_mid, dg_mlp = call(
        backward_kernel,
        [(half, F32), (flat, BF), (pairs, BF), (flat, BF), (vec, F32)],
        (down, swap(down), *parts, x_own, c_own, c_other, ga, gm, gate, up, *chunks),
        7,
    )
    d_middle, dp16, d_attn, dg_attn = call(
        d_attn_kernel,
        [(half, F32), (flat, BF), ((32, 64, HD), BF), (vec, F32)],
        (z_spots, d_mid, swap(d_mid), *parts, c_own, c_other, ga, *chunks[:4]),
        3,
    )

    d_attn, d_both = lax.optimization_barrier((d_attn, d_both))
    d_attn = lax.all_to_all(d_attn, SEQ, split_axis=0, concat_axis=0, tiled=False)
    sources = (mid16, dd16, d_both, act16)
    grads = call(
        weight_grads_kernel,
        [((1024, 640), BF)] * 4 + [((1024, 384), BF)] * 8,
        (z_spots, *sources, dp16, attn16),
        6,
    )
    grads = (grads[:4], grads[4:8], grads[8:])
    runs = [onward(g[1], ring) for g, ring in zip(grads, RINGS)]
    d_attn, *runs = lax.optimization_barrier((d_attn, *runs))
    runs = [plus(g[2], run) for g, run in zip(grads, runs)]
    d_attn, *runs = lax.optimization_barrier((d_attn, *runs))
    runs = [onward(run, ring) for run, ring in zip(runs, RINGS)]

    d_pairs = attend_grad(received, d_attn, acc, lse, low, mid, starts, task_spots)
    d_pairs, *runs = lax.optimization_barrier((d_pairs, *runs))
    runs = [plus(g[3], run) for g, run in zip(grads, runs)]
    runs = [onward(run, ring) for run, ring in zip(runs, RINGS)]
    d_pairs = d_pairs.reshape(8, 4, 320, HD)
    d_pairs = lax.all_to_all(d_pairs, ("y", "xl"), split_axis=0, concat_axis=0, tiled=False)
    tq, tk, dv16, dots, dots_other, dgq, dgk = unpack_grads(
        spots, d_pairs, q_pre, k_pre, scales, gq, gk, cos2, sin2
    )
    shares = ring_end([g[0] for g in grads] + list(runs))
    sums, shares = lax.optimization_barrier((group_rows(dots, dots_other), shares))

    gain_grads = (dgq, dgk, dg_attn, dg_mlp)
    d_pre, shares = qkv_grads(
        head[None], tq, tk, dv16, q_pre, k_pre, scales, gain_grads, sums, x_group, shares
    )
    shares = lax.all_to_all(
        shares.reshape(128, 8, 2048), AXES, split_axis=0, concat_axis=0, tiled=False
    )
    d_x = dot_nt(d_pre, w_head[:, :512]).astype(BF)
    d_x = (d_x[:512].astype(F32) + swap(d_x[512:]).astype(F32)).astype(BF)
    widths = (2048, 1024, 1024, 2048, 3072, 3072, 3072)
    outs = [((8, w), F32) for w in widths] + [((1, w), F32) for w in (16, 8, 8, 8)]
    gq, gk, gv, go, gg, gu, gd, *dgains = call(finish_kernel, outs, (shares,), 3)
    d_middle = d_middle + d_x[:128].astype(F32)
    for n, by in enumerate((-1, 1, 2)):
        piece = shift(d_x[128 * (n + 1) : 128 * (n + 2)], "z", by, False)
        d_middle = d_middle + after(piece, gq).astype(F32)

    return (output[None], d_middle[None], gq, gk, gv, go.T, gg, gu, gd.T, *[d[0] for d in dgains])


def solution(mesh):
    cube_mesh = Mesh(mesh.devices.reshape(2, 2, 4, 2, 4), AXES)
    row, seq = ("xh", "c"), SEQ
    everything = row + seq
    tokens, rows, cols, vec = (
        P(row, seq, None),
        P(everything, None),
        P(None, everything),
        P(everything),
    )
    in_specs = (tokens, tokens, P(row, None), rows, rows, rows, cols, rows, rows, cols) + (vec,) * 4
    out_specs = (tokens, tokens, rows, rows, rows, cols, rows, rows, cols) + (vec,) * 4
    return jax.shard_map(body, mesh=cube_mesh, in_specs=in_specs, out_specs=out_specs, check_vma=False)
```
